256 devices in a mesh: ctx: 8 (over x, core), clu: 8 (over z), mp: 4 (over y).
Axes of the slice: x: 4, y: 4, z: 8, core: 2. Of those that a mesh axis runs over, the one named last changes fastest.
Arguments:
- queries: bfloat16 [32768, 2048], P(('ctx', 'clu'), 'mp'), may hold values from -25 to 25
- tok_keys: bfloat16 [32768, 2048], P(('ctx', 'clu'), 'mp'), may hold values from -3.2 to 3.2
- tok_values: bfloat16 [32768, 2048], P(('ctx', 'clu'), 'mp'), may hold values from -6 to 6
- out_grad: bfloat16 [32768, 2048], P(('ctx', 'clu'), 'mp'), may hold values from -6 to 6
- out_weight: bfloat16 [2048, 2048], P('mp', ('ctx', 'clu')), may hold values from -0.125 to 0.125
- membership: int32 [16, 64, 512], P('mp', ('ctx', 'clu')), may hold values from 0 to 32767, as said below
- centroids: float32 [16, 64, 128], P('mp', ('ctx', 'clu')), may hold values from -0.25 to 0.25
Outputs:
- query_grad: bfloat16 [32768, 2048], P(('ctx', 'clu'), 'mp')
- key_grad: bfloat16 [32768, 2048], P(('ctx', 'clu'), 'mp')
- value_grad: bfloat16 [32768, 2048], P(('ctx', 'clu'), 'mp')
- weight_grad: float32 [2048, 2048], P('mp', ('ctx', 'clu'))
- new_centroids: float32 [16, 64, 128], P('mp', ('ctx', 'clu'))
The draws below stay inside these ranges and needn't reach their ends.
Inputs may be any that keep to these rules, and one draw needn't show every extreme that they name: membership[h, c] lists the 512 tokens of cluster c in head h; every token lies in exactly one cluster of each head; members of earlier blocks of 512 tokens come first; no block gives more than 12 tokens to one cluster, and in every head each block gives exactly 12 to some cluster.
All inputs are finite; a program needn't handle non-finite values.
Results may differ from the reference program's by a relative error of at most 0.0061.
Values may be sent and summed in bfloat16 or wider, within the bound.
No kernel may reach another device: no remote copies, remote signals or barrier semaphores. Data moves between devices by JAX's collectives and lax.ppermute only.
A program may use at most 64 MiB of HBM per device.

```python
import jax
import jax.numpy as jnp
from jax import lax

D = 2048
H = 16
DH = 128
TOK_DEV = 512
CLUSTERS = 64
TOKENS = 32768


def routing(key):
    key = jax.random.fold_in(key, 101)
    per_pair = TOK_DEV // CLUSTERS
    half_pair = per_pair // 2

    def one_head(head_key):
        first_key, second_key, third_key = jax.random.split(head_key, 3)
        cluster_order = jax.random.permutation(first_key, CLUSTERS)
        moves = jax.random.randint(second_key, (CLUSTERS // 2,), 0, half_pair + 1).at[0].set(half_pair)
        profile = jnp.full((CLUSTERS,), per_pair, jnp.int32)
        profile = profile.at[cluster_order[0::2]].add(moves).at[cluster_order[1::2]].add(-moves)
        blocks = jnp.arange(CLUSTERS, dtype=jnp.int32)
        counts = profile[(blocks[None, :] - blocks[:, None]) % CLUSTERS]
        col_start = jnp.cumsum(counts, axis=0) - counts
        row_start = jnp.cumsum(counts, axis=1) - counts

        def one_block(block_key, block):
            local = jax.random.permutation(block_key, TOK_DEV).astype(jnp.int32)
            label = jnp.repeat(blocks, counts[block], total_repeat_length=TOK_DEV)
            rank = jnp.arange(TOK_DEV, dtype=jnp.int32) - row_start[block][label]
            token = block * TOK_DEV + local
            list_spot = label * TOK_DEV + col_start[block][label] + rank
            return (token, list_spot)
        tokens, spots = jax.vmap(one_block)(jax.random.split(third_key, CLUSTERS), blocks)
        members = jnp.zeros((CLUSTERS * TOK_DEV,), jnp.int32).at[spots.reshape(-1)].set(tokens.reshape(-1))
        return members.reshape(CLUSTERS, TOK_DEV)
    return jax.vmap(one_head)(jax.random.split(key, H))


def draw_membership(key, part):
    return routing(key)


def draw_tok_keys(key, part):
    key = jax.random.fold_in(key, 3)
    return jnp.clip(jax.random.normal(key, (TOKENS, H * DH), jnp.float32), -2.5, 2.5).astype(jnp.bfloat16)


def draw_queries(key, part):
    key = jax.random.fold_in(key, 5)
    return jnp.clip(jax.random.normal(key, (TOKENS, H * DH), jnp.float32), -2.5, 2.5).astype(jnp.bfloat16)


def level_of(stream_key, shape, pieces, smallest, high):
    gain = 1.0
    for position, shards_of in pieces:
        heights = jax.random.uniform(jax.random.fold_in(jax.random.fold_in(stream_key, 6), position), (shards_of,), jnp.float32, smallest / len(pieces), high / len(pieces))
        gain = gain * jnp.repeat(jnp.exp(heights), shape[position] // shards_of).reshape((-1,) + (1,) * (len(shape) - 1 - position))
    return gain


def normal_values(own_key, extent, deviation, limit, shards=(), kind=jnp.bfloat16):
    factor_of = level_of(own_key, extent, shards, -0.22, 0.18) if shards else 1.0
    entries = jax.random.normal(own_key, extent, jnp.float32) * deviation * factor_of
    return jnp.minimum(jnp.maximum(entries, -limit), limit).astype(kind)


def setup_inputs(seed: int = 0) -> dict:
    key_of = jax.random.split(jax.random.key(seed), 8)
    return {
        "queries": draw_queries(jax.random.fold_in(key_of[7], 71), 0),
        "tok_keys": draw_tok_keys(jax.random.fold_in(key_of[7], 71), 0),
        "tok_values": normal_values(key_of[2], (TOKENS, H * DH), 1.0, 6.0, ((0, 64), (1, 4))),
        "out_grad": normal_values(key_of[3], (TOKENS, D), 1.0, 6.0, ((0, 64), (1, 4))),
        "out_weight": normal_values(key_of[4], (H * DH, D), (H * DH) ** -0.5, 0.125, ((0, 4), (1, 64))),
        "membership": draw_membership(jax.random.fold_in(key_of[7], 71), 0),
        "centroids": normal_values(key_of[6], (H, CLUSTERS, DH), TOK_DEV ** -0.5, 0.25, ((0, 4), (1, 64)), jnp.float32),
    }


epsilon = 1e-06

def attend(query_c, key_c, value_c, grad_c, allowed, scaling):
    scores = jnp.dot(query_c, key_c.T, preferred_element_type=jnp.float32) * scaling
    scores = jnp.where(allowed, scores, -jnp.inf)
    highest = lax.optimization_barrier(jnp.max(scores, axis=1, keepdims=True))
    weights = jnp.exp(scores - highest)
    weights = weights / lax.optimization_barrier(jnp.sum(weights, axis=1, keepdims=True))
    weights_b = weights.astype(jnp.bfloat16)
    attended = jnp.dot(weights_b, value_c, preferred_element_type=jnp.float32)
    value_g = jnp.dot(weights_b.T, grad_c, preferred_element_type=jnp.float32)
    grad_probs = jnp.dot(grad_c, value_c.T, preferred_element_type=jnp.float32)
    row_delta = lax.optimization_barrier(jnp.sum(grad_c.astype(jnp.float32) * attended, axis=1, keepdims=True))
    dscore = (weights * (grad_probs - row_delta) * scaling).astype(jnp.bfloat16)
    query_g = jnp.dot(dscore, key_c, preferred_element_type=jnp.float32)
    key_g = jnp.dot(dscore.T, query_c, preferred_element_type=jnp.float32)
    return (query_g.astype(jnp.bfloat16), key_g.astype(jnp.bfloat16), value_g.astype(jnp.bfloat16), attended.astype(jnp.bfloat16))

def centroid_step(key_c, previous, member_count):
    values = key_c.astype(jnp.float32)
    unit_rows = values / jnp.sqrt(lax.optimization_barrier(jnp.mean(values * values, axis=1, keepdims=True)) + epsilon)
    mixed = 0.5 * previous + 0.5 * lax.optimization_barrier(jnp.sum(unit_rows, axis=0)) / member_count
    return mixed / jnp.sqrt(jnp.mean(mixed * mixed) + epsilon)

def reference(queries, tok_keys, tok_values, out_grad, out_weight, membership, centroids):
    scaling = DH ** (-0.5)
    head_grad = jnp.dot(out_grad, out_weight.T, preferred_element_type=jnp.float32).astype(jnp.bfloat16)

    def one_head(head):

        def columns(source):
            return lax.dynamic_slice_in_dim(source, head * DH, DH, 1)
        query_h = columns(queries)
        key_h = columns(tok_keys)
        value_h = columns(tok_values)
        grad_h = columns(head_grad)
        members = membership[head]

        def one_cluster(inputs):
            member_list, previous = inputs
            allowed = member_list[None, :] <= member_list[:, None]
            results = attend(query_h[member_list], key_h[member_list], value_h[member_list], grad_h[member_list], allowed, scaling)
            center = centroid_step(key_h[member_list], previous, TOK_DEV)
            return results + (center,)
        query_g, key_g, value_g, attended, center = lax.map(one_cluster, (members, centroids[head]))
        flat = members.reshape(-1)

        def place(source):
            return jnp.zeros((TOKENS, DH), jnp.bfloat16).at[flat].set(source.reshape(-1, DH))
        return (place(query_g), place(key_g), place(value_g), place(attended), center)
    query_g, key_g, value_g, attended, center = lax.map(one_head, jnp.arange(H, dtype=jnp.int32))

    def joined(source):
        return source.transpose(1, 0, 2).reshape(TOKENS, H * DH)
    attn_out = joined(attended)
    weight_grad = jnp.dot(attn_out.T, out_grad, preferred_element_type=jnp.float32)
    return (joined(query_g), joined(key_g), joined(value_g), weight_grad, center)
```

```python
import functools

import jax
import jax.numpy as jnp
from jax import lax
from jax.experimental import pallas as pl
from jax.experimental.pallas import tpu as pltpu
from jax.sharding import PartitionSpec as P

epsilon = 1e-06
GROUP = ("ctx", "clu")
CAP = 12
LOW = 8
VMEM = 56 * 1024 * 1024
f32 = jnp.float32
bf16 = jnp.bfloat16


def dot_nn(a, b):
    return lax.dot_general(a, b, (((1,), (0,)), ((), ())), preferred_element_type=f32)


def dot_nt(a, b):
    return lax.dot_general(a, b, (((1,), (1,)), ((), ())), preferred_element_type=f32)


def iota(shape, dim):
    return lax.broadcasted_iota(jnp.int32, shape, dim).astype(f32)


def columns_of(rows):
    copies = 128 // rows.shape[0]
    return jnp.concatenate([rows] * copies, axis=0).T


def onehot(mask):
    return jnp.where(mask, 1.0, 0.0).astype(bf16)


def prep_body(members, blocks, tok_rows):
    heads, count = members.shape
    pieces, rows = [], []
    lane = iota((1, count), 1)
    block_col = iota((blocks, count), 0)
    for h in range(heads):
        member = members[h : h + 1, :]
        block = jnp.floor(member * (1.0 / tok_rows))
        local = member - block * tok_rows
        here = block == block_col
        start_of = jnp.sum(jnp.where(block < block_col, 1.0, 0.0), axis=1, keepdims=True)
        start = jnp.sum(jnp.where(here, start_of, 0.0), axis=0, keepdims=True)
        rank = lane - start
        low = block * LOW + rank
        high = block * LOW + (h % 2) * (CAP - LOW) + (rank - LOW)
        rows += [member, jnp.where(rank < LOW, low, -1.0), jnp.where(rank >= LOW, high, -1.0)]
        at_rank = rank == iota((16, count), 0)
        large = jnp.floor(local * (1.0 / 32))
        small = local - large * 32
        right = jnp.concatenate(
            [
                jnp.where(at_rank, large, 0.0),
                jnp.where(at_rank, small, 0.0),
                jnp.where(at_rank, 1.0, 0.0),
                jnp.zeros((80, count), f32),
            ],
            axis=0,
        ).astype(bf16)
        got = dot_nt(onehot(here), right)
        value = got[:, 0:16] * 32 + got[:, 16:32]
        filled = got[:, 32:48] > 0.5
        pieces.append((value, filled))
    low_cols = [jnp.where(f, v, -1.0)[:, :LOW] for v, f in pieces]
    high_cols = [
        jnp.where(f, v + (h % 2) * tok_rows, -1.0)[:, LOW:CAP]
        for h, (v, f) in enumerate(pieces)
    ]
    used = heads * CAP
    table = jnp.concatenate(
        low_cols + high_cols + [jnp.full((blocks, 128 - used), -1.0, f32)], axis=1
    )
    return table, jnp.concatenate(rows + [jnp.zeros((4, count), f32)], axis=0)


def pack_body(index_rows, sources):
    cols = columns_of(index_rows)
    tokens = sources[0].shape[0]
    slots = index_rows.shape[1]
    n = sources[0].shape[1]
    token = iota((slots, tokens), 1)

    def part(value):
        return value.reshape(slots // LOW, LOW, n)

    low = [
        part(dot_nn(onehot(cols[:, h : h + 1] == token), sources[h]))
        for h in range(4)
    ]
    high = []
    for p in range(2):
        col = cols[:, 4 + p : 5 + p]
        high.append(
            part(
                dot_nn(onehot(col == token), sources[2 * p])
                + dot_nn(onehot(col == token + tokens), sources[2 * p + 1])
            )
        )
    return [
        jnp.concatenate(two, axis=1).astype(bf16)
        for two in (low[:2], low[2:], high)
    ]


def head_slots(parts, h):
    p, q = divmod(h, 2)

    def take(part, q):
        part = part.astype(f32)[:, 8 * q : 8 * q + 8, :]
        return part.reshape(part.shape[0] * 8, part.shape[2]).astype(bf16)

    return take(parts[p], q), take(parts[2], p)


def unpack_body(index_rows, parts, h, tokens):
    low, high = head_slots(parts, h)
    token = iota((tokens, index_rows.shape[1]), 0)
    row_low = index_rows[h : h + 1, :]
    row_high = index_rows[4 + h // 2 : 5 + h // 2, :]
    return dot_nn(onehot(token == row_low), low) + dot_nn(
        onehot(token + (h % 2) * tokens == row_high), high
    )


def compact(cols, parts, h, slots):
    low, high = head_slots(parts, h)
    count = cols.shape[0]
    slot = iota((count, slots), 1)
    return (
        dot_nn(onehot(cols[:, 3 * h + 1 : 3 * h + 2] == slot), low)
        + dot_nn(onehot(cols[:, 3 * h + 2 : 3 * h + 3] == slot), high)
    ).astype(bf16)


def weights_of(rows, cols, query, key, h, scaling):
    scores = dot_nt(key, query) * scaling
    allowed = cols[:, 3 * h : 3 * h + 1] <= rows[3 * h : 3 * h + 1, :]
    scores = jnp.where(allowed, scores, -jnp.inf)
    highest = jnp.max(scores, axis=0, keepdims=True)
    weights = jnp.exp(scores - highest)
    return weights * (1.0 / jnp.sum(weights, axis=0, keepdims=True))


def spread(rows, h, transposed, plain):
    slots = rows.shape[1]
    slot = iota((slots, rows.shape[1]), 0)
    out = []
    for k in (1, 2):
        pick = onehot(slot == rows[3 * h + k : 3 * h + k + 1, :])
        got = [dot_nt(pick, t) for t in transposed] + [dot_nn(pick, v) for v in plain]
        out.append(jnp.concatenate(got, axis=1) if len(got) > 1 else got[0])
    return out


def gathered_parts(results):
    def part(value):
        return value.reshape(value.shape[0] // LOW, LOW, value.shape[1])

    low = [part(r[0]) for r in results]
    high = [part(results[2 * p][1] + results[2 * p + 1][1]) for p in range(2)]
    return [
        jnp.concatenate(two, axis=1).astype(bf16)
        for two in (low[:2], low[2:], high)
    ]


def prep_kernel(tok_rows, members_ref, table_ref, rows_ref):
    table, rows = prep_body(members_ref[...].astype(f32), table_ref.shape[0], tok_rows)
    table_ref[...] = table.astype(jnp.int32)
    rows_ref[...] = rows


def load_parts(ref):
    return [ref[:, 16 * k : 16 * k + 16, :] for k in range(3)]


def store_parts(ref, parts):
    for k in range(3):
        ref[:, 16 * k : 16 * k + 16, :] = parts[k]


def pack_kernel(index_ref, *refs):
    *source_refs, out_ref = refs
    sources = []
    for h in range(4):
        got = [r[:, 128 * h : 128 * h + 128] for r in source_refs]
        sources.append(jnp.concatenate(got, axis=1) if len(got) > 1 else got[0])
    store_parts(out_ref, pack_body(index_ref[...].astype(f32), sources))


def unpack_kernel(index_ref, packed_ref, *out_refs):
    parts = load_parts(packed_ref)
    index_rows = index_ref[...].astype(f32)
    for h in range(4):
        got = unpack_body(index_rows, parts, h, out_refs[0].shape[0]).astype(bf16)
        for k, ref in enumerate(out_refs):
            ref[:, 128 * h : 128 * h + 128] = got[:, 128 * k : 128 * k + 128]


def forward_kernel(scaling, rows_ref, centroids_ref, qkv_ref, out_ref, centers_ref):
    rows = rows_ref[...]
    cols = columns_of(rows)
    parts = load_parts(qkv_ref)
    slots = qkv_ref.shape[0] * LOW
    count = rows.shape[1]
    results = []
    for h in range(4):
        got = compact(cols, parts, h, slots)
        query, key, value = (got[:, 128 * k : 128 * k + 128] for k in range(3))
        keys = key.astype(f32)
        unit = keys / jnp.sqrt(jnp.mean(keys * keys, axis=1, keepdims=True) + epsilon)
        mixed = 0.5 * centroids_ref[h : h + 1, :] + 0.5 * jnp.sum(
            unit, axis=0, keepdims=True
        ) * (1.0 / count)
        centers_ref[h : h + 1, :] = mixed / jnp.sqrt(
            jnp.mean(mixed * mixed, axis=1, keepdims=True) + epsilon
        )
        weights = weights_of(rows, cols, query, key, h, scaling).astype(bf16)
        attended = dot_nn(value.T, weights).astype(bf16)
        results.append(spread(rows, h, [attended], []))
    store_parts(out_ref, gathered_parts(results))


def backward_kernel(scaling, rows_ref, qkv_ref, grad_ref, out_ref):
    rows = rows_ref[...]
    cols = columns_of(rows)
    parts = load_parts(qkv_ref)
    grad_parts = load_parts(grad_ref)
    slots = qkv_ref.shape[0] * LOW
    results = []
    for h in range(4):
        got = compact(cols, parts, h, slots)
        query, key, value = (got[:, 128 * k : 128 * k + 128] for k in range(3))
        grad = compact(cols, grad_parts, h, slots)
        weights = weights_of(rows, cols, query, key, h, scaling)
        weights_b = weights.astype(bf16)
        attended = dot_nn(value.T, weights_b)
        grad_t = grad.astype(f32).T
        delta = jnp.sum(grad_t * attended, axis=0, keepdims=True)
        probs = dot_nt(value, grad)
        dscore = (weights * (probs - delta) * scaling).astype(bf16)
        query_g = dot_nn(key.T, dscore).astype(bf16)
        key_g = dot_nn(dscore, query).astype(bf16)
        value_g = dot_nn(weights_b, grad).astype(bf16)
        results.append(spread(rows, h, [query_g], [jnp.concatenate([key_g, value_g], axis=1)]))
    store_parts(out_ref, gathered_parts(results))


def call(kernel, outs, flops, *args):
    size = sum(a.size * a.dtype.itemsize for a in args)
    size += sum(o.size * o.dtype.itemsize for o in outs)
    whole = pl.BlockSpec(memory_space=pltpu.VMEM)
    got = pl.pallas_call(
        kernel,
        out_shape=outs,
        in_specs=[whole] * len(args),
        out_specs=[whole] * len(outs),
        compiler_params=pltpu.CompilerParams(vmem_limit_bytes=VMEM),
        cost_estimate=pl.CostEstimate(flops=flops, bytes_accessed=size, transcendentals=0),
    )(*args)
    return got[0] if len(outs) == 1 else got


def shape_of(dims, dtype):
    return jax.ShapeDtypeStruct(dims, dtype)


def shifted(x, axis, step, unit=1):
    n = lax.axis_size(axis)
    return lax.ppermute(x, axis, [(i, (i + step * unit) % n) for i in range(n)])


def swapped(x):
    n = lax.axis_size("ctx")
    return lax.ppermute(x, "ctx", [(i, i ^ 1) for i in range(n)])


def gather_tokens(out_grad):
    n = lax.axis_size("mp")
    me = lax.axis_index("mp")
    width = out_grad.shape[1]
    full = jnp.zeros((out_grad.shape[0], n * width), out_grad.dtype)
    for k in range(n):
        piece = shifted(out_grad, "mp", k) if k else out_grad
        full = lax.dynamic_update_slice(full, piece, (0, (me + n - k) % n * width))
    return full


def gather_weight(weight):
    n = lax.axis_size("clu")
    me = lax.axis_index("clu")
    rows, width = weight.shape
    part = jnp.zeros((n * rows, width), weight.dtype)
    for k in range(n):
        piece = shifted(weight, "clu", k) if k else weight
        part = lax.dynamic_update_slice(part, piece, ((me + n - k) % n * rows, 0))
    chips = lax.axis_size("ctx") // 2
    index = lax.axis_index("ctx")
    chip, core = index // 2, index % 2
    mine = jnp.zeros((chips, 1, n * rows, width), weight.dtype)
    for k in range(chips):
        piece = shifted(part, "ctx", k, 2) if k else part
        mine = lax.dynamic_update_slice(
            mine, piece[None, None], ((chip + chips - k) % chips, 0, 0, 0)
        )
    other = swapped(mine)
    full = jnp.zeros((chips, 2, n * rows, width), weight.dtype)
    full = lax.dynamic_update_slice(full, mine, (0, core, 0, 0))
    full = lax.dynamic_update_slice(full, other, (0, 1 - core, 0, 0))
    return full.reshape(chips * 2 * n * rows, width)


def scatter_sum(partial):
    ctx, clu = lax.axis_size("ctx"), lax.axis_size("clu")
    chips = ctx // 2
    index = lax.axis_index("ctx")
    chip, core = index // 2, index % 2
    place = lax.axis_index("clu")
    rows = partial.shape[0] // ctx // clu
    width = partial.shape[1]
    shares = partial.reshape(chips, 2, clu * rows, width)

    def pick(x, i, dim):
        return lax.dynamic_index_in_dim(x, i, dim, keepdims=False)

    other = swapped(pick(shares, 1 - core, 1).astype(bf16))
    shares = pick(shares, core, 1) + other.astype(f32)
    total = pick(shares, chip, 0)
    for k in range(1, chips):
        piece = pick(shares, (chip + k) % chips, 0).astype(bf16)
        total = total + shifted(piece, "ctx", k, 2).astype(f32)
    shares = total.reshape(clu, rows, width)
    total = pick(shares, place, 0)
    for k in range(1, clu):
        piece = pick(shares, (place + k) % clu, 0).astype(bf16)
        total = total + shifted(piece, "clu", k).astype(f32)
    return total


def exchange(x):
    return lax.all_to_all(x, GROUP, split_axis=0, concat_axis=0, tiled=True)


def per_device(queries, tok_keys, tok_values, out_grad, out_weight, membership, centroids):
    tok_rows, width = queries.shape
    heads = membership.shape[0]
    count = membership.shape[2]
    head_size = width // heads
    owners = lax.axis_size(GROUP)
    pair_rows = heads * CAP
    slots = owners * LOW
    scaling = head_size ** (-0.5)

    table, rows = call(
        functools.partial(prep_kernel, tok_rows),
        [shape_of((owners, 128), jnp.int32), shape_of((16, count), f32)],
        10**8,
        membership[:, 0, :],
    )
    table = exchange(table)
    index_low = table[:, : heads * LOW].reshape(owners, heads, LOW)
    index_high = table[:, heads * LOW : pair_rows].reshape(owners, heads // 2, LOW)
    index_rows = jnp.concatenate([index_low, index_high, index_high], axis=1)
    index_rows = index_rows.transpose(1, 0, 2).reshape(2 * heads, slots)

    def packed_shape(n):
        return shape_of((owners, pair_rows, n * head_size), bf16)

    def pack(*sources):
        n = len(sources)
        return call(pack_kernel, [packed_shape(n)], n * 10**9, index_rows, *sources)

    def unpack(packed, n):
        outs = [shape_of((tok_rows, width), bf16)] * n
        return call(unpack_kernel, outs, n * 10**9, index_rows, packed)

    grad_full = gather_tokens(out_grad)
    weight_full = gather_weight(out_weight.T)
    got_qkv = exchange(pack(queries, tok_keys, tok_values))
    head_grad = dot_nn(grad_full, weight_full).astype(bf16)
    got_grad = exchange(pack(head_grad))

    attended, centers = call(
        functools.partial(forward_kernel, scaling),
        [packed_shape(1), shape_of((heads, head_size), f32)],
        4 * 10**9,
        rows,
        centroids[:, 0, :],
        got_qkv,
    )
    back_out = exchange(attended)
    grads = call(
        functools.partial(backward_kernel, scaling),
        [packed_shape(3)],
        8 * 10**9,
        rows,
        got_qkv,
        got_grad,
    )
    back_grads = exchange(grads)
    attn_out = unpack(back_out, 1)
    partial = lax.dot_general(
        grad_full, attn_out, (((0,), (0,)), ((), ())), preferred_element_type=f32
    )
    share = scatter_sum(partial)
    query_g, key_g, value_g = unpack(back_grads, 3)
    return (query_g, key_g, value_g, share.T, centers[:, None, :])


def solution(mesh):
    token = P(GROUP, "mp")
    owner = P("mp", GROUP, None)
    return jax.shard_map(
        per_device,
        mesh=mesh,
        in_specs=(token, token, token, token, P("mp", GROUP), owner, owner),
        out_specs=(token, token, token, P("mp", GROUP), owner),
        check_vma=False,
    )
```

```python
import functools

import jax
import jax.numpy as jnp
from jax import lax
from jax.experimental import pallas as pl
from jax.experimental.pallas import tpu as pltpu
from jax.sharding import PartitionSpec as P

epsilon = 1e-06
GROUP = ("ctx", "clu")
CAP = 12
LOW = 8
VMEM = 56 * 1024 * 1024
f32 = jnp.float32
bf16 = jnp.bfloat16


def dot_nn(a, b):
    return lax.dot_general(a, b, (((1,), (0,)), ((), ())), preferred_element_type=f32)


def dot_nt(a, b):
    return lax.dot_general(a, b, (((1,), (1,)), ((), ())), preferred_element_type=f32)


def iota(shape, dim):
    return lax.broadcasted_iota(jnp.int32, shape, dim).astype(f32)


def columns_of(rows):
    copies = 128 // rows.shape[0]
    return jnp.concatenate([rows] * copies, axis=0).T


def onehot(mask):
    return jnp.where(mask, 1.0, 0.0).astype(bf16)


def prep_body(members, blocks, tok_rows):
    heads, count = members.shape
    pieces, rows = [], []
    lane = iota((1, count), 1)
    block_col = iota((blocks, count), 0)
    for h in range(heads):
        member = members[h : h + 1, :]
        block = jnp.floor(member * (1.0 / tok_rows))
        local = member - block * tok_rows
        here = block == block_col
        start_of = jnp.sum(jnp.where(block < block_col, 1.0, 0.0), axis=1, keepdims=True)
        start = jnp.sum(jnp.where(here, start_of, 0.0), axis=0, keepdims=True)
        rank = lane - start
        low = block * LOW + rank
        high = block * LOW + (h % 2) * (CAP - LOW) + (rank - LOW)
        rows += [member, jnp.where(rank < LOW, low, -1.0), jnp.where(rank >= LOW, high, -1.0)]
        at_rank = rank == iota((16, count), 0)
        large = jnp.floor(local * (1.0 / 32))
        small = local - large * 32
        right = jnp.concatenate(
            [
                jnp.where(at_rank, large, 0.0),
                jnp.where(at_rank, small, 0.0),
                jnp.where(at_rank, 1.0, 0.0),
                jnp.zeros((80, count), f32),
            ],
            axis=0,
        ).astype(bf16)
        got = dot_nt(onehot(here), right)
        value = got[:, 0:16] * 32 + got[:, 16:32]
        filled = got[:, 32:48] > 0.5
        pieces.append((value, filled))
    low_cols = [jnp.where(f, v, -1.0)[:, :LOW] for v, f in pieces]
    high_cols = [
        jnp.where(f, v + (h % 2) * tok_rows, -1.0)[:, LOW:CAP]
        for h, (v, f) in enumerate(pieces)
    ]
    used = heads * CAP
    table = jnp.concatenate(
        low_cols + high_cols + [jnp.full((blocks, 128 - used), -1.0, f32)], axis=1
    )
    return table, jnp.concatenate(rows + [jnp.zeros((4, count), f32)], axis=0)


def pack_body(index_rows, sources):
    cols = columns_of(index_rows)
    tokens = sources[0].shape[0]
    slots = index_rows.shape[1]
    n = sources[0].shape[1]
    token = iota((slots, tokens), 1)

    def part(value):
        return value.reshape(slots // LOW, LOW, n)

    low = [
        part(dot_nn(onehot(cols[:, h : h + 1] == token), sources[h]))
        for h in range(4)
    ]
    high = []
    for p in range(2):
        col = cols[:, 4 + p : 5 + p]
        high.append(
            part(
                dot_nn(onehot(col == token), sources[2 * p])
                + dot_nn(onehot(col == token + tokens), sources[2 * p + 1])
            )
        )
    return [
        jnp.concatenate(two, axis=1).astype(bf16)
        for two in (low[:2], low[2:], high)
    ]


def head_slots(parts, h):
    p, q = divmod(h, 2)

    def take(part, q):
        part = part.astype(f32)[:, 8 * q : 8 * q + 8, :]
        return part.reshape(part.shape[0] * 8, part.shape[2]).astype(bf16)

    return take(parts[p], q), take(parts[2], p)


def unpack_body(index_rows, parts, h, tokens):
    low, high = head_slots(parts, h)
    token = iota((tokens, index_rows.shape[1]), 0)
    row_low = index_rows[h : h + 1, :]
    row_high = index_rows[4 + h // 2 : 5 + h // 2, :]
    return dot_nn(onehot(token == row_low), low) + dot_nn(
        onehot(token + (h % 2) * tokens == row_high), high
    )


def compact(cols, parts, h, slots):
    low, high = head_slots(parts, h)
    count = cols.shape[0]
    slot = iota((count, slots), 1)
    return (
        dot_nn(onehot(cols[:, 3 * h + 1 : 3 * h + 2] == slot), low)
        + dot_nn(onehot(cols[:, 3 * h + 2 : 3 * h + 3] == slot), high)
    ).astype(bf16)


def weights_of(rows, cols, query, key, h, scaling):
    scores = dot_nt(key, query) * scaling
    allowed = cols[:, 3 * h : 3 * h + 1] <= rows[3 * h : 3 * h + 1, :]
    scores = jnp.where(allowed, scores, -jnp.inf)
    highest = jnp.max(scores, axis=0, keepdims=True)
    weights = jnp.exp(scores - highest)
    return weights * (1.0 / jnp.sum(weights, axis=0, keepdims=True))


def spread(rows, h, transposed, plain):
    slots = rows.shape[1]
    slot = iota((slots, rows.shape[1]), 0)
    out = []
    for k in (1, 2):
        pick = onehot(slot == rows[3 * h + k : 3 * h + k + 1, :])
        got = [dot_nt(pick, t) for t in transposed] + [dot_nn(pick, v) for v in plain]
        out.append(jnp.concatenate(got, axis=1) if len(got) > 1 else got[0])
    return out


def gathered_parts(results):
    def part(value):
        return value.reshape(value.shape[0] // LOW, LOW, value.shape[1])

    low = [part(r[0]) for r in results]
    high = [part(results[2 * p][1] + results[2 * p + 1][1]) for p in range(2)]
    return [
        jnp.concatenate(two, axis=1).astype(bf16)
        for two in (low[:2], low[2:], high)
    ]


def prep_kernel(tok_rows, members_ref, table_ref, rows_ref):
    table, rows = prep_body(members_ref[:, 0, :].astype(f32), table_ref.shape[0], tok_rows)
    table_ref[...] = table.astype(jnp.int32)
    rows_ref[...] = rows


def load_parts(ref):
    return [ref[:, 16 * k : 16 * k + 16, :] for k in range(3)]


def store_parts(ref, parts):
    for k in range(3):
        ref[:, 16 * k : 16 * k + 16, :] = parts[k]


def pack_kernel(index_ref, *refs):
    *source_refs, out_ref = refs
    sources = []
    for h in range(4):
        got = [r[:, 128 * h : 128 * h + 128] for r in source_refs]
        sources.append(jnp.concatenate(got, axis=1) if len(got) > 1 else got[0])
    store_parts(out_ref, pack_body(index_ref[...].astype(f32), sources))


def unpack_kernel(index_ref, packed_ref, *out_refs):
    parts = load_parts(packed_ref)
    index_rows = index_ref[...].astype(f32)
    for h in range(4):
        got = unpack_body(index_rows, parts, h, out_refs[0].shape[0]).astype(bf16)
        for k, ref in enumerate(out_refs):
            ref[:, 128 * h : 128 * h + 128] = got[:, 128 * k : 128 * k + 128]


def forward_kernel(scaling, rows_ref, centroids_ref, qkv_ref, out_ref, centers_ref):
    rows = rows_ref[...]
    cols = columns_of(rows)
    parts = load_parts(qkv_ref)
    slots = qkv_ref.shape[0] * LOW
    count = rows.shape[1]
    results = []
    for h in range(4):
        got = compact(cols, parts, h, slots)
        query, key, value = (got[:, 128 * k : 128 * k + 128] for k in range(3))
        keys = key.astype(f32)
        unit = keys / jnp.sqrt(jnp.mean(keys * keys, axis=1, keepdims=True) + epsilon)
        mixed = 0.5 * centroids_ref[h : h + 1, :] + 0.5 * jnp.sum(
            unit, axis=0, keepdims=True
        ) * (1.0 / count)
        centers_ref[h : h + 1, :] = mixed / jnp.sqrt(
            jnp.mean(mixed * mixed, axis=1, keepdims=True) + epsilon
        )
        weights = weights_of(rows, cols, query, key, h, scaling).astype(bf16)
        attended = dot_nn(value.T, weights).astype(bf16)
        results.append(spread(rows, h, [attended], []))
    store_parts(out_ref, gathered_parts(results))


def backward_kernel(scaling, rows_ref, qkv_ref, grad_ref, out_ref):
    rows = rows_ref[...]
    cols = columns_of(rows)
    parts = load_parts(qkv_ref)
    grad_parts = load_parts(grad_ref)
    slots = qkv_ref.shape[0] * LOW
    results = []
    for h in range(4):
        got = compact(cols, parts, h, slots)
        query, key, value = (got[:, 128 * k : 128 * k + 128] for k in range(3))
        grad = compact(cols, grad_parts, h, slots)
        weights = weights_of(rows, cols, query, key, h, scaling)
        weights_b = weights.astype(bf16)
        attended = dot_nn(value.T, weights_b)
        grad_t = grad.astype(f32).T
        delta = jnp.sum(grad_t * attended, axis=0, keepdims=True)
        probs = dot_nt(value, grad)
        dscore = (weights * (probs - delta) * scaling).astype(bf16)
        query_g = dot_nn(key.T, dscore).astype(bf16)
        key_g = dot_nn(dscore, query).astype(bf16)
        value_g = dot_nn(weights_b, grad).astype(bf16)
        results.append(spread(rows, h, [query_g], [jnp.concatenate([key_g, value_g], axis=1)]))
    store_parts(out_ref, gathered_parts(results))


def call(kernel, outs, flops, *args):
    size = sum(a.size * a.dtype.itemsize for a in args)
    size += sum(o.size * o.dtype.itemsize for o in outs)
    whole = pl.BlockSpec(memory_space=pltpu.VMEM)
    got = pl.pallas_call(
        kernel,
        out_shape=outs,
        in_specs=[whole] * len(args),
        out_specs=[whole] * len(outs),
        compiler_params=pltpu.CompilerParams(vmem_limit_bytes=VMEM),
        cost_estimate=pl.CostEstimate(flops=flops, bytes_accessed=size, transcendentals=0),
    )(*args)
    return got[0] if len(outs) == 1 else got


def shape_of(dims, dtype):
    return jax.ShapeDtypeStruct(dims, dtype)


def shifted(x, axis, step, unit=1):
    n = lax.axis_size(axis)
    return lax.ppermute(x, axis, [(i, (i + step * unit) % n) for i in range(n)])


def swapped(x):
    n = lax.axis_size("ctx")
    return lax.ppermute(x, "ctx", [(i, i ^ 1) for i in range(n)])


def neighbour_tokens(out_grad):
    n = lax.axis_size("mp")
    return shifted(out_grad, "mp", 1), shifted(out_grad, "mp", n - 1)


def all_tokens(out_grad, before, after):
    n = lax.axis_size("mp")
    me = lax.axis_index("mp")
    rows, width = out_grad.shape
    half = rows // 2
    upper = shifted(before[:half], "mp", 1)
    lower = shifted(after[half:], "mp", n - 1)
    full = jnp.zeros((rows, n * width), out_grad.dtype)
    full = lax.dynamic_update_slice(full, out_grad, (0, me * width))
    full = lax.dynamic_update_slice(full, before, (0, (me + n - 1) % n * width))
    full = lax.dynamic_update_slice(full, after, (0, (me + 1) % n * width))
    opposite = (me + 2) % n * width
    full = lax.dynamic_update_slice(full, upper, (0, opposite))
    return lax.dynamic_update_slice(full, lower, (half, opposite))


def clu_weight(weight):
    n = lax.axis_size("clu")
    me = lax.axis_index("clu")
    step = 1
    while step < n:
        other = lax.ppermute(weight, "clu", [(i, i ^ step) for i in range(n)])
        first = me // step % 2 == 0
        weight = jnp.concatenate(
            [jnp.where(first, weight, other), jnp.where(first, other, weight)], axis=0
        )
        step *= 2
    return weight


def ctx_weight(part):
    rows, width = part.shape
    chips = lax.axis_size("ctx") // 2
    index = lax.axis_index("ctx")
    chip, core = index // 2, index % 2
    mine = jnp.zeros((chips, 1, rows, width), part.dtype)
    for k in range(chips):
        piece = shifted(part, "ctx", k, 2) if k else part
        mine = lax.dynamic_update_slice(
            mine, piece[None, None], ((chip + chips - k) % chips, 0, 0, 0)
        )
    other = swapped(mine)
    full = jnp.zeros((chips, 2, rows, width), part.dtype)
    full = lax.dynamic_update_slice(full, mine, (0, core, 0, 0))
    full = lax.dynamic_update_slice(full, other, (0, 1 - core, 0, 0))
    return full.reshape(chips * 2 * rows, width)


def scatter_sum(partial):
    ctx, clu = lax.axis_size("ctx"), lax.axis_size("clu")
    chips = ctx // 2
    index = lax.axis_index("ctx")
    chip, core = index // 2, index % 2
    place = lax.axis_index("clu")
    rows = partial.shape[0] // ctx // clu
    width = partial.shape[1]
    shares = partial.reshape(chips, 2, clu * rows, width)

    def pick(x, i, dim):
        return lax.dynamic_index_in_dim(x, i, dim, keepdims=False)

    other = swapped(pick(shares, 1 - core, 1).astype(bf16))
    shares = pick(shares, core, 1) + other.astype(f32)
    total = pick(shares, chip, 0)
    for k in range(1, chips):
        piece = pick(shares, (chip + k) % chips, 0).astype(bf16)
        total = total + shifted(piece, "ctx", k, 2).astype(f32)
    step = 1
    while step < clu:
        bit = place // step % 2
        halves = total.reshape(clu // (2 * step), 2, rows, width)
        piece = pick(halves, 1 - bit, 1).astype(bf16)
        other = lax.ppermute(piece, "clu", [(i, i ^ step) for i in range(clu)])
        total = pick(halves, bit, 1) + other.astype(f32)
        step *= 2
    return total.reshape(rows, width)


def exchange(x):
    return lax.all_to_all(x, GROUP, split_axis=0, concat_axis=0, tiled=True)


def per_device(queries, tok_keys, tok_values, out_grad, out_weight, membership, centroids):
    tok_rows, width = queries.shape
    heads = membership.shape[0]
    count = membership.shape[2]
    head_size = width // heads
    owners = lax.axis_size(GROUP)
    pair_rows = heads * CAP
    slots = owners * LOW
    scaling = head_size ** (-0.5)

    table, rows = call(
        functools.partial(prep_kernel, tok_rows),
        [shape_of((owners, 128), jnp.int32), shape_of((16, count), f32)],
        10**8,
        membership,
    )
    before, after = neighbour_tokens(out_grad)
    weight_part = clu_weight(out_weight.T)
    table = exchange(table)
    index_low = table[:, : heads * LOW].reshape(owners, heads, LOW)
    index_high = table[:, heads * LOW : pair_rows].reshape(owners, heads // 2, LOW)
    index_rows = jnp.concatenate([index_low, index_high, index_high], axis=1)
    index_rows = index_rows.transpose(1, 0, 2).reshape(2 * heads, slots)
    index_rows, before, after, weight_part = lax.optimization_barrier(
        (index_rows, before, after, weight_part)
    )

    def packed_shape(n):
        return shape_of((owners, pair_rows, n * head_size), bf16)

    def pack(*sources):
        n = len(sources)
        return call(pack_kernel, [packed_shape(n)], n * 10**9, index_rows, *sources)

    def unpack(packed, n):
        outs = [shape_of((tok_rows, width), bf16)] * n
        return call(unpack_kernel, outs, n * 10**9, index_rows, packed)

    got_qkv = exchange(pack(queries, tok_keys, tok_values))
    grad_full = all_tokens(out_grad, before, after)
    weight_full = ctx_weight(weight_part)
    head_grad = dot_nn(grad_full, weight_full).astype(bf16)
    got_grad = exchange(pack(head_grad))

    attended, centers = call(
        functools.partial(forward_kernel, scaling),
        [packed_shape(1), shape_of((heads, head_size), f32)],
        4 * 10**9,
        rows,
        centroids[:, 0, :],
        got_qkv,
    )
    back_out = exchange(attended)
    grads = call(
        functools.partial(backward_kernel, scaling),
        [packed_shape(3)],
        8 * 10**9,
        rows,
        got_qkv,
        got_grad,
    )
    back_grads = exchange(grads)
    attn_out = unpack(back_out, 1)
    partial = lax.dot_general(
        grad_full, attn_out, (((0,), (0,)), ((), ())), preferred_element_type=f32
    )
    share = scatter_sum(partial)
    query_g, key_g, value_g = unpack(back_grads, 3)
    return (query_g, key_g, value_g, share.T, centers[:, None, :])


def solution(mesh):
    token = P(GROUP, "mp")
    owner = P("mp", GROUP, None)
    return jax.shard_map(
        per_device,
        mesh=mesh,
        in_specs=(token, token, token, token, P("mp", GROUP), owner, owner),
        out_specs=(token, token, token, P("mp", GROUP), owner),
        check_vma=False,
    )
```

```python
import functools

import jax
import jax.numpy as jnp
from jax import lax
from jax.experimental import pallas as pl
from jax.experimental.pallas import tpu as pltpu
from jax.sharding import PartitionSpec as P

epsilon = 1e-06
GROUP = ("ctx", "clu")
CAP = 12
LOW = 8
VMEM = 56 * 1024 * 1024
f32 = jnp.float32
bf16 = jnp.bfloat16


def dot_nn(a, b):
    return lax.dot_general(a, b, (((1,), (0,)), ((), ())), preferred_element_type=f32)


def dot_nt(a, b):
    return lax.dot_general(a, b, (((1,), (1,)), ((), ())), preferred_element_type=f32)


def iota(shape, dim):
    return lax.broadcasted_iota(jnp.int32, shape, dim).astype(f32)


def columns_of(rows):
    copies = 128 // rows.shape[0]
    return jnp.concatenate([rows] * copies, axis=0).T


def onehot(mask):
    return jnp.where(mask, 1.0, 0.0).astype(bf16)


def prep_body(members, blocks, tok_rows):
    heads, count = members.shape
    pieces, rows = [], []
    lane = iota((1, count), 1)
    block_col = iota((blocks, count), 0)
    for h in range(heads):
        member = members[h : h + 1, :]
        block = jnp.floor(member * (1.0 / tok_rows))
        local = member - block * tok_rows
        here = block == block_col
        start_of = jnp.sum(jnp.where(block < block_col, 1.0, 0.0), axis=1, keepdims=True)
        start = jnp.sum(jnp.where(here, start_of, 0.0), axis=0, keepdims=True)
        rank = lane - start
        low = block * LOW + rank
        high = block * LOW + (h % 2) * (CAP - LOW) + (rank - LOW)
        rows += [member, jnp.where(rank < LOW, low, -1.0), jnp.where(rank >= LOW, high, -1.0)]
        at_rank = rank == iota((16, count), 0)
        large = jnp.floor(local * (1.0 / 32))
        small = local - large * 32
        right = jnp.concatenate(
            [
                jnp.where(at_rank, large, 0.0),
                jnp.where(at_rank, small, 0.0),
                jnp.where(at_rank, 1.0, 0.0),
                jnp.zeros((80, count), f32),
            ],
            axis=0,
        ).astype(bf16)
        got = dot_nt(onehot(here), right)
        value = got[:, 0:16] * 32 + got[:, 16:32]
        filled = got[:, 32:48] > 0.5
        pieces.append((value, filled))
    low_cols = [jnp.where(f, v, -1.0)[:, :LOW] for v, f in pieces]
    high_cols = [
        jnp.where(f, v + (h % 2) * tok_rows, -1.0)[:, LOW:CAP]
        for h, (v, f) in enumerate(pieces)
    ]
    used = heads * CAP
    table = jnp.concatenate(
        low_cols + high_cols + [jnp.full((blocks, 128 - used), -1.0, f32)], axis=1
    )
    return table, jnp.concatenate(rows + [jnp.zeros((4, count), f32)], axis=0)


def pack_body(index_rows, sources):
    cols = columns_of(index_rows)
    tokens = sources[0].shape[0]
    slots = index_rows.shape[1]
    n = sources[0].shape[1]
    token = iota((slots, tokens), 1)

    def part(value):
        return value.reshape(slots // LOW, LOW, n)

    low = [
        part(dot_nn(onehot(cols[:, h : h + 1] == token), sources[h]))
        for h in range(4)
    ]
    high = []
    for p in range(2):
        col = cols[:, 4 + p : 5 + p]
        high.append(
            part(
                dot_nn(onehot(col == token), sources[2 * p])
                + dot_nn(onehot(col == token + tokens), sources[2 * p + 1])
            )
        )
    return [
        jnp.concatenate(two, axis=1).astype(bf16)
        for two in (low[:2], low[2:], high)
    ]


def head_slots(parts, h):
    p, q = divmod(h, 2)

    def take(part, q):
        part = part.astype(f32)[:, 8 * q : 8 * q + 8, :]
        return part.reshape(part.shape[0] * 8, part.shape[2]).astype(bf16)

    return take(parts[p], q), take(parts[2], p)


def unpack_body(index_rows, parts, h, tokens):
    low, high = head_slots(parts, h)
    token = iota((tokens, index_rows.shape[1]), 0)
    row_low = index_rows[h : h + 1, :]
    row_high = index_rows[4 + h // 2 : 5 + h // 2, :]
    return dot_nn(onehot(token == row_low), low) + dot_nn(
        onehot(token + (h % 2) * tokens == row_high), high
    )


def compact(cols, parts, h, slots):
    low, high = head_slots(parts, h)
    count = cols.shape[0]
    slot = iota((count, slots), 1)
    return (
        dot_nn(onehot(cols[:, 3 * h + 1 : 3 * h + 2] == slot), low)
        + dot_nn(onehot(cols[:, 3 * h + 2 : 3 * h + 3] == slot), high)
    ).astype(bf16)


def weights_of(rows, cols, query, key, h, scaling):
    scores = dot_nt(key, query) * scaling
    allowed = cols[:, 3 * h : 3 * h + 1] <= rows[3 * h : 3 * h + 1, :]
    scores = jnp.where(allowed, scores, -jnp.inf)
    highest = jnp.max(scores, axis=0, keepdims=True)
    weights = jnp.exp(scores - highest)
    return weights * (1.0 / jnp.sum(weights, axis=0, keepdims=True))


def spread(rows, h, transposed, plain):
    slots = rows.shape[1]
    slot = iota((slots, rows.shape[1]), 0)
    out = []
    for k in (1, 2):
        pick = onehot(slot == rows[3 * h + k : 3 * h + k + 1, :])
        got = [dot_nt(pick, t) for t in transposed] + [dot_nn(pick, v) for v in plain]
        out.append(jnp.concatenate(got, axis=1) if len(got) > 1 else got[0])
    return out


def gathered_parts(results):
    def part(value):
        return value.reshape(value.shape[0] // LOW, LOW, value.shape[1])

    low = [part(r[0]) for r in results]
    high = [part(results[2 * p][1] + results[2 * p + 1][1]) for p in range(2)]
    return [
        jnp.concatenate(two, axis=1).astype(bf16)
        for two in (low[:2], low[2:], high)
    ]


def prep_kernel(tok_rows, members_ref, table_ref, rows_ref):
    table, rows = prep_body(members_ref[:, 0, :].astype(f32), table_ref.shape[0], tok_rows)
    table_ref[...] = table.astype(jnp.int32)
    rows_ref[...] = rows


def load_parts(ref):
    return [ref[:, 16 * k : 16 * k + 16, :] for k in range(3)]


def store_parts(ref, parts):
    for k in range(3):
        ref[:, 16 * k : 16 * k + 16, :] = parts[k]


def pack_kernel(index_ref, *refs):
    *source_refs, out_ref = refs
    sources = []
    for h in range(4):
        got = [r[:, 128 * h : 128 * h + 128] for r in source_refs]
        sources.append(jnp.concatenate(got, axis=1) if len(got) > 1 else got[0])
    store_parts(out_ref, pack_body(index_ref[...].astype(f32), sources))


def unpack_kernel(index_ref, packed_ref, *out_refs):
    parts = load_parts(packed_ref)
    index_rows = index_ref[...].astype(f32)
    for h in range(4):
        got = unpack_body(index_rows, parts, h, out_refs[0].shape[0]).astype(bf16)
        for k, ref in enumerate(out_refs):
            ref[:, 128 * h : 128 * h + 128] = got[:, 128 * k : 128 * k + 128]


def forward_kernel(scaling, rows_ref, centroids_ref, qkv_ref, out_ref, centers_ref):
    rows = rows_ref[...]
    cols = columns_of(rows)
    parts = load_parts(qkv_ref)
    slots = qkv_ref.shape[0] * LOW
    count = rows.shape[1]
    results = []
    for h in range(4):
        got = compact(cols, parts, h, slots)
        query, key, value = (got[:, 128 * k : 128 * k + 128] for k in range(3))
        keys = key.astype(f32)
        unit = keys / jnp.sqrt(jnp.mean(keys * keys, axis=1, keepdims=True) + epsilon)
        mixed = 0.5 * centroids_ref[h : h + 1, :] + 0.5 * jnp.sum(
            unit, axis=0, keepdims=True
        ) * (1.0 / count)
        centers_ref[h : h + 1, :] = mixed / jnp.sqrt(
            jnp.mean(mixed * mixed, axis=1, keepdims=True) + epsilon
        )
        weights = weights_of(rows, cols, query, key, h, scaling).astype(bf16)
        attended = dot_nn(value.T, weights).astype(bf16)
        results.append(spread(rows, h, [attended], []))
    store_parts(out_ref, gathered_parts(results))


def backward_kernel(scaling, rows_ref, qkv_ref, grad_ref, out_ref):
    rows = rows_ref[...]
    cols = columns_of(rows)
    parts = load_parts(qkv_ref)
    grad_parts = load_parts(grad_ref)
    slots = qkv_ref.shape[0] * LOW
    results = []
    for h in range(4):
        got = compact(cols, parts, h, slots)
        query, key, value = (got[:, 128 * k : 128 * k + 128] for k in range(3))
        grad = compact(cols, grad_parts, h, slots)
        weights = weights_of(rows, cols, query, key, h, scaling)
        weights_b = weights.astype(bf16)
        attended = dot_nn(value.T, weights_b)
        grad_t = grad.astype(f32).T
        delta = jnp.sum(grad_t * attended, axis=0, keepdims=True)
        probs = dot_nt(value, grad)
        dscore = (weights * (probs - delta) * scaling).astype(bf16)
        query_g = dot_nn(key.T, dscore).astype(bf16)
        key_g = dot_nn(dscore, query).astype(bf16)
        value_g = dot_nn(weights_b, grad).astype(bf16)
        results.append(spread(rows, h, [query_g], [jnp.concatenate([key_g, value_g], axis=1)]))
    store_parts(out_ref, gathered_parts(results))


def call(kernel, outs, flops, *args):
    size = sum(a.size * a.dtype.itemsize for a in args)
    size += sum(o.size * o.dtype.itemsize for o in outs)
    whole = pl.BlockSpec(memory_space=pltpu.VMEM)
    got = pl.pallas_call(
        kernel,
        out_shape=outs,
        in_specs=[whole] * len(args),
        out_specs=[whole] * len(outs),
        compiler_params=pltpu.CompilerParams(vmem_limit_bytes=VMEM),
        cost_estimate=pl.CostEstimate(flops=flops, bytes_accessed=size, transcendentals=0),
    )(*args)
    return got[0] if len(outs) == 1 else got


def shape_of(dims, dtype):
    return jax.ShapeDtypeStruct(dims, dtype)


def shifted(x, axis, step, unit=1):
    n = lax.axis_size(axis)
    return lax.ppermute(x, axis, [(i, (i + step * unit) % n) for i in range(n)])


def swapped(x):
    n = lax.axis_size("ctx")
    return lax.ppermute(x, "ctx", [(i, i ^ 1) for i in range(n)])


def neighbour_tokens(out_grad):
    n = lax.axis_size("mp")
    return shifted(out_grad, "mp", 1), shifted(out_grad, "mp", n - 1)


def all_tokens(out_grad, before, after):
    n = lax.axis_size("mp")
    me = lax.axis_index("mp")
    rows, width = out_grad.shape
    half = rows // 2
    upper = shifted(before[:half], "mp", 1)
    lower = shifted(after[half:], "mp", n - 1)
    full = jnp.zeros((rows, n * width), out_grad.dtype)
    full = lax.dynamic_update_slice(full, out_grad, (0, me * width))
    full = lax.dynamic_update_slice(full, before, (0, (me + n - 1) % n * width))
    full = lax.dynamic_update_slice(full, after, (0, (me + 1) % n * width))
    opposite = (me + 2) % n * width
    full = lax.dynamic_update_slice(full, upper, (0, opposite))
    return lax.dynamic_update_slice(full, lower, (half, opposite))


def clu_weight_parts(weight):
    n = lax.axis_size("clu")
    me = lax.axis_index("clu")
    other = lax.ppermute(weight, "clu", [(i, i ^ 1) for i in range(n)])
    first = me % 2 == 0
    pair = jnp.concatenate(
        [jnp.where(first, weight, other), jnp.where(first, other, weight)], axis=0
    )
    return [pair] + [shifted(pair, "clu", k, 2) for k in range(1, n // 2)]


def clu_weight(parts):
    n = len(parts)
    pair = lax.axis_index("clu") // 2
    rows, width = parts[0].shape
    full = jnp.zeros((n * rows, width), parts[0].dtype)
    for k, part in enumerate(parts):
        full = lax.dynamic_update_slice(full, part, ((pair + n - k) % n * rows, 0))
    return full


def ctx_weight(part):
    rows, width = part.shape
    chips = lax.axis_size("ctx") // 2
    index = lax.axis_index("ctx")
    chip, core = index // 2, index % 2
    mine = jnp.zeros((chips, 1, rows, width), part.dtype)
    for k in range(chips):
        piece = shifted(part, "ctx", k, 2) if k else part
        mine = lax.dynamic_update_slice(
            mine, piece[None, None], ((chip + chips - k) % chips, 0, 0, 0)
        )
    other = swapped(mine)
    full = jnp.zeros((chips, 2, rows, width), part.dtype)
    full = lax.dynamic_update_slice(full, mine, (0, core, 0, 0))
    full = lax.dynamic_update_slice(full, other, (0, 1 - core, 0, 0))
    return full.reshape(chips * 2 * rows, width)


def scatter_sum(partial):
    ctx, clu = lax.axis_size("ctx"), lax.axis_size("clu")
    chips = ctx // 2
    index = lax.axis_index("ctx")
    chip, core = index // 2, index % 2
    place = lax.axis_index("clu")
    rows = partial.shape[0] // ctx // clu
    width = partial.shape[1]
    shares = partial.reshape(chips, 2, clu * rows, width)

    def pick(x, i, dim):
        return lax.dynamic_index_in_dim(x, i, dim, keepdims=False)

    other = swapped(pick(shares, 1 - core, 1).astype(bf16))
    shares = pick(shares, core, 1) + other.astype(f32)
    total = pick(shares, chip, 0)
    for k in range(1, chips):
        piece = pick(shares, (chip + k) % chips, 0).astype(bf16)
        total = total + shifted(piece, "ctx", k, 2).astype(f32)
    pairs = clu // 2
    shares = total.reshape(pairs, 2, rows, width)
    total = pick(shares, place // 2, 0)
    for k in range(1, pairs):
        piece = pick(shares, (place // 2 + k) % pairs, 0).astype(bf16)
        total = total + shifted(piece, "clu", k, 2).astype(f32)
    return total


def scatter_last(shares):
    clu = lax.axis_size("clu")
    bit = lax.axis_index("clu") % 2
    piece = lax.dynamic_index_in_dim(shares, 1 - bit, 0, keepdims=False).astype(bf16)
    other = lax.ppermute(piece, "clu", [(i, i ^ 1) for i in range(clu)])
    return lax.dynamic_index_in_dim(shares, bit, 0, keepdims=False) + other.astype(f32)


def exchange(x):
    return lax.all_to_all(x, GROUP, split_axis=0, concat_axis=0, tiled=True)


def per_device(queries, tok_keys, tok_values, out_grad, out_weight, membership, centroids):
    tok_rows, width = queries.shape
    heads = membership.shape[0]
    count = membership.shape[2]
    head_size = width // heads
    owners = lax.axis_size(GROUP)
    pair_rows = heads * CAP
    slots = owners * LOW
    scaling = head_size ** (-0.5)

    table, rows = call(
        functools.partial(prep_kernel, tok_rows),
        [shape_of((owners, 128), jnp.int32), shape_of((16, count), f32)],
        10**8,
        membership,
    )
    before, after = neighbour_tokens(out_grad)
    weight_parts = clu_weight_parts(out_weight.T)
    table = exchange(table)
    index_low = table[:, : heads * LOW].reshape(owners, heads, LOW)
    index_high = table[:, heads * LOW : pair_rows].reshape(owners, heads // 2, LOW)
    index_rows = jnp.concatenate([index_low, index_high, index_high], axis=1)
    index_rows = index_rows.transpose(1, 0, 2).reshape(2 * heads, slots)
    index_rows, before, after, weight_parts = lax.optimization_barrier(
        (index_rows, before, after, weight_parts)
    )

    def packed_shape(n):
        return shape_of((owners, pair_rows, n * head_size), bf16)

    def pack(*sources):
        n = len(sources)
        return call(pack_kernel, [packed_shape(n)], n * 10**9, index_rows, *sources)

    def unpack(packed, n):
        outs = [shape_of((tok_rows, width), bf16)] * n
        return call(unpack_kernel, outs, n * 10**9, index_rows, packed)

    got_qkv = exchange(pack(queries, tok_keys, tok_values))
    grad_full = all_tokens(out_grad, before, after)
    weight_full = ctx_weight(clu_weight(weight_parts))
    head_grad = dot_nn(grad_full, weight_full).astype(bf16)
    got_grad = exchange(pack(head_grad))

    attended, centers = call(
        functools.partial(forward_kernel, scaling),
        [packed_shape(1), shape_of((heads, head_size), f32)],
        4 * 10**9,
        rows,
        centroids[:, 0, :],
        got_qkv,
    )
    back_out = exchange(attended)
    grads = call(
        functools.partial(backward_kernel, scaling),
        [packed_shape(3)],
        8 * 10**9,
        rows,
        got_qkv,
        got_grad,
    )
    back_grads = exchange(grads)
    attn_out = unpack(back_out, 1)
    partial = lax.dot_general(
        grad_full, attn_out, (((0,), (0,)), ((), ())), preferred_element_type=f32
    )
    back_grads, shares = lax.optimization_barrier((back_grads, scatter_sum(partial)))
    share = scatter_last(shares)
    query_g, key_g, value_g = unpack(back_grads, 3)
    return (query_g, key_g, value_g, share.T, centers[:, None, :])


def solution(mesh):
    token = P(GROUP, "mp")
    owner = P("mp", GROUP, None)
    return jax.shard_map(
        per_device,
        mesh=mesh,
        in_specs=(token, token, token, token, P("mp", GROUP), owner, owner),
        out_specs=(token, token, token, P("mp", GROUP), owner),
        check_vma=False,
    )
```

```python
import functools

import jax
import jax.numpy as jnp
from jax import lax
from jax.experimental import pallas as pl
from jax.experimental.pallas import tpu as pltpu
from jax.sharding import PartitionSpec as P

epsilon = 1e-06
GROUP = ("ctx", "clu")
CAP = 12
LOW = 8
VMEM = 56 * 1024 * 1024
f32 = jnp.float32
bf16 = jnp.bfloat16


def dot_nn(a, b):
    return lax.dot_general(a, b, (((1,), (0,)), ((), ())), preferred_element_type=f32)


def dot_nt(a, b):
    return lax.dot_general(a, b, (((1,), (1,)), ((), ())), preferred_element_type=f32)


def iota(shape, dim):
    return lax.broadcasted_iota(jnp.int32, shape, dim).astype(f32)


def columns_of(rows):
    copies = 128 // rows.shape[0]
    return jnp.concatenate([rows] * copies, axis=0).T


def onehot(mask):
    return jnp.where(mask, 1.0, 0.0).astype(bf16)


def prep_body(members, blocks, tok_rows):
    heads, count = members.shape
    pieces, rows = [], []
    lane = iota((1, count), 1)
    block_col = iota((blocks, count), 0)
    for h in range(heads):
        member = members[h : h + 1, :]
        block = jnp.floor(member * (1.0 / tok_rows))
        local = member - block * tok_rows
        here = block == block_col
        start_of = jnp.sum(jnp.where(block < block_col, 1.0, 0.0), axis=1, keepdims=True)
        start = jnp.sum(jnp.where(here, start_of, 0.0), axis=0, keepdims=True)
        rank = lane - start
        low = block * LOW + rank
        high = block * LOW + (h % 2) * (CAP - LOW) + (rank - LOW)
        rows += [member, jnp.where(rank < LOW, low, -1.0), jnp.where(rank >= LOW, high, -1.0)]
        at_rank = rank == iota((16, count), 0)
        large = jnp.floor(local * (1.0 / 32))
        small = local - large * 32
        right = jnp.concatenate(
            [
                jnp.where(at_rank, large, 0.0),
                jnp.where(at_rank, small, 0.0),
                jnp.where(at_rank, 1.0, 0.0),
                jnp.zeros((80, count), f32),
            ],
            axis=0,
        ).astype(bf16)
        got = dot_nt(onehot(here), right)
        value = got[:, 0:16] * 32 + got[:, 16:32]
        filled = got[:, 32:48] > 0.5
        pieces.append((value, filled))
    low_cols = [jnp.where(f, v, -1.0)[:, :LOW] for v, f in pieces]
    high_cols = [
        jnp.where(f, v + (h % 2) * tok_rows, -1.0)[:, LOW:CAP]
        for h, (v, f) in enumerate(pieces)
    ]
    used = heads * CAP
    table = jnp.concatenate(
        low_cols + high_cols + [jnp.full((blocks, 128 - used), -1.0, f32)], axis=1
    )
    return table, jnp.concatenate(rows + [jnp.zeros((4, count), f32)], axis=0)


def pack_body(index_rows, sources):
    cols = columns_of(index_rows)
    tokens = sources[0].shape[0]
    slots = index_rows.shape[1]
    n = sources[0].shape[1]
    token = iota((slots, tokens), 1)

    def part(value):
        return value.reshape(slots // LOW, LOW, n)

    low = [
        part(dot_nn(onehot(cols[:, h : h + 1] == token), sources[h]))
        for h in range(4)
    ]
    high = []
    for p in range(2):
        col = cols[:, 4 + p : 5 + p]
        high.append(
            part(
                dot_nn(onehot(col == token), sources[2 * p])
                + dot_nn(onehot(col == token + tokens), sources[2 * p + 1])
            )
        )
    return [
        jnp.concatenate(two, axis=1).astype(bf16)
        for two in (low[:2], low[2:], high)
    ]


def head_slots(parts, h):
    p, q = divmod(h, 2)

    def take(part, q):
        part = part.astype(f32)[:, 8 * q : 8 * q + 8, :]
        return part.reshape(part.shape[0] * 8, part.shape[2]).astype(bf16)

    return take(parts[p], q), take(parts[2], p)


def unpack_body(index_rows, parts, h, tokens):
    low, high = head_slots(parts, h)
    token = iota((tokens, index_rows.shape[1]), 0)
    row_low = index_rows[h : h + 1, :]
    row_high = index_rows[4 + h // 2 : 5 + h // 2, :]
    return dot_nn(onehot(token == row_low), low) + dot_nn(
        onehot(token + (h % 2) * tokens == row_high), high
    )


def compact(cols, parts, h, slots):
    low, high = head_slots(parts, h)
    count = cols.shape[0]
    slot = iota((count, slots), 1)
    return (
        dot_nn(onehot(cols[:, 3 * h + 1 : 3 * h + 2] == slot), low)
        + dot_nn(onehot(cols[:, 3 * h + 2 : 3 * h + 3] == slot), high)
    ).astype(bf16)


def weights_of(rows, cols, query, key, h, scaling):
    scores = dot_nt(key, query) * scaling
    allowed = cols[:, 3 * h : 3 * h + 1] <= rows[3 * h : 3 * h + 1, :]
    scores = jnp.where(allowed, scores, -jnp.inf)
    highest = jnp.max(scores, axis=0, keepdims=True)
    weights = jnp.exp(scores - highest)
    return weights * (1.0 / jnp.sum(weights, axis=0, keepdims=True))


def spread(rows, h, transposed, plain):
    slots = rows.shape[1]
    slot = iota((slots, rows.shape[1]), 0)
    out = []
    for k in (1, 2):
        pick = onehot(slot == rows[3 * h + k : 3 * h + k + 1, :])
        got = [dot_nt(pick, t) for t in transposed] + [dot_nn(pick, v) for v in plain]
        out.append(jnp.concatenate(got, axis=1) if len(got) > 1 else got[0])
    return out


def gathered_parts(results):
    def part(value):
        return value.reshape(value.shape[0] // LOW, LOW, value.shape[1])

    low = [part(r[0]) for r in results]
    high = [part(results[2 * p][1] + results[2 * p + 1][1]) for p in range(2)]
    return [
        jnp.concatenate(two, axis=1).astype(bf16)
        for two in (low[:2], low[2:], high)
    ]


def prep_kernel(tok_rows, members_ref, table_ref, rows_ref):
    table, rows = prep_body(members_ref[:, 0, :].astype(f32), table_ref.shape[0], tok_rows)
    table_ref[...] = table.astype(jnp.int32)
    rows_ref[...] = rows


def load_parts(ref):
    return [ref[:, 16 * k : 16 * k + 16, :] for k in range(3)]


def store_parts(ref, parts):
    for k in range(3):
        ref[:, 16 * k : 16 * k + 16, :] = parts[k]


def pack_kernel(index_ref, *refs):
    *source_refs, out_ref = refs
    sources = []
    for h in range(4):
        got = [r[:, 128 * h : 128 * h + 128] for r in source_refs]
        sources.append(jnp.concatenate(got, axis=1) if len(got) > 1 else got[0])
    store_parts(out_ref, pack_body(index_ref[...].astype(f32), sources))


def unpack_kernel(index_ref, packed_ref, *out_refs):
    parts = load_parts(packed_ref)
    index_rows = index_ref[...].astype(f32)
    for h in range(4):
        got = unpack_body(index_rows, parts, h, out_refs[0].shape[0]).astype(bf16)
        for k, ref in enumerate(out_refs):
            ref[:, 128 * h : 128 * h + 128] = got[:, 128 * k : 128 * k + 128]


def forward_kernel(scaling, rows_ref, centroids_ref, qkv_ref, out_ref, centers_ref):
    rows = rows_ref[...]
    cols = columns_of(rows)
    parts = load_parts(qkv_ref)
    slots = qkv_ref.shape[0] * LOW
    count = rows.shape[1]
    results = []
    for h in range(4):
        got = compact(cols, parts, h, slots)
        query, key, value = (got[:, 128 * k : 128 * k + 128] for k in range(3))
        keys = key.astype(f32)
        unit = keys / jnp.sqrt(jnp.mean(keys * keys, axis=1, keepdims=True) + epsilon)
        mixed = 0.5 * centroids_ref[h : h + 1, :] + 0.5 * jnp.sum(
            unit, axis=0, keepdims=True
        ) * (1.0 / count)
        centers_ref[h : h + 1, :] = mixed / jnp.sqrt(
            jnp.mean(mixed * mixed, axis=1, keepdims=True) + epsilon
        )
        weights = weights_of(rows, cols, query, key, h, scaling).astype(bf16)
        attended = dot_nn(value.T, weights).astype(bf16)
        results.append(spread(rows, h, [attended], []))
    store_parts(out_ref, gathered_parts(results))


def backward_kernel(scaling, rows_ref, qkv_ref, grad_ref, out_ref):
    rows = rows_ref[...]
    cols = columns_of(rows)
    parts = load_parts(qkv_ref)
    grad_parts = load_parts(grad_ref)
    slots = qkv_ref.shape[0] * LOW
    results = []
    for h in range(4):
        got = compact(cols, parts, h, slots)
        query, key, value = (got[:, 128 * k : 128 * k + 128] for k in range(3))
        grad = compact(cols, grad_parts, h, slots)
        weights = weights_of(rows, cols, query, key, h, scaling)
        weights_b = weights.astype(bf16)
        attended = dot_nn(value.T, weights_b)
        grad_t = grad.astype(f32).T
        delta = jnp.sum(grad_t * attended, axis=0, keepdims=True)
        probs = dot_nt(value, grad)
        dscore = (weights * (probs - delta) * scaling).astype(bf16)
        query_g = dot_nn(key.T, dscore).astype(bf16)
        key_g = dot_nn(dscore, query).astype(bf16)
        value_g = dot_nn(weights_b, grad).astype(bf16)
        results.append(spread(rows, h, [query_g], [jnp.concatenate([key_g, value_g], axis=1)]))
    store_parts(out_ref, gathered_parts(results))


def call(kernel, outs, flops, *args):
    size = sum(a.size * a.dtype.itemsize for a in args)
    size += sum(o.size * o.dtype.itemsize for o in outs)
    whole = pl.BlockSpec(memory_space=pltpu.VMEM)
    got = pl.pallas_call(
        kernel,
        out_shape=outs,
        in_specs=[whole] * len(args),
        out_specs=[whole] * len(outs),
        compiler_params=pltpu.CompilerParams(vmem_limit_bytes=VMEM),
        cost_estimate=pl.CostEstimate(flops=flops, bytes_accessed=size, transcendentals=0),
    )(*args)
    return got[0] if len(outs) == 1 else got


def shape_of(dims, dtype):
    return jax.ShapeDtypeStruct(dims, dtype)


def shifted(x, axis, step, unit=1):
    n = lax.axis_size(axis)
    return lax.ppermute(x, axis, [(i, (i + step * unit) % n) for i in range(n)])


def swapped(x):
    n = lax.axis_size("ctx")
    return lax.ppermute(x, "ctx", [(i, i ^ 1) for i in range(n)])


def neighbour_tokens(out_grad):
    n = lax.axis_size("mp")
    return shifted(out_grad, "mp", 1), shifted(out_grad, "mp", n - 1)


def all_tokens(out_grad, before, after):
    n = lax.axis_size("mp")
    me = lax.axis_index("mp")
    rows, width = out_grad.shape
    half = rows // 2
    upper = shifted(before[:half], "mp", 1)
    lower = shifted(after[half:], "mp", n - 1)
    full = jnp.zeros((rows, n * width), out_grad.dtype)
    full = lax.dynamic_update_slice(full, out_grad, (0, me * width))
    full = lax.dynamic_update_slice(full, before, (0, (me + n - 1) % n * width))
    full = lax.dynamic_update_slice(full, after, (0, (me + 1) % n * width))
    opposite = (me + 2) % n * width
    full = lax.dynamic_update_slice(full, upper, (0, opposite))
    return lax.dynamic_update_slice(full, lower, (half, opposite))


def ctx_weight(part):
    rows, width = part.shape
    chips = lax.axis_size("ctx") // 2
    index = lax.axis_index("ctx")
    chip, core = index // 2, index % 2
    mine = jnp.zeros((chips, 1, rows, width), part.dtype)
    for k in range(chips):
        piece = shifted(part, "ctx", k, 2) if k else part
        mine = lax.dynamic_update_slice(
            mine, piece[None, None], ((chip + chips - k) % chips, 0, 0, 0)
        )
    other = swapped(mine)
    full = jnp.zeros((chips, 2, rows, width), part.dtype)
    full = lax.dynamic_update_slice(full, mine, (0, core, 0, 0))
    full = lax.dynamic_update_slice(full, other, (0, 1 - core, 0, 0))
    return full.reshape(chips * 2 * rows, width)


def scatter_sum(partial):
    ctx, clu = lax.axis_size("ctx"), lax.axis_size("clu")
    chips = ctx // 2
    index = lax.axis_index("ctx")
    chip, core = index // 2, index % 2
    place = lax.axis_index("clu")
    rows = partial.shape[0] // ctx // clu
    width = partial.shape[1]
    shares = partial.reshape(chips, 2, clu * rows, width)

    def pick(x, i, dim):
        return lax.dynamic_index_in_dim(x, i, dim, keepdims=False)

    other = swapped(pick(shares, 1 - core, 1).astype(bf16))
    shares = pick(shares, core, 1) + other.astype(f32)
    total = pick(shares, chip, 0)
    for k in range(1, chips):
        piece = pick(shares, (chip + k) % chips, 0).astype(bf16)
        total = total + shifted(piece, "ctx", k, 2).astype(f32)
    pairs = clu // 2
    shares = total.reshape(pairs, 2, rows, width)
    total = pick(shares, place // 2, 0)
    for k in range(1, pairs):
        piece = pick(shares, (place // 2 + k) % pairs, 0).astype(bf16)
        total = total + shifted(piece, "clu", k, 2).astype(f32)
    return total


def scatter_last(shares):
    clu = lax.axis_size("clu")
    bit = lax.axis_index("clu") % 2
    piece = lax.dynamic_index_in_dim(shares, 1 - bit, 0, keepdims=False).astype(bf16)
    other = lax.ppermute(piece, "clu", [(i, i ^ 1) for i in range(clu)])
    return lax.dynamic_index_in_dim(shares, bit, 0, keepdims=False) + other.astype(f32)


def exchange(x):
    return lax.all_to_all(x, GROUP, split_axis=0, concat_axis=0, tiled=True)


def per_device(queries, tok_keys, tok_values, out_grad, out_weight, membership, centroids):
    tok_rows, width = queries.shape
    heads = membership.shape[0]
    count = membership.shape[2]
    head_size = width // heads
    owners = lax.axis_size(GROUP)
    pair_rows = heads * CAP
    slots = owners * LOW
    scaling = head_size ** (-0.5)

    table, rows = call(
        functools.partial(prep_kernel, tok_rows),
        [shape_of((owners, 128), jnp.int32), shape_of((16, count), f32)],
        10**8,
        membership,
    )
    before, after = neighbour_tokens(out_grad)
    weight_part = lax.all_gather(out_weight.T, "clu", axis=0, tiled=True)
    table = exchange(table)
    index_low = table[:, : heads * LOW].reshape(owners, heads, LOW)
    index_high = table[:, heads * LOW : pair_rows].reshape(owners, heads // 2, LOW)
    index_rows = jnp.concatenate([index_low, index_high, index_high], axis=1)
    index_rows = index_rows.transpose(1, 0, 2).reshape(2 * heads, slots)
    index_rows, before, after = lax.optimization_barrier((index_rows, before, after))

    def packed_shape(n):
        return shape_of((owners, pair_rows, n * head_size), bf16)

    def pack(*sources):
        n = len(sources)
        return call(pack_kernel, [packed_shape(n)], n * 10**9, index_rows, *sources)

    def unpack(packed, n):
        outs = [shape_of((tok_rows, width), bf16)] * n
        return call(unpack_kernel, outs, n * 10**9, index_rows, packed)

    got_qkv = exchange(pack(queries, tok_keys, tok_values))
    grad_full = all_tokens(out_grad, before, after)
    weight_full = ctx_weight(weight_part)
    head_grad = dot_nn(grad_full, weight_full).astype(bf16)
    got_grad = exchange(pack(head_grad))

    attended, centers = call(
        functools.partial(forward_kernel, scaling),
        [packed_shape(1), shape_of((heads, head_size), f32)],
        4 * 10**9,
        rows,
        centroids[:, 0, :],
        got_qkv,
    )
    back_out = exchange(attended)
    grads = call(
        functools.partial(backward_kernel, scaling),
        [packed_shape(3)],
        8 * 10**9,
        rows,
        got_qkv,
        got_grad,
    )
    back_grads = exchange(grads)
    attn_out = unpack(back_out, 1)
    partial = lax.dot_general(
        grad_full, attn_out, (((0,), (0,)), ((), ())), preferred_element_type=f32
    )
    back_grads, shares = lax.optimization_barrier((back_grads, scatter_sum(partial)))
    share = scatter_last(shares)
    query_g, key_g, value_g = unpack(back_grads, 3)
    return (query_g, key_g, value_g, share.T, centers[:, None, :])


def solution(mesh):
    token = P(GROUP, "mp")
    owner = P("mp", GROUP, None)
    return jax.shard_map(
        per_device,
        mesh=mesh,
        in_specs=(token, token, token, token, P("mp", GROUP), owner, owner),
        out_specs=(token, token, token, P("mp", GROUP), owner),
        check_vma=False,
    )
```

```python
import functools

import jax
import jax.numpy as jnp
from jax import lax
from jax.experimental import pallas as pl
from jax.experimental.pallas import tpu as pltpu
from jax.sharding import PartitionSpec as P

epsilon = 1e-06
GROUP = ("ctx", "clu")
CAP = 12
LOW = 8
VMEM = 56 * 1024 * 1024
f32 = jnp.float32
bf16 = jnp.bfloat16


def dot_nn(a, b):
    return lax.dot_general(a, b, (((1,), (0,)), ((), ())), preferred_element_type=f32)


def dot_nt(a, b):
    return lax.dot_general(a, b, (((1,), (1,)), ((), ())), preferred_element_type=f32)


def iota(shape, dim):
    return lax.broadcasted_iota(jnp.int32, shape, dim).astype(f32)


def columns_of(rows):
    copies = 128 // rows.shape[0]
    return jnp.concatenate([rows] * copies, axis=0).T


def onehot(mask):
    return jnp.where(mask, 1.0, 0.0).astype(bf16)


def prep_body(members, blocks, tok_rows):
    heads, count = members.shape
    pieces, rows = [], []
    lane = iota((1, count), 1)
    block_col = iota((blocks, count), 0)
    for h in range(heads):
        member = members[h : h + 1, :]
        block = jnp.floor(member * (1.0 / tok_rows))
        local = member - block * tok_rows
        here = block == block_col
        start_of = jnp.sum(jnp.where(block < block_col, 1.0, 0.0), axis=1, keepdims=True)
        start = jnp.sum(jnp.where(here, start_of, 0.0), axis=0, keepdims=True)
        rank = lane - start
        low = block * LOW + rank
        high = block * LOW + (h % 2) * (CAP - LOW) + (rank - LOW)
        rows += [member, jnp.where(rank < LOW, low, -1.0), jnp.where(rank >= LOW, high, -1.0)]
        at_rank = rank == iota((16, count), 0)
        large = jnp.floor(local * (1.0 / 32))
        small = local - large * 32
        right = jnp.concatenate(
            [
                jnp.where(at_rank, large, 0.0),
                jnp.where(at_rank, small, 0.0),
                jnp.where(at_rank, 1.0, 0.0),
                jnp.zeros((80, count), f32),
            ],
            axis=0,
        ).astype(bf16)
        got = dot_nt(onehot(here), right)
        value = got[:, 0:16] * 32 + got[:, 16:32]
        filled = got[:, 32:48] > 0.5
        pieces.append((value, filled))
    low_cols = [jnp.where(f, v, -1.0)[:, :LOW] for v, f in pieces]
    high_cols = [
        jnp.where(f, v + (h % 2) * tok_rows, -1.0)[:, LOW:CAP]
        for h, (v, f) in enumerate(pieces)
    ]
    used = heads * CAP
    table = jnp.concatenate(
        low_cols + high_cols + [jnp.full((blocks, 128 - used), -1.0, f32)], axis=1
    )
    return table, jnp.concatenate(rows + [jnp.zeros((4, count), f32)], axis=0)


def pack_body(index_rows, sources):
    cols = columns_of(index_rows)
    tokens = sources[0].shape[0]
    slots = index_rows.shape[1]
    n = sources[0].shape[1]
    token = iota((slots, tokens), 1)

    def part(value):
        return value.reshape(slots // LOW, LOW, n)

    low = [
        part(dot_nn(onehot(cols[:, h : h + 1] == token), sources[h]))
        for h in range(4)
    ]
    high = []
    for p in range(2):
        col = cols[:, 4 + p : 5 + p]
        high.append(
            part(
                dot_nn(onehot(col == token), sources[2 * p])
                + dot_nn(onehot(col == token + tokens), sources[2 * p + 1])
            )
        )
    return [
        jnp.concatenate(two, axis=1).astype(bf16)
        for two in (low[:2], low[2:], high)
    ]


def head_slots(parts, h):
    p, q = divmod(h, 2)

    def take(part, q):
        part = part.astype(f32)[:, 8 * q : 8 * q + 8, :]
        return part.reshape(part.shape[0] * 8, part.shape[2]).astype(bf16)

    return take(parts[p], q), take(parts[2], p)


def unpack_body(index_rows, parts, h, tokens):
    low, high = head_slots(parts, h)
    token = iota((tokens, index_rows.shape[1]), 0)
    row_low = index_rows[h : h + 1, :]
    row_high = index_rows[4 + h // 2 : 5 + h // 2, :]
    return dot_nn(onehot(token == row_low), low) + dot_nn(
        onehot(token + (h % 2) * tokens == row_high), high
    )


def compact(cols, parts, h, slots):
    low, high = head_slots(parts, h)
    count = cols.shape[0]
    slot = iota((count, slots), 1)
    return (
        dot_nn(onehot(cols[:, 3 * h + 1 : 3 * h + 2] == slot), low)
        + dot_nn(onehot(cols[:, 3 * h + 2 : 3 * h + 3] == slot), high)
    ).astype(bf16)


def weights_of(rows, cols, query, key, h, scaling):
    scores = dot_nt(key, query) * scaling
    allowed = cols[:, 3 * h : 3 * h + 1] <= rows[3 * h : 3 * h + 1, :]
    scores = jnp.where(allowed, scores, -jnp.inf)
    highest = jnp.max(scores, axis=0, keepdims=True)
    weights = jnp.exp(scores - highest)
    return weights * (1.0 / jnp.sum(weights, axis=0, keepdims=True))


def spread(rows, h, transposed, plain):
    slots = rows.shape[1]
    slot = iota((slots, rows.shape[1]), 0)
    out = []
    for k in (1, 2):
        pick = onehot(slot == rows[3 * h + k : 3 * h + k + 1, :])
        got = [dot_nt(pick, t) for t in transposed] + [dot_nn(pick, v) for v in plain]
        out.append(jnp.concatenate(got, axis=1) if len(got) > 1 else got[0])
    return out


def gathered_parts(results):
    def part(value):
        return value.reshape(value.shape[0] // LOW, LOW, value.shape[1])

    low = [part(r[0]) for r in results]
    high = [part(results[2 * p][1] + results[2 * p + 1][1]) for p in range(2)]
    return [
        jnp.concatenate(two, axis=1).astype(bf16)
        for two in (low[:2], low[2:], high)
    ]


def prep_kernel(tok_rows, members_ref, table_ref, rows_ref):
    table, rows = prep_body(members_ref[:, 0, :].astype(f32), table_ref.shape[0], tok_rows)
    table_ref[...] = table.astype(jnp.int32)
    rows_ref[...] = rows


def load_parts(ref):
    return [ref[:, 16 * k : 16 * k + 16, :] for k in range(3)]


def store_parts(ref, parts):
    for k in range(3):
        ref[:, 16 * k : 16 * k + 16, :] = parts[k]


def pack_kernel(index_ref, *refs):
    *source_refs, out_ref = refs
    sources = []
    for h in range(4):
        got = [r[:, 128 * h : 128 * h + 128] for r in source_refs]
        sources.append(jnp.concatenate(got, axis=1) if len(got) > 1 else got[0])
    store_parts(out_ref, pack_body(index_ref[...].astype(f32), sources))


def unpack_kernel(index_ref, packed_ref, *out_refs):
    parts = load_parts(packed_ref)
    index_rows = index_ref[...].astype(f32)
    for h in range(4):
        got = unpack_body(index_rows, parts, h, out_refs[0].shape[0]).astype(bf16)
        for k, ref in enumerate(out_refs):
            ref[:, 128 * h : 128 * h + 128] = got[:, 128 * k : 128 * k + 128]


def forward_kernel(scaling, rows_ref, centroids_ref, qkv_ref, out_ref, centers_ref):
    rows = rows_ref[...]
    cols = columns_of(rows)
    parts = load_parts(qkv_ref)
    slots = qkv_ref.shape[0] * LOW
    count = rows.shape[1]
    results = []
    for h in range(4):
        got = compact(cols, parts, h, slots)
        query, key, value = (got[:, 128 * k : 128 * k + 128] for k in range(3))
        keys = key.astype(f32)
        unit = keys / jnp.sqrt(jnp.mean(keys * keys, axis=1, keepdims=True) + epsilon)
        mixed = 0.5 * centroids_ref[h : h + 1, :] + 0.5 * jnp.sum(
            unit, axis=0, keepdims=True
        ) * (1.0 / count)
        centers_ref[h : h + 1, :] = mixed / jnp.sqrt(
            jnp.mean(mixed * mixed, axis=1, keepdims=True) + epsilon
        )
        weights = weights_of(rows, cols, query, key, h, scaling).astype(bf16)
        attended = dot_nn(value.T, weights).astype(bf16)
        results.append(spread(rows, h, [attended], []))
    store_parts(out_ref, gathered_parts(results))


def backward_kernel(scaling, rows_ref, qkv_ref, grad_ref, out_ref):
    rows = rows_ref[...]
    cols = columns_of(rows)
    parts = load_parts(qkv_ref)
    grad_parts = load_parts(grad_ref)
    slots = qkv_ref.shape[0] * LOW
    results = []
    for h in range(4):
        got = compact(cols, parts, h, slots)
        query, key, value = (got[:, 128 * k : 128 * k + 128] for k in range(3))
        grad = compact(cols, grad_parts, h, slots)
        weights = weights_of(rows, cols, query, key, h, scaling)
        weights_b = weights.astype(bf16)
        attended = dot_nn(value.T, weights_b)
        grad_t = grad.astype(f32).T
        delta = jnp.sum(grad_t * attended, axis=0, keepdims=True)
        probs = dot_nt(value, grad)
        dscore = (weights * (probs - delta) * scaling).astype(bf16)
        query_g = dot_nn(key.T, dscore).astype(bf16)
        key_g = dot_nn(dscore, query).astype(bf16)
        value_g = dot_nn(weights_b, grad).astype(bf16)
        results.append(spread(rows, h, [query_g], [jnp.concatenate([key_g, value_g], axis=1)]))
    store_parts(out_ref, gathered_parts(results))


def call(kernel, outs, flops, *args):
    size = sum(a.size * a.dtype.itemsize for a in args)
    size += sum(o.size * o.dtype.itemsize for o in outs)
    whole = pl.BlockSpec(memory_space=pltpu.VMEM)
    got = pl.pallas_call(
        kernel,
        out_shape=outs,
        in_specs=[whole] * len(args),
        out_specs=[whole] * len(outs),
        compiler_params=pltpu.CompilerParams(vmem_limit_bytes=VMEM),
        cost_estimate=pl.CostEstimate(flops=flops, bytes_accessed=size, transcendentals=0),
    )(*args)
    return got[0] if len(outs) == 1 else got


def shape_of(dims, dtype):
    return jax.ShapeDtypeStruct(dims, dtype)


def shifted(x, axis, step, unit=1):
    n = lax.axis_size(axis)
    return lax.ppermute(x, axis, [(i, (i + step * unit) % n) for i in range(n)])


def swapped(x):
    n = lax.axis_size("ctx")
    return lax.ppermute(x, "ctx", [(i, i ^ 1) for i in range(n)])


def neighbour_tokens(out_grad):
    n = lax.axis_size("mp")
    return shifted(out_grad, "mp", 1), shifted(out_grad, "mp", n - 1)


def all_tokens(out_grad, before, after):
    n = lax.axis_size("mp")
    me = lax.axis_index("mp")
    rows, width = out_grad.shape
    half = rows // 2
    upper = shifted(before[:half], "mp", 1)
    lower = shifted(after[half:], "mp", n - 1)
    full = jnp.zeros((rows, n * width), out_grad.dtype)
    full = lax.dynamic_update_slice(full, out_grad, (0, me * width))
    full = lax.dynamic_update_slice(full, before, (0, (me + n - 1) % n * width))
    full = lax.dynamic_update_slice(full, after, (0, (me + 1) % n * width))
    opposite = (me + 2) % n * width
    full = lax.dynamic_update_slice(full, upper, (0, opposite))
    return lax.dynamic_update_slice(full, lower, (half, opposite))


def clu_weight_parts(weight):
    n = lax.axis_size("clu")
    pair = lax.axis_index("clu") // 2
    rows, width = weight.shape
    mine = jnp.zeros((n // 2, 1, rows, width), weight.dtype)
    for k in range(n // 2):
        part = shifted(weight, "clu", k, 2) if k else weight
        mine = lax.dynamic_update_slice(
            mine, part[None, None], ((pair + n // 2 - k) % (n // 2), 0, 0, 0)
        )
    return mine, lax.ppermute(mine, "clu", [(i, i ^ 1) for i in range(n)])


def clu_weight(parts):
    mine, other = parts
    bit = lax.axis_index("clu") % 2
    pairs, _, rows, width = mine.shape
    full = jnp.zeros((pairs, 2, rows, width), mine.dtype)
    full = lax.dynamic_update_slice(full, mine, (0, bit, 0, 0))
    full = lax.dynamic_update_slice(full, other, (0, 1 - bit, 0, 0))
    return full.reshape(2 * pairs * rows, width)


def ctx_weight(part):
    rows, width = part.shape
    chips = lax.axis_size("ctx") // 2
    index = lax.axis_index("ctx")
    chip, core = index // 2, index % 2
    mine = jnp.zeros((chips, 1, rows, width), part.dtype)
    for k in range(chips):
        piece = shifted(part, "ctx", k, 2) if k else part
        mine = lax.dynamic_update_slice(
            mine, piece[None, None], ((chip + chips - k) % chips, 0, 0, 0)
        )
    other = swapped(mine)
    full = jnp.zeros((chips, 2, rows, width), part.dtype)
    full = lax.dynamic_update_slice(full, mine, (0, core, 0, 0))
    full = lax.dynamic_update_slice(full, other, (0, 1 - core, 0, 0))
    return full.reshape(chips * 2 * rows, width)


def scatter_sum(partial):
    ctx, clu = lax.axis_size("ctx"), lax.axis_size("clu")
    chips = ctx // 2
    index = lax.axis_index("ctx")
    chip, core = index // 2, index % 2
    place = lax.axis_index("clu")
    rows = partial.shape[0] // ctx // clu
    width = partial.shape[1]
    shares = partial.reshape(chips, 2, clu * rows, width)

    def pick(x, i, dim):
        return lax.dynamic_index_in_dim(x, i, dim, keepdims=False)

    other = swapped(pick(shares, 1 - core, 1).astype(bf16))
    shares = pick(shares, core, 1) + other.astype(f32)
    total = pick(shares, chip, 0)
    for k in range(1, chips):
        piece = pick(shares, (chip + k) % chips, 0).astype(bf16)
        total = total + shifted(piece, "ctx", k, 2).astype(f32)
    pairs = clu // 2
    shares = total.reshape(pairs, 2, rows, width)
    total = pick(shares, place // 2, 0)
    for k in range(1, pairs):
        piece = pick(shares, (place // 2 + k) % pairs, 0).astype(bf16)
        total = total + shifted(piece, "clu", k, 2).astype(f32)
    return total


def scatter_last(shares):
    clu = lax.axis_size("clu")
    bit = lax.axis_index("clu") % 2
    piece = lax.dynamic_index_in_dim(shares, 1 - bit, 0, keepdims=False).astype(bf16)
    other = lax.ppermute(piece, "clu", [(i, i ^ 1) for i in range(clu)])
    return lax.dynamic_index_in_dim(shares, bit, 0, keepdims=False) + other.astype(f32)


def exchange(x):
    return lax.all_to_all(x, GROUP, split_axis=0, concat_axis=0, tiled=True)


def per_device(queries, tok_keys, tok_values, out_grad, out_weight, membership, centroids):
    tok_rows, width = queries.shape
    heads = membership.shape[0]
    count = membership.shape[2]
    head_size = width // heads
    owners = lax.axis_size(GROUP)
    pair_rows = heads * CAP
    slots = owners * LOW
    scaling = head_size ** (-0.5)

    table, rows = call(
        functools.partial(prep_kernel, tok_rows),
        [shape_of((owners, 128), jnp.int32), shape_of((16, count), f32)],
        10**8,
        membership,
    )
    before, after = neighbour_tokens(out_grad)
    weight_parts = clu_weight_parts(out_weight.T)
    table = exchange(table)
    index_low = table[:, : heads * LOW].reshape(owners, heads, LOW)
    index_high = table[:, heads * LOW : pair_rows].reshape(owners, heads // 2, LOW)
    index_rows = jnp.concatenate([index_low, index_high, index_high], axis=1)
    index_rows = index_rows.transpose(1, 0, 2).reshape(2 * heads, slots)
    index_rows, before, after, weight_parts = lax.optimization_barrier(
        (index_rows, before, after, weight_parts)
    )

    def packed_shape(n):
        return shape_of((owners, pair_rows, n * head_size), bf16)

    def pack(*sources):
        n = len(sources)
        return call(pack_kernel, [packed_shape(n)], n * 10**9, index_rows, *sources)

    def unpack(packed, n):
        outs = [shape_of((tok_rows, width), bf16)] * n
        return call(unpack_kernel, outs, n * 10**9, index_rows, packed)

    got_qkv = exchange(pack(queries, tok_keys, tok_values))
    grad_full = all_tokens(out_grad, before, after)
    weight_full = ctx_weight(clu_weight(weight_parts))
    head_grad = dot_nn(grad_full, weight_full).astype(bf16)
    got_grad = exchange(pack(head_grad))

    attended, centers = call(
        functools.partial(forward_kernel, scaling),
        [packed_shape(1), shape_of((heads, head_size), f32)],
        4 * 10**9,
        rows,
        centroids[:, 0, :],
        got_qkv,
    )
    back_out = exchange(attended)
    grads = call(
        functools.partial(backward_kernel, scaling),
        [packed_shape(3)],
        8 * 10**9,
        rows,
        got_qkv,
        got_grad,
    )
    back_grads = exchange(grads)
    attn_out = unpack(back_out, 1)
    partial = lax.dot_general(
        grad_full, attn_out, (((0,), (0,)), ((), ())), preferred_element_type=f32
    )
    back_grads, shares = lax.optimization_barrier((back_grads, scatter_sum(partial)))
    share = scatter_last(shares)
    query_g, key_g, value_g = unpack(back_grads, 3)
    return (query_g, key_g, value_g, share.T, centers[:, None, :])


def solution(mesh):
    token = P(GROUP, "mp")
    owner = P("mp", GROUP, None)
    return jax.shard_map(
        per_device,
        mesh=mesh,
        in_specs=(token, token, token, token, P("mp", GROUP), owner, owner),
        out_specs=(token, token, token, P("mp", GROUP), owner),
        check_vma=False,
    )
```

```python
import functools

import jax
import jax.numpy as jnp
from jax import lax
from jax.experimental import pallas as pl
from jax.experimental.pallas import tpu as pltpu
from jax.sharding import PartitionSpec as P

epsilon = 1e-06
GROUP = ("ctx", "clu")
CAP = 12
LOW = 8
VMEM = 24 * 1024 * 1024
f32 = jnp.float32
bf16 = jnp.bfloat16


def dot_nn(a, b):
    return lax.dot_general(a, b, (((1,), (0,)), ((), ())), preferred_element_type=f32)


def dot_nt(a, b):
    return lax.dot_general(a, b, (((1,), (1,)), ((), ())), preferred_element_type=f32)


def iota(shape, dim):
    return lax.broadcasted_iota(jnp.int32, shape, dim).astype(f32)


def columns_of(rows):
    copies = 128 // rows.shape[0]
    return jnp.concatenate([rows] * copies, axis=0).T


def onehot(mask):
    return jnp.where(mask, 1.0, 0.0).astype(bf16)


def prep_body(members, blocks, tok_rows):
    heads, count = members.shape
    pieces, rows = [], []
    lane = iota((1, count), 1)
    block_col = iota((blocks, count), 0)
    for h in range(heads):
        member = members[h : h + 1, :]
        block = jnp.floor(member * (1.0 / tok_rows))
        local = member - block * tok_rows
        here = block == block_col
        start_of = jnp.sum(jnp.where(block < block_col, 1.0, 0.0), axis=1, keepdims=True)
        start = jnp.sum(jnp.where(here, start_of, 0.0), axis=0, keepdims=True)
        rank = lane - start
        low = block * LOW + rank
        high = block * LOW + (h % 2) * (CAP - LOW) + (rank - LOW)
        rows += [member, jnp.where(rank < LOW, low, -1.0), jnp.where(rank >= LOW, high, -1.0)]
        at_rank = rank == iota((16, count), 0)
        large = jnp.floor(local * (1.0 / 32))
        small = local - large * 32
        right = jnp.concatenate(
            [
                jnp.where(at_rank, large, 0.0),
                jnp.where(at_rank, small, 0.0),
                jnp.where(at_rank, 1.0, 0.0),
                jnp.zeros((80, count), f32),
            ],
            axis=0,
        ).astype(bf16)
        got = dot_nt(onehot(here), right)
        value = got[:, 0:16] * 32 + got[:, 16:32]
        filled = got[:, 32:48] > 0.5
        pieces.append((value, filled))
    low_cols = [jnp.where(f, v, -1.0)[:, :LOW] for v, f in pieces]
    high_cols = [
        jnp.where(f, v + (h % 2) * tok_rows, -1.0)[:, LOW:CAP]
        for h, (v, f) in enumerate(pieces)
    ]
    used = heads * CAP
    table = jnp.concatenate(
        low_cols + high_cols + [jnp.full((blocks, 128 - used), -1.0, f32)], axis=1
    )
    return table, jnp.concatenate(rows + [jnp.zeros((4, count), f32)], axis=0)


def pack_body(index_rows, sources):
    cols = columns_of(index_rows)
    tokens = sources[0].shape[0]
    slots = index_rows.shape[1]
    n = sources[0].shape[1]
    token = iota((slots, tokens), 1)

    def part(value):
        return value.reshape(slots // LOW, LOW, n)

    low = [
        part(dot_nn(onehot(cols[:, h : h + 1] == token), sources[h]))
        for h in range(4)
    ]
    high = []
    for p in range(2):
        col = cols[:, 4 + p : 5 + p]
        high.append(
            part(
                dot_nn(onehot(col == token), sources[2 * p])
                + dot_nn(onehot(col == token + tokens), sources[2 * p + 1])
            )
        )
    return [
        jnp.concatenate(two, axis=1).astype(bf16)
        for two in (low[:2], low[2:], high)
    ]


def head_slots(parts, h):
    p, q = divmod(h, 2)

    def take(part, q):
        part = part.astype(f32)[:, 8 * q : 8 * q + 8, :]
        return part.reshape(part.shape[0] * 8, part.shape[2]).astype(bf16)

    return take(parts[p], q), take(parts[2], p)


def unpack_body(index_rows, parts, h, tokens):
    low, high = head_slots(parts, h)
    token = iota((tokens, index_rows.shape[1]), 0)
    row_low = index_rows[h : h + 1, :]
    row_high = index_rows[4 + h // 2 : 5 + h // 2, :]
    return dot_nn(onehot(token == row_low), low) + dot_nn(
        onehot(token + (h % 2) * tokens == row_high), high
    )


def compact(cols, parts, h, slots):
    low, high = head_slots(parts, h)
    count = cols.shape[0]
    slot = iota((count, slots), 1)
    return (
        dot_nn(onehot(cols[:, 3 * h + 1 : 3 * h + 2] == slot), low)
        + dot_nn(onehot(cols[:, 3 * h + 2 : 3 * h + 3] == slot), high)
    ).astype(bf16)


def weights_of(rows, cols, query, key, h, scaling):
    scores = dot_nt(key, query) * scaling
    allowed = cols[:, 3 * h : 3 * h + 1] <= rows[3 * h : 3 * h + 1, :]
    scores = jnp.where(allowed, scores, -jnp.inf)
    highest = jnp.max(scores, axis=0, keepdims=True)
    weights = jnp.exp(scores - highest)
    return weights * (1.0 / jnp.sum(weights, axis=0, keepdims=True))


def spread(rows, h, transposed, plain):
    slots = rows.shape[1]
    slot = iota((slots, rows.shape[1]), 0)
    out = []
    for k in (1, 2):
        pick = onehot(slot == rows[3 * h + k : 3 * h + k + 1, :])
        got = [dot_nt(pick, t) for t in transposed] + [dot_nn(pick, v) for v in plain]
        out.append(jnp.concatenate(got, axis=1) if len(got) > 1 else got[0])
    return out


def gathered_parts(results):
    def part(value):
        return value.reshape(value.shape[0] // LOW, LOW, value.shape[1])

    low = [part(r[0]) for r in results]
    high = [part(results[2 * p][1] + results[2 * p + 1][1]) for p in range(2)]
    return [
        jnp.concatenate(two, axis=1).astype(bf16)
        for two in (low[:2], low[2:], high)
    ]


def prep_kernel(tok_rows, members_ref, table_ref, rows_ref):
    table, rows = prep_body(members_ref[:, 0, :].astype(f32), table_ref.shape[0], tok_rows)
    table_ref[...] = table.astype(jnp.int32)
    rows_ref[...] = rows


def load_parts(ref):
    return [ref[:, 16 * k : 16 * k + 16, :] for k in range(3)]


def store_parts(ref, parts):
    for k in range(3):
        ref[:, 16 * k : 16 * k + 16, :] = parts[k]


def pack_kernel(index_ref, *refs):
    *source_refs, out_ref = refs
    sources = []
    for h in range(4):
        got = [r[:, 128 * h : 128 * h + 128] for r in source_refs]
        sources.append(jnp.concatenate(got, axis=1) if len(got) > 1 else got[0])
    store_parts(out_ref, pack_body(index_ref[...].astype(f32), sources))


def unpack_kernel(index_ref, packed_ref, *out_refs):
    parts = load_parts(packed_ref)
    index_rows = index_ref[...].astype(f32)
    for h in range(4):
        got = unpack_body(index_rows, parts, h, out_refs[0].shape[0]).astype(bf16)
        for k, ref in enumerate(out_refs):
            ref[:, 128 * h : 128 * h + 128] = got[:, 128 * k : 128 * k + 128]


def forward_kernel(scaling, rows_ref, centroids_ref, qkv_ref, out_ref, centers_ref):
    rows = rows_ref[...]
    cols = columns_of(rows)
    parts = load_parts(qkv_ref)
    slots = qkv_ref.shape[0] * LOW
    count = rows.shape[1]
    results = []
    for h in range(4):
        got = compact(cols, parts, h, slots)
        query, key, value = (got[:, 128 * k : 128 * k + 128] for k in range(3))
        keys = key.astype(f32)
        unit = keys / jnp.sqrt(jnp.mean(keys * keys, axis=1, keepdims=True) + epsilon)
        mixed = 0.5 * centroids_ref[h : h + 1, :] + 0.5 * jnp.sum(
            unit, axis=0, keepdims=True
        ) * (1.0 / count)
        centers_ref[h : h + 1, :] = mixed / jnp.sqrt(
            jnp.mean(mixed * mixed, axis=1, keepdims=True) + epsilon
        )
        weights = weights_of(rows, cols, query, key, h, scaling).astype(bf16)
        attended = dot_nn(value.T, weights).astype(bf16)
        results.append(spread(rows, h, [attended], []))
    store_parts(out_ref, gathered_parts(results))


def backward_kernel(scaling, rows_ref, qkv_ref, grad_ref, out_ref):
    rows = rows_ref[...]
    cols = columns_of(rows)
    parts = load_parts(qkv_ref)
    grad_parts = load_parts(grad_ref)
    slots = qkv_ref.shape[0] * LOW
    results = []
    for h in range(4):
        got = compact(cols, parts, h, slots)
        query, key, value = (got[:, 128 * k : 128 * k + 128] for k in range(3))
        grad = compact(cols, grad_parts, h, slots)
        weights = weights_of(rows, cols, query, key, h, scaling)
        weights_b = weights.astype(bf16)
        attended = dot_nn(value.T, weights_b)
        grad_t = grad.astype(f32).T
        delta = jnp.sum(grad_t * attended, axis=0, keepdims=True)
        probs = dot_nt(value, grad)
        dscore = (weights * (probs - delta) * scaling).astype(bf16)
        query_g = dot_nn(key.T, dscore).astype(bf16)
        key_g = dot_nn(dscore, query).astype(bf16)
        value_g = dot_nn(weights_b, grad).astype(bf16)
        results.append(spread(rows, h, [query_g], [jnp.concatenate([key_g, value_g], axis=1)]))
    store_parts(out_ref, gathered_parts(results))


def call(kernel, outs, flops, *args):
    size = sum(a.size * a.dtype.itemsize for a in args)
    size += sum(o.size * o.dtype.itemsize for o in outs)
    whole = pl.BlockSpec(memory_space=pltpu.VMEM)
    got = pl.pallas_call(
        kernel,
        out_shape=outs,
        in_specs=[whole] * len(args),
        out_specs=[whole] * len(outs),
        compiler_params=pltpu.CompilerParams(vmem_limit_bytes=VMEM),
        cost_estimate=pl.CostEstimate(flops=flops, bytes_accessed=size, transcendentals=0),
    )(*args)
    return got[0] if len(outs) == 1 else got


def shape_of(dims, dtype):
    return jax.ShapeDtypeStruct(dims, dtype)


def shifted(x, axis, step, unit=1):
    n = lax.axis_size(axis)
    return lax.ppermute(x, axis, [(i, (i + step * unit) % n) for i in range(n)])


def swapped(x):
    n = lax.axis_size("ctx")
    return lax.ppermute(x, "ctx", [(i, i ^ 1) for i in range(n)])


def neighbour_tokens(out_grad):
    n = lax.axis_size("mp")
    return shifted(out_grad, "mp", 1), shifted(out_grad, "mp", n - 1)


def all_tokens(out_grad, before, after):
    n = lax.axis_size("mp")
    me = lax.axis_index("mp")
    rows, width = out_grad.shape
    half = rows // 2
    upper = shifted(before[:half], "mp", 1)
    lower = shifted(after[half:], "mp", n - 1)
    full = jnp.zeros((rows, n * width), out_grad.dtype)
    full = lax.dynamic_update_slice(full, out_grad, (0, me * width))
    full = lax.dynamic_update_slice(full, before, (0, (me + n - 1) % n * width))
    full = lax.dynamic_update_slice(full, after, (0, (me + 1) % n * width))
    opposite = (me + 2) % n * width
    full = lax.dynamic_update_slice(full, upper, (0, opposite))
    return lax.dynamic_update_slice(full, lower, (half, opposite))


def clu_weight_parts(weight):
    n = lax.axis_size("clu")
    pair = lax.axis_index("clu") // 2
    rows, width = weight.shape
    mine = jnp.zeros((n // 2, 1, rows, width), weight.dtype)
    for k in range(n // 2):
        part = shifted(weight, "clu", k, 2) if k else weight
        mine = lax.dynamic_update_slice(
            mine, part[None, None], ((pair + n // 2 - k) % (n // 2), 0, 0, 0)
        )
    return mine, lax.ppermute(mine, "clu", [(i, i ^ 1) for i in range(n)])


def clu_weight(parts):
    mine, other = parts
    bit = lax.axis_index("clu") % 2
    pairs, _, rows, width = mine.shape
    full = jnp.zeros((pairs, 2, rows, width), mine.dtype)
    full = lax.dynamic_update_slice(full, mine, (0, bit, 0, 0))
    full = lax.dynamic_update_slice(full, other, (0, 1 - bit, 0, 0))
    return full.reshape(2 * pairs * rows, width)


def ctx_weight(part):
    rows, width = part.shape
    chips = lax.axis_size("ctx") // 2
    index = lax.axis_index("ctx")
    chip, core = index // 2, index % 2
    mine = jnp.zeros((chips, 1, rows, width), part.dtype)
    for k in range(chips):
        piece = shifted(part, "ctx", k, 2) if k else part
        mine = lax.dynamic_update_slice(
            mine, piece[None, None], ((chip + chips - k) % chips, 0, 0, 0)
        )
    other = swapped(mine)
    full = jnp.zeros((chips, 2, rows, width), part.dtype)
    full = lax.dynamic_update_slice(full, mine, (0, core, 0, 0))
    full = lax.dynamic_update_slice(full, other, (0, 1 - core, 0, 0))
    return full.reshape(chips * 2 * rows, width)


def scatter_sum(partial):
    ctx, clu = lax.axis_size("ctx"), lax.axis_size("clu")
    chips = ctx // 2
    index = lax.axis_index("ctx")
    chip, core = index // 2, index % 2
    place = lax.axis_index("clu")
    rows = partial.shape[0] // ctx // clu
    width = partial.shape[1]
    shares = partial.reshape(chips, 2, clu * rows, width)

    def pick(x, i, dim):
        return lax.dynamic_index_in_dim(x, i, dim, keepdims=False)

    other = swapped(pick(shares, 1 - core, 1).astype(bf16))
    shares = pick(shares, core, 1) + other.astype(f32)
    total = pick(shares, chip, 0)
    for k in range(1, chips):
        piece = pick(shares, (chip + k) % chips, 0).astype(bf16)
        total = total + shifted(piece, "ctx", k, 2).astype(f32)
    pairs = clu // 2
    shares = total.reshape(pairs, 2, rows, width)
    total = pick(shares, place // 2, 0)
    for k in range(1, pairs):
        piece = pick(shares, (place // 2 + k) % pairs, 0).astype(bf16)
        total = total + shifted(piece, "clu", k, 2).astype(f32)
    return total


def scatter_last(shares):
    clu = lax.axis_size("clu")
    bit = lax.axis_index("clu") % 2
    piece = lax.dynamic_index_in_dim(shares, 1 - bit, 0, keepdims=False).astype(bf16)
    other = lax.ppermute(piece, "clu", [(i, i ^ 1) for i in range(clu)])
    return lax.dynamic_index_in_dim(shares, bit, 0, keepdims=False) + other.astype(f32)


def exchange(x):
    return lax.all_to_all(x, GROUP, split_axis=0, concat_axis=0, tiled=True)


def per_device(queries, tok_keys, tok_values, out_grad, out_weight, membership, centroids):
    tok_rows, width = queries.shape
    heads = membership.shape[0]
    count = membership.shape[2]
    head_size = width // heads
    owners = lax.axis_size(GROUP)
    pair_rows = heads * CAP
    slots = owners * LOW
    scaling = head_size ** (-0.5)

    table, rows = call(
        functools.partial(prep_kernel, tok_rows),
        [shape_of((owners, 128), jnp.int32), shape_of((16, count), f32)],
        10**8,
        membership,
    )
    before, after = neighbour_tokens(out_grad)
    weight_parts = clu_weight_parts(out_weight.T)
    table = exchange(table)
    index_low = table[:, : heads * LOW].reshape(owners, heads, LOW)
    index_high = table[:, heads * LOW : pair_rows].reshape(owners, heads // 2, LOW)
    index_rows = jnp.concatenate([index_low, index_high, index_high], axis=1)
    index_rows = index_rows.transpose(1, 0, 2).reshape(2 * heads, slots)
    index_rows, before, after, weight_parts = lax.optimization_barrier(
        (index_rows, before, after, weight_parts)
    )

    def packed_shape(n):
        return shape_of((owners, pair_rows, n * head_size), bf16)

    def pack(*sources):
        n = len(sources)
        return call(pack_kernel, [packed_shape(n)], n * 10**9, index_rows, *sources)

    def unpack(packed, n):
        outs = [shape_of((tok_rows, width), bf16)] * n
        return call(unpack_kernel, outs, n * 10**9, index_rows, packed)

    got_qkv = exchange(pack(queries, tok_keys, tok_values))
    grad_full = all_tokens(out_grad, before, after)
    weight_full = ctx_weight(clu_weight(weight_parts))
    head_grad = dot_nn(grad_full, weight_full).astype(bf16)
    got_grad = exchange(pack(head_grad))

    attended, centers = call(
        functools.partial(forward_kernel, scaling),
        [packed_shape(1), shape_of((heads, head_size), f32)],
        4 * 10**9,
        rows,
        centroids[:, 0, :],
        got_qkv,
    )
    back_out = exchange(attended)
    grads = call(
        functools.partial(backward_kernel, scaling),
        [packed_shape(3)],
        8 * 10**9,
        rows,
        got_qkv,
        got_grad,
    )
    back_grads = exchange(grads)
    attn_out = unpack(back_out, 1)
    partial = lax.dot_general(
        grad_full, attn_out, (((0,), (0,)), ((), ())), preferred_element_type=f32
    )
    back_grads, shares = lax.optimization_barrier((back_grads, scatter_sum(partial)))
    share = scatter_last(shares)
    query_g, key_g, value_g = unpack(back_grads, 3)
    return (query_g, key_g, value_g, share.T, centers[:, None, :])


def solution(mesh):
    token = P(GROUP, "mp")
    owner = P("mp", GROUP, None)
    return jax.shard_map(
        per_device,
        mesh=mesh,
        in_specs=(token, token, token, token, P("mp", GROUP), owner, owner),
        out_specs=(token, token, token, P("mp", GROUP), owner),
        check_vma=False,
    )
```

```python
import functools

import jax
import jax.numpy as jnp
from jax import lax
from jax.experimental import pallas as pl
from jax.experimental.pallas import tpu as pltpu
from jax.sharding import PartitionSpec as P

epsilon = 1e-06
GROUP = ("ctx", "clu")
CAP = 12
LOW = 8
VMEM = 56 * 1024 * 1024
LESS = 24 * 1024 * 1024
f32 = jnp.float32
bf16 = jnp.bfloat16


def dot_nn(a, b):
    return lax.dot_general(a, b, (((1,), (0,)), ((), ())), preferred_element_type=f32)


def dot_nt(a, b):
    return lax.dot_general(a, b, (((1,), (1,)), ((), ())), preferred_element_type=f32)


def iota(shape, dim):
    return lax.broadcasted_iota(jnp.int32, shape, dim).astype(f32)


def columns_of(rows):
    copies = 128 // rows.shape[0]
    return jnp.concatenate([rows] * copies, axis=0).T


def onehot(mask):
    return jnp.where(mask, 1.0, 0.0).astype(bf16)


def prep_body(members, blocks, tok_rows):
    heads, count = members.shape
    pieces, rows = [], []
    lane = iota((1, count), 1)
    block_col = iota((blocks, count), 0)
    for h in range(heads):
        member = members[h : h + 1, :]
        block = jnp.floor(member * (1.0 / tok_rows))
        local = member - block * tok_rows
        here = block == block_col
        start_of = jnp.sum(jnp.where(block < block_col, 1.0, 0.0), axis=1, keepdims=True)
        start = jnp.sum(jnp.where(here, start_of, 0.0), axis=0, keepdims=True)
        rank = lane - start
        low = block * LOW + rank
        high = block * LOW + (h % 2) * (CAP - LOW) + (rank - LOW)
        rows += [member, jnp.where(rank < LOW, low, -1.0), jnp.where(rank >= LOW, high, -1.0)]
        at_rank = rank == iota((16, count), 0)
        large = jnp.floor(local * (1.0 / 32))
        small = local - large * 32
        right = jnp.concatenate(
            [
                jnp.where(at_rank, large, 0.0),
                jnp.where(at_rank, small, 0.0),
                jnp.where(at_rank, 1.0, 0.0),
                jnp.zeros((80, count), f32),
            ],
            axis=0,
        ).astype(bf16)
        got = dot_nt(onehot(here), right)
        value = got[:, 0:16] * 32 + got[:, 16:32]
        filled = got[:, 32:48] > 0.5
        pieces.append((value, filled))
    low_cols = [jnp.where(f, v, -1.0)[:, :LOW] for v, f in pieces]
    high_cols = [
        jnp.where(f, v + (h % 2) * tok_rows, -1.0)[:, LOW:CAP]
        for h, (v, f) in enumerate(pieces)
    ]
    used = heads * CAP
    table = jnp.concatenate(
        low_cols + high_cols + [jnp.full((blocks, 128 - used), -1.0, f32)], axis=1
    )
    return table, jnp.concatenate(rows + [jnp.zeros((4, count), f32)], axis=0)


def pack_body(index_rows, sources):
    cols = columns_of(index_rows)
    tokens = sources[0].shape[0]
    slots = index_rows.shape[1]
    n = sources[0].shape[1]
    token = iota((slots, tokens), 1)

    def part(value):
        return value.reshape(slots // LOW, LOW, n)

    low = [
        part(dot_nn(onehot(cols[:, h : h + 1] == token), sources[h]))
        for h in range(4)
    ]
    high = []
    for p in range(2):
        col = cols[:, 4 + p : 5 + p]
        high.append(
            part(
                dot_nn(onehot(col == token), sources[2 * p])
                + dot_nn(onehot(col == token + tokens), sources[2 * p + 1])
            )
        )
    return [
        jnp.concatenate(two, axis=1).astype(bf16)
        for two in (low[:2], low[2:], high)
    ]


def head_slots(parts, h):
    p, q = divmod(h, 2)

    def take(part, q):
        part = part.astype(f32)[:, 8 * q : 8 * q + 8, :]
        return part.reshape(part.shape[0] * 8, part.shape[2]).astype(bf16)

    return take(parts[p], q), take(parts[2], p)


def unpack_body(index_rows, parts, h, tokens):
    low, high = head_slots(parts, h)
    token = iota((tokens, index_rows.shape[1]), 0)
    row_low = index_rows[h : h + 1, :]
    row_high = index_rows[4 + h // 2 : 5 + h // 2, :]
    return dot_nn(onehot(token == row_low), low) + dot_nn(
        onehot(token + (h % 2) * tokens == row_high), high
    )


def compact(cols, parts, h, slots):
    low, high = head_slots(parts, h)
    count = cols.shape[0]
    slot = iota((count, slots), 1)
    return (
        dot_nn(onehot(cols[:, 3 * h + 1 : 3 * h + 2] == slot), low)
        + dot_nn(onehot(cols[:, 3 * h + 2 : 3 * h + 3] == slot), high)
    ).astype(bf16)


def weights_of(rows, cols, query, key, h, scaling):
    scores = dot_nt(key, query) * scaling
    allowed = cols[:, 3 * h : 3 * h + 1] <= rows[3 * h : 3 * h + 1, :]
    scores = jnp.where(allowed, scores, -jnp.inf)
    highest = jnp.max(scores, axis=0, keepdims=True)
    weights = jnp.exp(scores - highest)
    return weights * (1.0 / jnp.sum(weights, axis=0, keepdims=True))


def spread(rows, h, transposed, plain):
    slots = rows.shape[1]
    slot = iota((slots, rows.shape[1]), 0)
    out = []
    for k in (1, 2):
        pick = onehot(slot == rows[3 * h + k : 3 * h + k + 1, :])
        got = [dot_nt(pick, t) for t in transposed] + [dot_nn(pick, v) for v in plain]
        out.append(jnp.concatenate(got, axis=1) if len(got) > 1 else got[0])
    return out


def gathered_parts(results):
    def part(value):
        return value.reshape(value.shape[0] // LOW, LOW, value.shape[1])

    low = [part(r[0]) for r in results]
    high = [part(results[2 * p][1] + results[2 * p + 1][1]) for p in range(2)]
    return [
        jnp.concatenate(two, axis=1).astype(bf16)
        for two in (low[:2], low[2:], high)
    ]


def prep_kernel(tok_rows, members_ref, table_ref, rows_ref):
    table, rows = prep_body(members_ref[:, 0, :].astype(f32), table_ref.shape[0], tok_rows)
    table_ref[...] = table.astype(jnp.int32)
    rows_ref[...] = rows


def load_parts(ref):
    return [ref[:, 16 * k : 16 * k + 16, :] for k in range(3)]


def store_parts(ref, parts):
    for k in range(3):
        ref[:, 16 * k : 16 * k + 16, :] = parts[k]


def pack_kernel(index_ref, source_ref, out_ref):
    sources = []
    for h in range(4):
        starts = range(128 * h, source_ref.shape[1], 512)
        got = [source_ref[:, i : i + 128] for i in starts]
        sources.append(jnp.concatenate(got, axis=1) if len(got) > 1 else got[0])
    store_parts(out_ref, pack_body(index_ref[...].astype(f32), sources))


def unpack_kernel(index_ref, packed_ref, *out_refs):
    parts = load_parts(packed_ref)
    index_rows = index_ref[...].astype(f32)
    for h in range(4):
        got = unpack_body(index_rows, parts, h, out_refs[0].shape[0]).astype(bf16)
        for k, ref in enumerate(out_refs):
            ref[:, 128 * h : 128 * h + 128] = got[:, 128 * k : 128 * k + 128]


def forward_kernel(scaling, rows_ref, centroids_ref, qkv_ref, out_ref, centers_ref):
    rows = rows_ref[...]
    cols = columns_of(rows)
    parts = load_parts(qkv_ref)
    slots = qkv_ref.shape[0] * LOW
    count = rows.shape[1]
    results = []
    for h in range(4):
        got = compact(cols, parts, h, slots)
        query, key, value = (got[:, 128 * k : 128 * k + 128] for k in range(3))
        keys = key.astype(f32)
        unit = keys / jnp.sqrt(jnp.mean(keys * keys, axis=1, keepdims=True) + epsilon)
        mixed = 0.5 * centroids_ref[h : h + 1, :] + 0.5 * jnp.sum(
            unit, axis=0, keepdims=True
        ) * (1.0 / count)
        centers_ref[h : h + 1, :] = mixed / jnp.sqrt(
            jnp.mean(mixed * mixed, axis=1, keepdims=True) + epsilon
        )
        weights = weights_of(rows, cols, query, key, h, scaling).astype(bf16)
        attended = dot_nn(value.T, weights).astype(bf16)
        results.append(spread(rows, h, [attended], []))
    store_parts(out_ref, gathered_parts(results))


def backward_kernel(scaling, rows_ref, qkv_ref, grad_ref, out_ref):
    rows = rows_ref[...]
    cols = columns_of(rows)
    parts = load_parts(qkv_ref)
    grad_parts = load_parts(grad_ref)
    slots = qkv_ref.shape[0] * LOW
    results = []
    for h in range(4):
        got = compact(cols, parts, h, slots)
        query, key, value = (got[:, 128 * k : 128 * k + 128] for k in range(3))
        grad = compact(cols, grad_parts, h, slots)
        weights = weights_of(rows, cols, query, key, h, scaling)
        weights_b = weights.astype(bf16)
        attended = dot_nn(value.T, weights_b)
        grad_t = grad.astype(f32).T
        delta = jnp.sum(grad_t * attended, axis=0, keepdims=True)
        probs = dot_nt(value, grad)
        dscore = (weights * (probs - delta) * scaling).astype(bf16)
        query_g = dot_nn(key.T, dscore).astype(bf16)
        key_g = dot_nn(dscore, query).astype(bf16)
        value_g = dot_nn(weights_b, grad).astype(bf16)
        results.append(spread(rows, h, [query_g], [jnp.concatenate([key_g, value_g], axis=1)]))
    store_parts(out_ref, gathered_parts(results))


def call(kernel, outs, flops, *args, vmem=VMEM):
    size = sum(a.size * a.dtype.itemsize for a in args)
    size += sum(o.size * o.dtype.itemsize for o in outs)
    whole = pl.BlockSpec(memory_space=pltpu.VMEM)
    got = pl.pallas_call(
        kernel,
        out_shape=outs,
        in_specs=[whole] * len(args),
        out_specs=[whole] * len(outs),
        compiler_params=pltpu.CompilerParams(vmem_limit_bytes=vmem),
        cost_estimate=pl.CostEstimate(flops=flops, bytes_accessed=size, transcendentals=0),
    )(*args)
    return got[0] if len(outs) == 1 else got


def shape_of(dims, dtype):
    return jax.ShapeDtypeStruct(dims, dtype)


def shifted(x, axis, step, unit=1):
    n = lax.axis_size(axis)
    return lax.ppermute(x, axis, [(i, (i + step * unit) % n) for i in range(n)])


def swapped(x):
    n = lax.axis_size("ctx")
    return lax.ppermute(x, "ctx", [(i, i ^ 1) for i in range(n)])


def neighbour_tokens(out_grad):
    n = lax.axis_size("mp")
    return shifted(out_grad, "mp", 1), shifted(out_grad, "mp", n - 1)


def all_tokens(out_grad, before, after):
    n = lax.axis_size("mp")
    me = lax.axis_index("mp")
    rows, width = out_grad.shape
    half = rows // 2
    upper = shifted(before[:half], "mp", 1)
    lower = shifted(after[half:], "mp", n - 1)
    full = jnp.zeros((rows, n * width), out_grad.dtype)
    full = lax.dynamic_update_slice(full, out_grad, (0, me * width))
    full = lax.dynamic_update_slice(full, before, (0, (me + n - 1) % n * width))
    full = lax.dynamic_update_slice(full, after, (0, (me + 1) % n * width))
    opposite = (me + 2) % n * width
    full = lax.dynamic_update_slice(full, upper, (0, opposite))
    return lax.dynamic_update_slice(full, lower, (half, opposite))


def clu_weight_parts(weight):
    n = lax.axis_size("clu")
    pair = lax.axis_index("clu") // 2
    rows, width = weight.shape
    mine = jnp.zeros((n // 2, 1, rows, width), weight.dtype)
    for k in range(n // 2):
        part = shifted(weight, "clu", k, 2) if k else weight
        mine = lax.dynamic_update_slice(
            mine, part[None, None], ((pair + n // 2 - k) % (n // 2), 0, 0, 0)
        )
    return mine, lax.ppermute(mine, "clu", [(i, i ^ 1) for i in range(n)])


def clu_weight(parts):
    mine, other = parts
    bit = lax.axis_index("clu") % 2
    pairs, _, rows, width = mine.shape
    full = jnp.zeros((pairs, 2, rows, width), mine.dtype)
    full = lax.dynamic_update_slice(full, mine, (0, bit, 0, 0))
    full = lax.dynamic_update_slice(full, other, (0, 1 - bit, 0, 0))
    return full.reshape(2 * pairs * rows, width)


def ctx_weight(part):
    rows, width = part.shape
    chips = lax.axis_size("ctx") // 2
    index = lax.axis_index("ctx")
    chip, core = index // 2, index % 2
    mine = jnp.zeros((chips, 1, rows, width), part.dtype)
    for k in range(chips):
        piece = shifted(part, "ctx", k, 2) if k else part
        mine = lax.dynamic_update_slice(
            mine, piece[None, None], ((chip + chips - k) % chips, 0, 0, 0)
        )
    other = swapped(mine)
    full = jnp.zeros((chips, 2, rows, width), part.dtype)
    full = lax.dynamic_update_slice(full, mine, (0, core, 0, 0))
    full = lax.dynamic_update_slice(full, other, (0, 1 - core, 0, 0))
    return full.reshape(chips * 2 * rows, width)


def scatter_sum(partial):
    ctx, clu = lax.axis_size("ctx"), lax.axis_size("clu")
    chips = ctx // 2
    index = lax.axis_index("ctx")
    chip, core = index // 2, index % 2
    place = lax.axis_index("clu")
    rows = partial.shape[0] // ctx // clu
    width = partial.shape[1]
    shares = partial.reshape(chips, 2, clu * rows, width)

    def pick(x, i, dim):
        return lax.dynamic_index_in_dim(x, i, dim, keepdims=False)

    other = swapped(pick(shares, 1 - core, 1).astype(bf16))
    shares = pick(shares, core, 1) + other.astype(f32)
    total = pick(shares, chip, 0)
    for k in range(1, chips):
        piece = pick(shares, (chip + k) % chips, 0).astype(bf16)
        total = total + shifted(piece, "ctx", k, 2).astype(f32)
    pairs = clu // 2
    shares = total.reshape(pairs, 2, rows, width)
    total = pick(shares, place // 2, 0)
    for k in range(1, pairs):
        piece = pick(shares, (place // 2 + k) % pairs, 0).astype(bf16)
        total = total + shifted(piece, "clu", k, 2).astype(f32)
    return total


def scatter_last(shares):
    clu = lax.axis_size("clu")
    bit = lax.axis_index("clu") % 2
    piece = lax.dynamic_index_in_dim(shares, 1 - bit, 0, keepdims=False).astype(bf16)
    other = lax.ppermute(piece, "clu", [(i, i ^ 1) for i in range(clu)])
    return lax.dynamic_index_in_dim(shares, bit, 0, keepdims=False) + other.astype(f32)


def exchange(x):
    return lax.all_to_all(x, GROUP, split_axis=0, concat_axis=0, tiled=True)


def per_device(queries, tok_keys, tok_values, out_grad, out_weight, membership, centroids):
    tok_rows, width = queries.shape
    heads = membership.shape[0]
    count = membership.shape[2]
    head_size = width // heads
    owners = lax.axis_size(GROUP)
    pair_rows = heads * CAP
    slots = owners * LOW
    scaling = head_size ** (-0.5)

    table, rows = call(
        functools.partial(prep_kernel, tok_rows),
        [shape_of((owners, 128), jnp.int32), shape_of((16, count), f32)],
        10**8,
        membership,
    )
    before, after = neighbour_tokens(out_grad)
    weight_parts = clu_weight_parts(out_weight.T)
    table = exchange(table)
    index_low = table[:, : heads * LOW].reshape(owners, heads, LOW)
    index_high = table[:, heads * LOW : pair_rows].reshape(owners, heads // 2, LOW)
    index_rows = jnp.concatenate([index_low, index_high, index_high], axis=1)
    index_rows = index_rows.transpose(1, 0, 2).reshape(2 * heads, slots)
    index_rows, before, after, weight_parts = lax.optimization_barrier(
        (index_rows, before, after, weight_parts)
    )

    def packed_shape(n):
        return shape_of((owners, pair_rows, n * head_size), bf16)

    def pack(source):
        n = source.shape[1] // width
        return call(pack_kernel, [packed_shape(n)], n * 10**9, index_rows, source, vmem=LESS)

    def unpack(packed, n):
        outs = [shape_of((tok_rows, width), bf16)] * n
        vmem = LESS if n == 1 else VMEM
        return call(unpack_kernel, outs, n * 10**9, index_rows, packed, vmem=vmem)

    got_qkv = exchange(pack(jnp.concatenate([queries, tok_keys, tok_values], axis=1)))
    grad_full = all_tokens(out_grad, before, after)
    weight_full = ctx_weight(clu_weight(weight_parts))
    head_grad = dot_nn(grad_full, weight_full).astype(bf16)
    got_grad = exchange(pack(head_grad))

    attended, centers = call(
        functools.partial(forward_kernel, scaling),
        [packed_shape(1), shape_of((heads, head_size), f32)],
        4 * 10**9,
        rows,
        centroids[:, 0, :],
        got_qkv,
    )
    back_out = exchange(attended)
    grads = call(
        functools.partial(backward_kernel, scaling),
        [packed_shape(3)],
        8 * 10**9,
        rows,
        got_qkv,
        got_grad,
    )
    back_grads = exchange(grads)
    attn_out = unpack(back_out, 1)
    partial = lax.dot_general(
        grad_full, attn_out, (((0,), (0,)), ((), ())), preferred_element_type=f32
    )
    back_grads, shares = lax.optimization_barrier((back_grads, scatter_sum(partial)))
    share = scatter_last(shares)
    query_g, key_g, value_g = unpack(back_grads, 3)
    return (query_g, key_g, value_g, share.T, centers[:, None, :])


def solution(mesh):
    token = P(GROUP, "mp")
    owner = P("mp", GROUP, None)
    return jax.shard_map(
        per_device,
        mesh=mesh,
        in_specs=(token, token, token, token, P("mp", GROUP), owner, owner),
        out_specs=(token, token, token, P("mp", GROUP), owner),
        check_vma=False,
    )
```

```python
import functools

import jax
import jax.numpy as jnp
from jax import lax
from jax.experimental import pallas as pl
from jax.experimental.pallas import tpu as pltpu
from jax.sharding import PartitionSpec as P

epsilon = 1e-06
GROUP = ("ctx", "clu")
CAP = 12
LOW = 8
VMEM = 56 * 1024 * 1024
LESS = 24 * 1024 * 1024
f32 = jnp.float32
bf16 = jnp.bfloat16


def dot_nn(a, b):
    return lax.dot_general(a, b, (((1,), (0,)), ((), ())), preferred_element_type=f32)


def dot_nt(a, b):
    return lax.dot_general(a, b, (((1,), (1,)), ((), ())), preferred_element_type=f32)


def iota(shape, dim):
    return lax.broadcasted_iota(jnp.int32, shape, dim).astype(f32)


def columns_of(rows):
    copies = 128 // rows.shape[0]
    return jnp.concatenate([rows] * copies, axis=0).T


def onehot(mask):
    return jnp.where(mask, 1.0, 0.0).astype(bf16)


def prep_body(members, blocks, tok_rows):
    heads, count = members.shape
    pieces, rows = [], []
    lane = iota((1, count), 1)
    block_col = iota((blocks, count), 0)
    for h in range(heads):
        member = members[h : h + 1, :]
        block = jnp.floor(member * (1.0 / tok_rows))
        local = member - block * tok_rows
        here = block == block_col
        start_of = jnp.sum(jnp.where(block < block_col, 1.0, 0.0), axis=1, keepdims=True)
        start = jnp.sum(jnp.where(here, start_of, 0.0), axis=0, keepdims=True)
        rank = lane - start
        low = block * LOW + rank
        high = block * LOW + (h % 2) * (CAP - LOW) + (rank - LOW)
        rows += [member, jnp.where(rank < LOW, low, -1.0), jnp.where(rank >= LOW, high, -1.0)]
        at_rank = rank == iota((16, count), 0)
        large = jnp.floor(local * (1.0 / 32))
        small = local - large * 32
        right = jnp.concatenate(
            [
                jnp.where(at_rank, large, 0.0),
                jnp.where(at_rank, small, 0.0),
                jnp.where(at_rank, 1.0, 0.0),
                jnp.zeros((80, count), f32),
            ],
            axis=0,
        ).astype(bf16)
        got = dot_nt(onehot(here), right)
        value = got[:, 0:16] * 32 + got[:, 16:32]
        filled = got[:, 32:48] > 0.5
        pieces.append((value, filled))
    low_cols = [jnp.where(f, v, -1.0)[:, :LOW] for v, f in pieces]
    high_cols = [
        jnp.where(f, v + (h % 2) * tok_rows, -1.0)[:, LOW:CAP]
        for h, (v, f) in enumerate(pieces)
    ]
    used = heads * CAP
    table = jnp.concatenate(
        low_cols + high_cols + [jnp.full((blocks, 128 - used), -1.0, f32)], axis=1
    )
    return table, jnp.concatenate(rows + [jnp.zeros((4, count), f32)], axis=0)


def pack_body(index_rows, sources):
    cols = columns_of(index_rows)
    tokens = sources[0].shape[0]
    slots = index_rows.shape[1]
    n = sources[0].shape[1]
    token = iota((slots, tokens), 1)

    def part(value):
        return value.reshape(slots // LOW, LOW, n)

    low = [
        part(dot_nn(onehot(cols[:, h : h + 1] == token), sources[h]))
        for h in range(4)
    ]
    high = []
    for p in range(2):
        col = cols[:, 4 + p : 5 + p]
        high.append(
            part(
                dot_nn(onehot(col == token), sources[2 * p])
                + dot_nn(onehot(col == token + tokens), sources[2 * p + 1])
            )
        )
    return [
        jnp.concatenate(two, axis=1).astype(bf16)
        for two in (low[:2], low[2:], high)
    ]


def head_slots(parts, h):
    p, q = divmod(h, 2)

    def take(part, q):
        part = part.astype(f32)[:, 8 * q : 8 * q + 8, :]
        return part.reshape(part.shape[0] * 8, part.shape[2]).astype(bf16)

    return take(parts[p], q), take(parts[2], p)


def unpack_body(index_rows, parts, h, tokens):
    low, high = head_slots(parts, h)
    token = iota((tokens, index_rows.shape[1]), 0)
    row_low = index_rows[h : h + 1, :]
    row_high = index_rows[4 + h // 2 : 5 + h // 2, :]
    return dot_nn(onehot(token == row_low), low) + dot_nn(
        onehot(token + (h % 2) * tokens == row_high), high
    )


def compact(cols, parts, h, slots):
    low, high = head_slots(parts, h)
    count = cols.shape[0]
    slot = iota((count, slots), 1)
    return (
        dot_nn(onehot(cols[:, 3 * h + 1 : 3 * h + 2] == slot), low)
        + dot_nn(onehot(cols[:, 3 * h + 2 : 3 * h + 3] == slot), high)
    ).astype(bf16)


def weights_of(rows, cols, query, key, h, scaling):
    scores = dot_nt(key, query) * scaling
    allowed = cols[:, 3 * h : 3 * h + 1] <= rows[3 * h : 3 * h + 1, :]
    scores = jnp.where(allowed, scores, -jnp.inf)
    highest = jnp.max(scores, axis=0, keepdims=True)
    weights = jnp.exp(scores - highest)
    return weights * (1.0 / jnp.sum(weights, axis=0, keepdims=True))


def spread(rows, h, transposed, plain):
    slots = rows.shape[1]
    slot = iota((slots, rows.shape[1]), 0)
    out = []
    for k in (1, 2):
        pick = onehot(slot == rows[3 * h + k : 3 * h + k + 1, :])
        got = [dot_nt(pick, t) for t in transposed] + [dot_nn(pick, v) for v in plain]
        out.append(jnp.concatenate(got, axis=1) if len(got) > 1 else got[0])
    return out


def gathered_parts(results):
    def part(value):
        return value.reshape(value.shape[0] // LOW, LOW, value.shape[1])

    low = [part(r[0]) for r in results]
    high = [part(results[2 * p][1] + results[2 * p + 1][1]) for p in range(2)]
    return [
        jnp.concatenate(two, axis=1).astype(bf16)
        for two in (low[:2], low[2:], high)
    ]


def prep_kernel(tok_rows, members_ref, table_ref, rows_ref):
    table, rows = prep_body(members_ref[:, 0, :].astype(f32), table_ref.shape[0], tok_rows)
    table_ref[...] = table.astype(jnp.int32)
    rows_ref[...] = rows


def load_parts(ref):
    return [ref[:, 16 * k : 16 * k + 16, :] for k in range(3)]


def store_parts(ref, parts):
    for k in range(3):
        ref[:, 16 * k : 16 * k + 16, :] = parts[k]


def pack_kernel(index_ref, source_ref, out_ref):
    sources = []
    for h in range(4):
        starts = range(128 * h, source_ref.shape[1], 512)
        got = [source_ref[:, i : i + 128] for i in starts]
        sources.append(jnp.concatenate(got, axis=1) if len(got) > 1 else got[0])
    store_parts(out_ref, pack_body(index_ref[...].astype(f32), sources))


def unpack_kernel(index_ref, packed_ref, *out_refs):
    parts = load_parts(packed_ref)
    index_rows = index_ref[...].astype(f32)
    for h in range(4):
        got = unpack_body(index_rows, parts, h, out_refs[0].shape[0]).astype(bf16)
        for k, ref in enumerate(out_refs):
            ref[:, 128 * h : 128 * h + 128] = got[:, 128 * k : 128 * k + 128]


def forward_kernel(scaling, rows_ref, centroids_ref, qkv_ref, out_ref, centers_ref):
    rows = rows_ref[...]
    cols = columns_of(rows)
    parts = load_parts(qkv_ref)
    slots = qkv_ref.shape[0] * LOW
    count = rows.shape[1]
    results = []
    for h in range(4):
        got = compact(cols, parts, h, slots)
        query, key, value = (got[:, 128 * k : 128 * k + 128] for k in range(3))
        keys = key.astype(f32)
        unit = keys / jnp.sqrt(jnp.mean(keys * keys, axis=1, keepdims=True) + epsilon)
        mixed = 0.5 * centroids_ref[h : h + 1, :] + 0.5 * jnp.sum(
            unit, axis=0, keepdims=True
        ) * (1.0 / count)
        centers_ref[h : h + 1, :] = mixed / jnp.sqrt(
            jnp.mean(mixed * mixed, axis=1, keepdims=True) + epsilon
        )
        weights = weights_of(rows, cols, query, key, h, scaling).astype(bf16)
        attended = dot_nn(value.T, weights).astype(bf16)
        results.append(spread(rows, h, [attended], []))
    store_parts(out_ref, gathered_parts(results))


def backward_kernel(scaling, rows_ref, qkv_ref, grad_ref, out_ref):
    rows = rows_ref[...]
    cols = columns_of(rows)
    parts = load_parts(qkv_ref)
    grad_parts = load_parts(grad_ref)
    slots = qkv_ref.shape[0] * LOW
    results = []
    for h in range(4):
        got = compact(cols, parts, h, slots)
        query, key, value = (got[:, 128 * k : 128 * k + 128] for k in range(3))
        grad = compact(cols, grad_parts, h, slots)
        weights = weights_of(rows, cols, query, key, h, scaling)
        weights_b = weights.astype(bf16)
        attended = dot_nn(value.T, weights_b)
        grad_t = grad.astype(f32).T
        delta = jnp.sum(grad_t * attended, axis=0, keepdims=True)
        probs = dot_nt(value, grad)
        dscore = (weights * (probs - delta) * scaling).astype(bf16)
        query_g = dot_nn(key.T, dscore).astype(bf16)
        key_g = dot_nn(dscore, query).astype(bf16)
        value_g = dot_nn(weights_b, grad).astype(bf16)
        results.append(spread(rows, h, [query_g], [jnp.concatenate([key_g, value_g], axis=1)]))
    store_parts(out_ref, gathered_parts(results))


def call(kernel, outs, flops, *args, vmem=VMEM):
    size = sum(a.size * a.dtype.itemsize for a in args)
    size += sum(o.size * o.dtype.itemsize for o in outs)
    whole = pl.BlockSpec(memory_space=pltpu.VMEM)
    got = pl.pallas_call(
        kernel,
        out_shape=outs,
        in_specs=[whole] * len(args),
        out_specs=[whole] * len(outs),
        compiler_params=pltpu.CompilerParams(vmem_limit_bytes=vmem),
        cost_estimate=pl.CostEstimate(flops=flops, bytes_accessed=size, transcendentals=0),
    )(*args)
    return got[0] if len(outs) == 1 else got


def shape_of(dims, dtype):
    return jax.ShapeDtypeStruct(dims, dtype)


def shifted(x, axis, step, unit=1):
    n = lax.axis_size(axis)
    return lax.ppermute(x, axis, [(i, (i + step * unit) % n) for i in range(n)])


def swapped(x):
    n = lax.axis_size("ctx")
    return lax.ppermute(x, "ctx", [(i, i ^ 1) for i in range(n)])


def other_tokens(out_grad):
    n = lax.axis_size("mp")
    half = out_grad.shape[0] // 2
    before, after = shifted(out_grad, "mp", 1), shifted(out_grad, "mp", n - 1)
    return (
        before,
        after,
        shifted(before[:half], "mp", 1),
        shifted(after[half:], "mp", n - 1),
    )


def all_tokens(out_grad, before, after, upper, lower):
    n = lax.axis_size("mp")
    me = lax.axis_index("mp")
    rows, width = out_grad.shape
    opposite = (me + 2) % n * width
    full = jnp.zeros((rows, n * width), out_grad.dtype)
    full = lax.dynamic_update_slice(full, out_grad, (0, me * width))
    full = lax.dynamic_update_slice(full, before, (0, (me + n - 1) % n * width))
    full = lax.dynamic_update_slice(full, after, (0, (me + 1) % n * width))
    full = lax.dynamic_update_slice(full, upper, (0, opposite))
    return lax.dynamic_update_slice(full, lower, (rows // 2, opposite))


def scatter_sum(partial):
    ctx, clu = lax.axis_size("ctx"), lax.axis_size("clu")
    chips = ctx // 2
    index = lax.axis_index("ctx")
    chip, core = index // 2, index % 2
    place = lax.axis_index("clu")
    rows = partial.shape[0] // ctx // clu
    width = partial.shape[1]
    shares = partial.reshape(chips, 2, clu * rows, width)

    def pick(x, i, dim):
        return lax.dynamic_index_in_dim(x, i, dim, keepdims=False)

    other = swapped(pick(shares, 1 - core, 1).astype(bf16))
    shares = pick(shares, core, 1) + other.astype(f32)
    total = pick(shares, chip, 0)
    for k in range(1, chips):
        piece = pick(shares, (chip + k) % chips, 0).astype(bf16)
        total = total + shifted(piece, "ctx", k, 2).astype(f32)
    shares = total.reshape(clu, rows, width)
    terms = [
        shifted(pick(shares, (place + k) % clu, 0).astype(bf16), "clu", k)
        for k in range(1, clu)
    ]
    return pick(shares, place, 0), terms


def exchange(x):
    return lax.all_to_all(x, GROUP, split_axis=0, concat_axis=0, tiled=True)


def per_device(queries, tok_keys, tok_values, out_grad, out_weight, membership, centroids):
    tok_rows, width = queries.shape
    heads = membership.shape[0]
    count = membership.shape[2]
    head_size = width // heads
    owners = lax.axis_size(GROUP)
    pair_rows = heads * CAP
    slots = owners * LOW
    scaling = head_size ** (-0.5)

    table, rows = call(
        functools.partial(prep_kernel, tok_rows),
        [shape_of((owners, 128), jnp.int32), shape_of((16, count), f32)],
        10**8,
        membership,
    )
    weight_full = lax.all_gather(out_weight.T, GROUP, axis=0, tiled=True)
    others = other_tokens(out_grad)
    table = exchange(table)
    index_low = table[:, : heads * LOW].reshape(owners, heads, LOW)
    index_high = table[:, heads * LOW : pair_rows].reshape(owners, heads // 2, LOW)
    index_rows = jnp.concatenate([index_low, index_high, index_high], axis=1)
    index_rows = index_rows.transpose(1, 0, 2).reshape(2 * heads, slots)
    index_rows, others = lax.optimization_barrier((index_rows, others))

    def packed_shape(n):
        return shape_of((owners, pair_rows, n * head_size), bf16)

    def pack(source):
        n = source.shape[1] // width
        return call(pack_kernel, [packed_shape(n)], n * 10**9, index_rows, source, vmem=LESS)

    def unpack(packed, n):
        outs = [shape_of((tok_rows, width), bf16)] * n
        vmem = LESS if n == 1 else VMEM
        return call(unpack_kernel, outs, n * 10**9, index_rows, packed, vmem=vmem)

    got_qkv = exchange(pack(jnp.concatenate([queries, tok_keys, tok_values], axis=1)))
    grad_full = all_tokens(out_grad, *others)
    head_grad = dot_nn(grad_full, weight_full).astype(bf16)
    got_grad = exchange(pack(head_grad))

    attended, centers = call(
        functools.partial(forward_kernel, scaling),
        [packed_shape(1), shape_of((heads, head_size), f32)],
        4 * 10**9,
        rows,
        centroids[:, 0, :],
        got_qkv,
    )
    back_out = exchange(attended)
    grads = call(
        functools.partial(backward_kernel, scaling),
        [packed_shape(3)],
        8 * 10**9,
        rows,
        got_qkv,
        got_grad,
    )
    back_grads = exchange(grads)
    attn_out = unpack(back_out, 1)
    partial = lax.dot_general(
        grad_full, attn_out, (((0,), (0,)), ((), ())), preferred_element_type=f32
    )
    share, terms = scatter_sum(partial)
    query_g, key_g, value_g = unpack(back_grads, 3)
    query_g, terms = lax.optimization_barrier((query_g, terms))
    for term in terms:
        share = share + term.astype(f32)
    return (query_g, key_g, value_g, share.T, centers[:, None, :])


def solution(mesh):
    token = P(GROUP, "mp")
    owner = P("mp", GROUP, None)
    return jax.shard_map(
        per_device,
        mesh=mesh,
        in_specs=(token, token, token, token, P("mp", GROUP), owner, owner),
        out_specs=(token, token, token, P("mp", GROUP), owner),
        check_vma=False,
    )
```

```python
import functools

import jax
import jax.numpy as jnp
from jax import lax
from jax.experimental import pallas as pl
from jax.experimental.pallas import tpu as pltpu
from jax.sharding import PartitionSpec as P

epsilon = 1e-06
GROUP = ("ctx", "clu")
CAP = 12
LOW = 8
VMEM = 56 * 1024 * 1024
LESS = 24 * 1024 * 1024
f32 = jnp.float32
bf16 = jnp.bfloat16


def dot_nn(a, b):
    return lax.dot_general(a, b, (((1,), (0,)), ((), ())), preferred_element_type=f32)


def dot_nt(a, b):
    return lax.dot_general(a, b, (((1,), (1,)), ((), ())), preferred_element_type=f32)


def iota(shape, dim):
    return lax.broadcasted_iota(jnp.int32, shape, dim).astype(f32)


def columns_of(rows):
    copies = 128 // rows.shape[0]
    return jnp.concatenate([rows] * copies, axis=0).T


def onehot(mask):
    return jnp.where(mask, 1.0, 0.0).astype(bf16)


def prep_body(members, blocks, tok_rows):
    heads, count = members.shape
    pieces, rows = [], []
    lane = iota((1, count), 1)
    block_col = iota((blocks, count), 0)
    for h in range(heads):
        member = members[h : h + 1, :]
        block = jnp.floor(member * (1.0 / tok_rows))
        local = member - block * tok_rows
        here = block == block_col
        start_of = jnp.sum(jnp.where(block < block_col, 1.0, 0.0), axis=1, keepdims=True)
        start = jnp.sum(jnp.where(here, start_of, 0.0), axis=0, keepdims=True)
        rank = lane - start
        low = block * LOW + rank
        high = block * LOW + (h % 2) * (CAP - LOW) + (rank - LOW)
        rows += [member, jnp.where(rank < LOW, low, -1.0), jnp.where(rank >= LOW, high, -1.0)]
        at_rank = rank == iota((16, count), 0)
        large = jnp.floor(local * (1.0 / 32))
        small = local - large * 32
        right = jnp.concatenate(
            [
                jnp.where(at_rank, large, 0.0),
                jnp.where(at_rank, small, 0.0),
                jnp.where(at_rank, 1.0, 0.0),
                jnp.zeros((80, count), f32),
            ],
            axis=0,
        ).astype(bf16)
        got = dot_nt(onehot(here), right)
        value = got[:, 0:16] * 32 + got[:, 16:32]
        filled = got[:, 32:48] > 0.5
        pieces.append((value, filled))
    low_cols = [jnp.where(f, v, -1.0)[:, :LOW] for v, f in pieces]
    high_cols = [
        jnp.where(f, v + (h % 2) * tok_rows, -1.0)[:, LOW:CAP]
        for h, (v, f) in enumerate(pieces)
    ]
    used = heads * CAP
    table = jnp.concatenate(
        low_cols + high_cols + [jnp.full((blocks, 128 - used), -1.0, f32)], axis=1
    )
    return table, jnp.concatenate(rows + [jnp.zeros((4, count), f32)], axis=0)


def pack_body(index_rows, sources):
    cols = columns_of(index_rows)
    tokens = sources[0].shape[0]
    slots = index_rows.shape[1]
    n = sources[0].shape[1]
    token = iota((slots, tokens), 1)

    def part(value):
        return value.reshape(slots // LOW, LOW, n)

    low = [
        part(dot_nn(onehot(cols[:, h : h + 1] == token), sources[h]))
        for h in range(4)
    ]
    high = []
    for p in range(2):
        col = cols[:, 4 + p : 5 + p]
        high.append(
            part(
                dot_nn(onehot(col == token), sources[2 * p])
                + dot_nn(onehot(col == token + tokens), sources[2 * p + 1])
            )
        )
    return [
        jnp.concatenate(two, axis=1).astype(bf16)
        for two in (low[:2], low[2:], high)
    ]


def head_slots(parts, h):
    p, q = divmod(h, 2)

    def take(part, q):
        part = part.astype(f32)[:, 8 * q : 8 * q + 8, :]
        return part.reshape(part.shape[0] * 8, part.shape[2]).astype(bf16)

    return take(parts[p], q), take(parts[2], p)


def unpack_body(index_rows, parts, h, tokens):
    low, high = head_slots(parts, h)
    token = iota((tokens, index_rows.shape[1]), 0)
    row_low = index_rows[h : h + 1, :]
    row_high = index_rows[4 + h // 2 : 5 + h // 2, :]
    return dot_nn(onehot(token == row_low), low) + dot_nn(
        onehot(token + (h % 2) * tokens == row_high), high
    )


def compact(cols, parts, h, slots):
    low, high = head_slots(parts, h)
    count = cols.shape[0]
    slot = iota((count, slots), 1)
    return (
        dot_nn(onehot(cols[:, 3 * h + 1 : 3 * h + 2] == slot), low)
        + dot_nn(onehot(cols[:, 3 * h + 2 : 3 * h + 3] == slot), high)
    ).astype(bf16)


def weights_of(rows, cols, query, key, h, scaling):
    scores = dot_nt(key, query) * scaling
    allowed = cols[:, 3 * h : 3 * h + 1] <= rows[3 * h : 3 * h + 1, :]
    scores = jnp.where(allowed, scores, -jnp.inf)
    highest = jnp.max(scores, axis=0, keepdims=True)
    weights = jnp.exp(scores - highest)
    return weights * (1.0 / jnp.sum(weights, axis=0, keepdims=True))


def spread(rows, h, transposed, plain):
    slots = rows.shape[1]
    slot = iota((slots, rows.shape[1]), 0)
    out = []
    for k in (1, 2):
        pick = onehot(slot == rows[3 * h + k : 3 * h + k + 1, :])
        got = [dot_nt(pick, t) for t in transposed] + [dot_nn(pick, v) for v in plain]
        out.append(jnp.concatenate(got, axis=1) if len(got) > 1 else got[0])
    return out


def gathered_parts(results):
    def part(value):
        return value.reshape(value.shape[0] // LOW, LOW, value.shape[1])

    low = [part(r[0]) for r in results]
    high = [part(results[2 * p][1] + results[2 * p + 1][1]) for p in range(2)]
    return [
        jnp.concatenate(two, axis=1).astype(bf16)
        for two in (low[:2], low[2:], high)
    ]


def prep_kernel(tok_rows, members_ref, table_ref, rows_ref):
    table, rows = prep_body(members_ref[:, 0, :].astype(f32), table_ref.shape[0], tok_rows)
    table_ref[...] = table.astype(jnp.int32)
    rows_ref[...] = rows


def load_parts(ref):
    return [ref[:, 16 * k : 16 * k + 16, :] for k in range(3)]


def store_parts(ref, parts):
    for k in range(3):
        ref[:, 16 * k : 16 * k + 16, :] = parts[k]


def pack_kernel(index_ref, source_ref, out_ref):
    sources = []
    for h in range(4):
        starts = range(128 * h, source_ref.shape[1], 512)
        got = [source_ref[:, i : i + 128] for i in starts]
        sources.append(jnp.concatenate(got, axis=1) if len(got) > 1 else got[0])
    store_parts(out_ref, pack_body(index_ref[...].astype(f32), sources))


def unpack_kernel(index_ref, packed_ref, *out_refs):
    parts = load_parts(packed_ref)
    index_rows = index_ref[...].astype(f32)
    for h in range(4):
        got = unpack_body(index_rows, parts, h, out_refs[0].shape[0]).astype(bf16)
        for k, ref in enumerate(out_refs):
            ref[:, 128 * h : 128 * h + 128] = got[:, 128 * k : 128 * k + 128]


def forward_kernel(scaling, rows_ref, centroids_ref, qkv_ref, out_ref, centers_ref):
    rows = rows_ref[...]
    cols = columns_of(rows)
    parts = load_parts(qkv_ref)
    slots = qkv_ref.shape[0] * LOW
    count = rows.shape[1]
    results = []
    for h in range(4):
        got = compact(cols, parts, h, slots)
        query, key, value = (got[:, 128 * k : 128 * k + 128] for k in range(3))
        keys = key.astype(f32)
        unit = keys / jnp.sqrt(jnp.mean(keys * keys, axis=1, keepdims=True) + epsilon)
        mixed = 0.5 * centroids_ref[h : h + 1, :] + 0.5 * jnp.sum(
            unit, axis=0, keepdims=True
        ) * (1.0 / count)
        centers_ref[h : h + 1, :] = mixed / jnp.sqrt(
            jnp.mean(mixed * mixed, axis=1, keepdims=True) + epsilon
        )
        weights = weights_of(rows, cols, query, key, h, scaling).astype(bf16)
        attended = dot_nn(value.T, weights).astype(bf16)
        results.append(spread(rows, h, [attended], []))
    store_parts(out_ref, gathered_parts(results))


def backward_kernel(scaling, rows_ref, qkv_ref, grad_ref, out_ref):
    rows = rows_ref[...]
    cols = columns_of(rows)
    parts = load_parts(qkv_ref)
    grad_parts = load_parts(grad_ref)
    slots = qkv_ref.shape[0] * LOW
    results = []
    for h in range(4):
        got = compact(cols, parts, h, slots)
        query, key, value = (got[:, 128 * k : 128 * k + 128] for k in range(3))
        grad = compact(cols, grad_parts, h, slots)
        weights = weights_of(rows, cols, query, key, h, scaling)
        weights_b = weights.astype(bf16)
        attended = dot_nn(value.T, weights_b)
        grad_t = grad.astype(f32).T
        delta = jnp.sum(grad_t * attended, axis=0, keepdims=True)
        probs = dot_nt(value, grad)
        dscore = (weights * (probs - delta) * scaling).astype(bf16)
        query_g = dot_nn(key.T, dscore).astype(bf16)
        key_g = dot_nn(dscore, query).astype(bf16)
        value_g = dot_nn(weights_b, grad).astype(bf16)
        results.append(spread(rows, h, [query_g], [jnp.concatenate([key_g, value_g], axis=1)]))
    store_parts(out_ref, gathered_parts(results))


def call(kernel, outs, flops, *args, vmem=VMEM):
    size = sum(a.size * a.dtype.itemsize for a in args)
    size += sum(o.size * o.dtype.itemsize for o in outs)
    whole = pl.BlockSpec(memory_space=pltpu.VMEM)
    got = pl.pallas_call(
        kernel,
        out_shape=outs,
        in_specs=[whole] * len(args),
        out_specs=[whole] * len(outs),
        compiler_params=pltpu.CompilerParams(vmem_limit_bytes=vmem),
        cost_estimate=pl.CostEstimate(flops=flops, bytes_accessed=size, transcendentals=0),
    )(*args)
    return got[0] if len(outs) == 1 else got


def shape_of(dims, dtype):
    return jax.ShapeDtypeStruct(dims, dtype)


def shifted(x, axis, step, unit=1):
    n = lax.axis_size(axis)
    return lax.ppermute(x, axis, [(i, (i + step * unit) % n) for i in range(n)])


def swapped(x):
    n = lax.axis_size("ctx")
    return lax.ppermute(x, "ctx", [(i, i ^ 1) for i in range(n)])


def neighbour_tokens(out_grad):
    n = lax.axis_size("mp")
    return shifted(out_grad, "mp", 1), shifted(out_grad, "mp", n - 1)


def all_tokens(out_grad, before, after):
    n = lax.axis_size("mp")
    me = lax.axis_index("mp")
    rows, width = out_grad.shape
    half = rows // 2
    upper = shifted(before[:half], "mp", 1)
    lower = shifted(after[half:], "mp", n - 1)
    full = jnp.zeros((rows, n * width), out_grad.dtype)
    full = lax.dynamic_update_slice(full, out_grad, (0, me * width))
    full = lax.dynamic_update_slice(full, before, (0, (me + n - 1) % n * width))
    full = lax.dynamic_update_slice(full, after, (0, (me + 1) % n * width))
    opposite = (me + 2) % n * width
    full = lax.dynamic_update_slice(full, upper, (0, opposite))
    return lax.dynamic_update_slice(full, lower, (half, opposite))


def clu_weight_parts(weight):
    n = lax.axis_size("clu")
    pair = lax.axis_index("clu") // 2
    rows, width = weight.shape
    mine = jnp.zeros((n // 2, 1, rows, width), weight.dtype)
    for k in range(n // 2):
        part = shifted(weight, "clu", k, 2) if k else weight
        mine = lax.dynamic_update_slice(
            mine, part[None, None], ((pair + n // 2 - k) % (n // 2), 0, 0, 0)
        )
    return mine, lax.ppermute(mine, "clu", [(i, i ^ 1) for i in range(n)])


def clu_weight(parts):
    mine, other = parts
    bit = lax.axis_index("clu") % 2
    pairs, _, rows, width = mine.shape
    full = jnp.zeros((pairs, 2, rows, width), mine.dtype)
    full = lax.dynamic_update_slice(full, mine, (0, bit, 0, 0))
    full = lax.dynamic_update_slice(full, other, (0, 1 - bit, 0, 0))
    return full.reshape(2 * pairs * rows, width)


def ctx_weight(part):
    rows, width = part.shape
    chips = lax.axis_size("ctx") // 2
    index = lax.axis_index("ctx")
    chip, core = index // 2, index % 2
    mine = jnp.zeros((chips, 1, rows, width), part.dtype)
    for k in range(chips):
        piece = shifted(part, "ctx", k, 2) if k else part
        mine = lax.dynamic_update_slice(
            mine, piece[None, None], ((chip + chips - k) % chips, 0, 0, 0)
        )
    other = swapped(mine)
    full = jnp.zeros((chips, 2, rows, width), part.dtype)
    full = lax.dynamic_update_slice(full, mine, (0, core, 0, 0))
    full = lax.dynamic_update_slice(full, other, (0, 1 - core, 0, 0))
    return full.reshape(chips * 2 * rows, width)


def scatter_sum(partial):
    ctx, clu = lax.axis_size("ctx"), lax.axis_size("clu")
    chips = ctx // 2
    index = lax.axis_index("ctx")
    chip, core = index // 2, index % 2
    place = lax.axis_index("clu")
    rows = partial.shape[0] // ctx // clu
    width = partial.shape[1]
    shares = partial.reshape(chips, 2, clu * rows, width)

    def pick(x, i, dim):
        return lax.dynamic_index_in_dim(x, i, dim, keepdims=False)

    other = swapped(pick(shares, 1 - core, 1).astype(bf16))
    shares = pick(shares, core, 1) + other.astype(f32)
    total = pick(shares, chip, 0)
    for k in range(1, chips):
        piece = pick(shares, (chip + k) % chips, 0).astype(bf16)
        total = total + shifted(piece, "ctx", k, 2).astype(f32)
    shares = total.reshape(clu, rows, width)
    terms = [
        shifted(pick(shares, (place + k) % clu, 0).astype(bf16), "clu", k)
        for k in range(1, clu)
    ]
    return pick(shares, place, 0), terms


def exchange(x):
    return lax.all_to_all(x, GROUP, split_axis=0, concat_axis=0, tiled=True)


def per_device(queries, tok_keys, tok_values, out_grad, out_weight, membership, centroids):
    tok_rows, width = queries.shape
    heads = membership.shape[0]
    count = membership.shape[2]
    head_size = width // heads
    owners = lax.axis_size(GROUP)
    pair_rows = heads * CAP
    slots = owners * LOW
    scaling = head_size ** (-0.5)

    table, rows = call(
        functools.partial(prep_kernel, tok_rows),
        [shape_of((owners, 128), jnp.int32), shape_of((16, count), f32)],
        10**8,
        membership,
    )
    before, after = neighbour_tokens(out_grad)
    weight_parts = clu_weight_parts(out_weight.T)
    table = exchange(table)
    index_low = table[:, : heads * LOW].reshape(owners, heads, LOW)
    index_high = table[:, heads * LOW : pair_rows].reshape(owners, heads // 2, LOW)
    index_rows = jnp.concatenate([index_low, index_high, index_high], axis=1)
    index_rows = index_rows.transpose(1, 0, 2).reshape(2 * heads, slots)
    index_rows, before, after, weight_parts = lax.optimization_barrier(
        (index_rows, before, after, weight_parts)
    )

    def packed_shape(n):
        return shape_of((owners, pair_rows, n * head_size), bf16)

    def pack(source):
        n = source.shape[1] // width
        return call(pack_kernel, [packed_shape(n)], n * 10**9, index_rows, source, vmem=LESS)

    def unpack(packed, n):
        outs = [shape_of((tok_rows, width), bf16)] * n
        vmem = LESS if n == 1 else VMEM
        return call(unpack_kernel, outs, n * 10**9, index_rows, packed, vmem=vmem)

    got_qkv = exchange(pack(jnp.concatenate([queries, tok_keys, tok_values], axis=1)))
    grad_full = all_tokens(out_grad, before, after)
    weight_full = ctx_weight(clu_weight(weight_parts))
    head_grad = dot_nn(grad_full, weight_full).astype(bf16)
    got_grad = exchange(pack(head_grad))

    attended, centers = call(
        functools.partial(forward_kernel, scaling),
        [packed_shape(1), shape_of((heads, head_size), f32)],
        4 * 10**9,
        rows,
        centroids[:, 0, :],
        got_qkv,
    )
    back_out = exchange(attended)
    grads = call(
        functools.partial(backward_kernel, scaling),
        [packed_shape(3)],
        8 * 10**9,
        rows,
        got_qkv,
        got_grad,
    )
    back_grads = exchange(grads)
    attn_out = unpack(back_out, 1)
    partial = lax.dot_general(
        grad_full, attn_out, (((0,), (0,)), ((), ())), preferred_element_type=f32
    )
    share, terms = scatter_sum(partial)
    query_g, key_g, value_g = unpack(back_grads, 3)
    query_g, terms = lax.optimization_barrier((query_g, terms))
    for term in terms:
        share = share + term.astype(f32)
    return (query_g, key_g, value_g, share.T, centers[:, None, :])


def solution(mesh):
    token = P(GROUP, "mp")
    owner = P("mp", GROUP, None)
    return jax.shard_map(
        per_device,
        mesh=mesh,
        in_specs=(token, token, token, token, P("mp", GROUP), owner, owner),
        out_specs=(token, token, token, P("mp", GROUP), owner),
        check_vma=False,
    )
```

```python
import functools

import jax
import jax.numpy as jnp
from jax import lax
from jax.experimental import pallas as pl
from jax.experimental.pallas import tpu as pltpu
from jax.sharding import PartitionSpec as P

epsilon = 1e-06
GROUP = ("ctx", "clu")
CAP = 12
LOW = 8
VMEM = 56 * 1024 * 1024
LESS = 24 * 1024 * 1024
f32 = jnp.float32
bf16 = jnp.bfloat16


def dot_nn(a, b):
    return lax.dot_general(a, b, (((1,), (0,)), ((), ())), preferred_element_type=f32)


def dot_nt(a, b):
    return lax.dot_general(a, b, (((1,), (1,)), ((), ())), preferred_element_type=f32)


def iota(shape, dim):
    return lax.broadcasted_iota(jnp.int32, shape, dim).astype(f32)


def columns_of(rows):
    copies = 128 // rows.shape[0]
    return jnp.concatenate([rows] * copies, axis=0).T


def onehot(mask):
    return jnp.where(mask, 1.0, 0.0).astype(bf16)


def prep_body(members, blocks, tok_rows):
    heads, count = members.shape
    pieces, rows = [], []
    lane = iota((1, count), 1)
    block_col = iota((blocks, count), 0)
    for h in range(heads):
        member = members[h : h + 1, :]
        block = jnp.floor(member * (1.0 / tok_rows))
        local = member - block * tok_rows
        here = block == block_col
        start_of = jnp.sum(jnp.where(block < block_col, 1.0, 0.0), axis=1, keepdims=True)
        start = jnp.sum(jnp.where(here, start_of, 0.0), axis=0, keepdims=True)
        rank = lane - start
        low = block * LOW + rank
        high = block * LOW + (h % 2) * (CAP - LOW) + (rank - LOW)
        rows += [member, jnp.where(rank < LOW, low, -1.0), jnp.where(rank >= LOW, high, -1.0)]
        at_rank = rank == iota((16, count), 0)
        large = jnp.floor(local * (1.0 / 32))
        small = local - large * 32
        right = jnp.concatenate(
            [
                jnp.where(at_rank, large, 0.0),
                jnp.where(at_rank, small, 0.0),
                jnp.where(at_rank, 1.0, 0.0),
                jnp.zeros((80, count), f32),
            ],
            axis=0,
        ).astype(bf16)
        got = dot_nt(onehot(here), right)
        value = got[:, 0:16] * 32 + got[:, 16:32]
        filled = got[:, 32:48] > 0.5
        pieces.append((value, filled))
    low_cols = [jnp.where(f, v, -1.0)[:, :LOW] for v, f in pieces]
    high_cols = [
        jnp.where(f, v + (h % 2) * tok_rows, -1.0)[:, LOW:CAP]
        for h, (v, f) in enumerate(pieces)
    ]
    used = heads * CAP
    table = jnp.concatenate(
        low_cols + high_cols + [jnp.full((blocks, 128 - used), -1.0, f32)], axis=1
    )
    return table, jnp.concatenate(rows + [jnp.zeros((4, count), f32)], axis=0)


def pack_body(index_rows, sources):
    cols = columns_of(index_rows)
    tokens = sources[0].shape[0]
    slots = index_rows.shape[1]
    n = sources[0].shape[1]
    token = iota((slots, tokens), 1)

    def part(value):
        return value.reshape(slots // LOW, LOW, n)

    low = [
        part(dot_nn(onehot(cols[:, h : h + 1] == token), sources[h]))
        for h in range(4)
    ]
    high = []
    for p in range(2):
        col = cols[:, 4 + p : 5 + p]
        high.append(
            part(
                dot_nn(onehot(col == token), sources[2 * p])
                + dot_nn(onehot(col == token + tokens), sources[2 * p + 1])
            )
        )
    return [
        jnp.concatenate(two, axis=1).astype(bf16)
        for two in (low[:2], low[2:], high)
    ]


def head_slots(parts, h):
    p, q = divmod(h, 2)

    def take(part, q):
        part = part.astype(f32)[:, 8 * q : 8 * q + 8, :]
        return part.reshape(part.shape[0] * 8, part.shape[2]).astype(bf16)

    return take(parts[p], q), take(parts[2], p)


def unpack_body(index_rows, parts, h, tokens):
    low, high = head_slots(parts, h)
    token = iota((tokens, index_rows.shape[1]), 0)
    row_low = index_rows[h : h + 1, :]
    row_high = index_rows[4 + h // 2 : 5 + h // 2, :]
    return dot_nn(onehot(token == row_low), low) + dot_nn(
        onehot(token + (h % 2) * tokens == row_high), high
    )


def compact(cols, parts, h, slots):
    low, high = head_slots(parts, h)
    count = cols.shape[0]
    slot = iota((count, slots), 1)
    return (
        dot_nn(onehot(cols[:, 3 * h + 1 : 3 * h + 2] == slot), low)
        + dot_nn(onehot(cols[:, 3 * h + 2 : 3 * h + 3] == slot), high)
    ).astype(bf16)


def weights_of(rows, cols, query, key, h, scaling):
    scores = dot_nt(key, query) * scaling
    allowed = cols[:, 3 * h : 3 * h + 1] <= rows[3 * h : 3 * h + 1, :]
    scores = jnp.where(allowed, scores, -jnp.inf)
    highest = jnp.max(scores, axis=0, keepdims=True)
    weights = jnp.exp(scores - highest)
    return weights * (1.0 / jnp.sum(weights, axis=0, keepdims=True))


def spread(rows, h, transposed, plain):
    slots = rows.shape[1]
    slot = iota((slots, rows.shape[1]), 0)
    out = []
    for k in (1, 2):
        pick = onehot(slot == rows[3 * h + k : 3 * h + k + 1, :])
        got = [dot_nt(pick, t) for t in transposed] + [dot_nn(pick, v) for v in plain]
        out.append(jnp.concatenate(got, axis=1) if len(got) > 1 else got[0])
    return out


def gathered_parts(results):
    def part(value):
        return value.reshape(value.shape[0] // LOW, LOW, value.shape[1])

    low = [part(r[0]) for r in results]
    high = [part(results[2 * p][1] + results[2 * p + 1][1]) for p in range(2)]
    return [
        jnp.concatenate(two, axis=1).astype(bf16)
        for two in (low[:2], low[2:], high)
    ]


def prep_kernel(tok_rows, members_ref, table_ref, rows_ref):
    table, rows = prep_body(members_ref[:, 0, :].astype(f32), table_ref.shape[0], tok_rows)
    table_ref[...] = table.astype(jnp.int32)
    rows_ref[...] = rows


def load_parts(ref):
    return [ref[:, 16 * k : 16 * k + 16, :] for k in range(3)]


def store_parts(ref, parts):
    for k in range(3):
        ref[:, 16 * k : 16 * k + 16, :] = parts[k]


def pack_kernel(index_ref, source_ref, out_ref):
    sources = []
    for h in range(4):
        starts = range(128 * h, source_ref.shape[1], 512)
        got = [source_ref[:, i : i + 128] for i in starts]
        sources.append(jnp.concatenate(got, axis=1) if len(got) > 1 else got[0])
    store_parts(out_ref, pack_body(index_ref[...].astype(f32), sources))


def unpack_kernel(index_ref, packed_ref, *out_refs):
    parts = load_parts(packed_ref)
    index_rows = index_ref[...].astype(f32)
    for h in range(4):
        got = unpack_body(index_rows, parts, h, out_refs[0].shape[0]).astype(bf16)
        for k, ref in enumerate(out_refs):
            ref[:, 128 * h : 128 * h + 128] = got[:, 128 * k : 128 * k + 128]


def forward_kernel(scaling, rows_ref, centroids_ref, qkv_ref, out_ref, centers_ref):
    rows = rows_ref[...]
    cols = columns_of(rows)
    parts = load_parts(qkv_ref)
    slots = qkv_ref.shape[0] * LOW
    count = rows.shape[1]
    results = []
    for h in range(4):
        got = compact(cols, parts, h, slots)
        query, key, value = (got[:, 128 * k : 128 * k + 128] for k in range(3))
        keys = key.astype(f32)
        unit = keys / jnp.sqrt(jnp.mean(keys * keys, axis=1, keepdims=True) + epsilon)
        mixed = 0.5 * centroids_ref[h : h + 1, :] + 0.5 * jnp.sum(
            unit, axis=0, keepdims=True
        ) * (1.0 / count)
        centers_ref[h : h + 1, :] = mixed / jnp.sqrt(
            jnp.mean(mixed * mixed, axis=1, keepdims=True) + epsilon
        )
        weights = weights_of(rows, cols, query, key, h, scaling).astype(bf16)
        attended = dot_nn(value.T, weights).astype(bf16)
        results.append(spread(rows, h, [attended], []))
    store_parts(out_ref, gathered_parts(results))


def backward_kernel(scaling, rows_ref, qkv_ref, grad_ref, out_ref):
    rows = rows_ref[...]
    cols = columns_of(rows)
    parts = load_parts(qkv_ref)
    grad_parts = load_parts(grad_ref)
    slots = qkv_ref.shape[0] * LOW
    results = []
    for h in range(4):
        got = compact(cols, parts, h, slots)
        query, key, value = (got[:, 128 * k : 128 * k + 128] for k in range(3))
        grad = compact(cols, grad_parts, h, slots)
        weights = weights_of(rows, cols, query, key, h, scaling)
        weights_b = weights.astype(bf16)
        attended = dot_nn(value.T, weights_b)
        grad_t = grad.astype(f32).T
        delta = jnp.sum(grad_t * attended, axis=0, keepdims=True)
        probs = dot_nt(value, grad)
        dscore = (weights * (probs - delta) * scaling).astype(bf16)
        query_g = dot_nn(key.T, dscore).astype(bf16)
        key_g = dot_nn(dscore, query).astype(bf16)
        value_g = dot_nn(weights_b, grad).astype(bf16)
        results.append(spread(rows, h, [query_g], [jnp.concatenate([key_g, value_g], axis=1)]))
    store_parts(out_ref, gathered_parts(results))


def call(kernel, outs, flops, *args, vmem=VMEM):
    size = sum(a.size * a.dtype.itemsize for a in args)
    size += sum(o.size * o.dtype.itemsize for o in outs)
    whole = pl.BlockSpec(memory_space=pltpu.VMEM)
    got = pl.pallas_call(
        kernel,
        out_shape=outs,
        in_specs=[whole] * len(args),
        out_specs=[whole] * len(outs),
        compiler_params=pltpu.CompilerParams(vmem_limit_bytes=vmem),
        cost_estimate=pl.CostEstimate(flops=flops, bytes_accessed=size, transcendentals=0),
    )(*args)
    return got[0] if len(outs) == 1 else got


def shape_of(dims, dtype):
    return jax.ShapeDtypeStruct(dims, dtype)


def shifted(x, axis, step, unit=1):
    n = lax.axis_size(axis)
    return lax.ppermute(x, axis, [(i, (i + step * unit) % n) for i in range(n)])


def swapped(x):
    n = lax.axis_size("ctx")
    return lax.ppermute(x, "ctx", [(i, i ^ 1) for i in range(n)])


def neighbour_tokens(out_grad):
    n = lax.axis_size("mp")
    return shifted(out_grad, "mp", 1), shifted(out_grad, "mp", n - 1)


def all_tokens(out_grad, before, after):
    n = lax.axis_size("mp")
    me = lax.axis_index("mp")
    rows, width = out_grad.shape
    half = rows // 2
    upper = shifted(before[:half], "mp", 1)
    lower = shifted(after[half:], "mp", n - 1)
    full = jnp.zeros((rows, n * width), out_grad.dtype)
    full = lax.dynamic_update_slice(full, out_grad, (0, me * width))
    full = lax.dynamic_update_slice(full, before, (0, (me + n - 1) % n * width))
    full = lax.dynamic_update_slice(full, after, (0, (me + 1) % n * width))
    opposite = (me + 2) % n * width
    full = lax.dynamic_update_slice(full, upper, (0, opposite))
    return lax.dynamic_update_slice(full, lower, (half, opposite))


def clu_weight_parts(weight):
    near = [weight, shifted(weight, "clu", 1), shifted(weight, "clu", 2)]
    joined = jnp.concatenate(near, axis=0)
    rows = weight.shape[0]
    return near, shifted(joined, "clu", 3), shifted(joined[: 2 * rows], "clu", 6)


def clu_weight(parts):
    n = lax.axis_size("clu")
    me = lax.axis_index("clu")
    near, middle, far = parts
    rows, width = near[0].shape
    blocks = near + [middle[k * rows : (k + 1) * rows] for k in range(3)]
    blocks += [far[k * rows : (k + 1) * rows] for k in range(2)]
    full = jnp.zeros((n * rows, width), near[0].dtype)
    for k, block in enumerate(blocks):
        full = lax.dynamic_update_slice(full, block, ((me + n - k) % n * rows, 0))
    return full


def ctx_weight(part):
    rows, width = part.shape
    chips = lax.axis_size("ctx") // 2
    index = lax.axis_index("ctx")
    chip, core = index // 2, index % 2
    mine = jnp.zeros((chips, 1, rows, width), part.dtype)
    for k in range(chips):
        piece = shifted(part, "ctx", k, 2) if k else part
        mine = lax.dynamic_update_slice(
            mine, piece[None, None], ((chip + chips - k) % chips, 0, 0, 0)
        )
    other = swapped(mine)
    full = jnp.zeros((chips, 2, rows, width), part.dtype)
    full = lax.dynamic_update_slice(full, mine, (0, core, 0, 0))
    full = lax.dynamic_update_slice(full, other, (0, 1 - core, 0, 0))
    return full.reshape(chips * 2 * rows, width)


def scatter_sum(partial):
    ctx, clu = lax.axis_size("ctx"), lax.axis_size("clu")
    chips = ctx // 2
    index = lax.axis_index("ctx")
    chip, core = index // 2, index % 2
    place = lax.axis_index("clu")
    rows = partial.shape[0] // ctx // clu
    width = partial.shape[1]
    shares = partial.reshape(chips, 2, clu * rows, width)

    def pick(x, i, dim):
        return lax.dynamic_index_in_dim(x, i, dim, keepdims=False)

    other = swapped(pick(shares, 1 - core, 1).astype(bf16))
    shares = pick(shares, core, 1) + other.astype(f32)
    total = pick(shares, chip, 0)
    for k in range(1, chips):
        piece = pick(shares, (chip + k) % chips, 0).astype(bf16)
        total = total + shifted(piece, "ctx", k, 2).astype(f32)
    shares = total.reshape(clu, rows, width)
    terms = [
        shifted(pick(shares, (place + k) % clu, 0).astype(bf16), "clu", k)
        for k in range(1, clu)
    ]
    return pick(shares, place, 0), terms


def exchange(x):
    return lax.all_to_all(x, GROUP, split_axis=0, concat_axis=0, tiled=True)


def per_device(queries, tok_keys, tok_values, out_grad, out_weight, membership, centroids):
    tok_rows, width = queries.shape
    heads = membership.shape[0]
    count = membership.shape[2]
    head_size = width // heads
    owners = lax.axis_size(GROUP)
    pair_rows = heads * CAP
    slots = owners * LOW
    scaling = head_size ** (-0.5)

    table, rows = call(
        functools.partial(prep_kernel, tok_rows),
        [shape_of((owners, 128), jnp.int32), shape_of((16, count), f32)],
        10**8,
        membership,
    )
    before, after = neighbour_tokens(out_grad)
    weight_parts = clu_weight_parts(out_weight.T)
    table = exchange(table)
    index_low = table[:, : heads * LOW].reshape(owners, heads, LOW)
    index_high = table[:, heads * LOW : pair_rows].reshape(owners, heads // 2, LOW)
    index_rows = jnp.concatenate([index_low, index_high, index_high], axis=1)
    index_rows = index_rows.transpose(1, 0, 2).reshape(2 * heads, slots)
    index_rows, before, after, weight_parts = lax.optimization_barrier(
        (index_rows, before, after, weight_parts)
    )

    def packed_shape(n):
        return shape_of((owners, pair_rows, n * head_size), bf16)

    def pack(source):
        n = source.shape[1] // width
        return call(pack_kernel, [packed_shape(n)], n * 10**9, index_rows, source, vmem=LESS)

    def unpack(packed, n):
        outs = [shape_of((tok_rows, width), bf16)] * n
        vmem = LESS if n == 1 else VMEM
        return call(unpack_kernel, outs, n * 10**9, index_rows, packed, vmem=vmem)

    got_qkv = exchange(pack(jnp.concatenate([queries, tok_keys, tok_values], axis=1)))
    grad_full = all_tokens(out_grad, before, after)
    weight_full = ctx_weight(clu_weight(weight_parts))
    head_grad = dot_nn(grad_full, weight_full).astype(bf16)
    got_grad = exchange(pack(head_grad))

    attended, centers = call(
        functools.partial(forward_kernel, scaling),
        [packed_shape(1), shape_of((heads, head_size), f32)],
        4 * 10**9,
        rows,
        centroids[:, 0, :],
        got_qkv,
    )
    back_out = exchange(attended)
    grads = call(
        functools.partial(backward_kernel, scaling),
        [packed_shape(3)],
        8 * 10**9,
        rows,
        got_qkv,
        got_grad,
    )
    back_grads = exchange(grads)
    attn_out = unpack(back_out, 1)
    partial = lax.dot_general(
        grad_full, attn_out, (((0,), (0,)), ((), ())), preferred_element_type=f32
    )
    share, terms = scatter_sum(partial)
    query_g, key_g, value_g = unpack(back_grads, 3)
    query_g, terms = lax.optimization_barrier((query_g, terms))
    for term in terms:
        share = share + term.astype(f32)
    return (query_g, key_g, value_g, share.T, centers[:, None, :])


def solution(mesh):
    token = P(GROUP, "mp")
    owner = P("mp", GROUP, None)
    return jax.shard_map(
        per_device,
        mesh=mesh,
        in_specs=(token, token, token, token, P("mp", GROUP), owner, owner),
        out_specs=(token, token, token, P("mp", GROUP), owner),
        check_vma=False,
    )
```

```python
import functools

import jax
import jax.numpy as jnp
from jax import lax
from jax.experimental import pallas as pl
from jax.experimental.pallas import tpu as pltpu
from jax.sharding import PartitionSpec as P

epsilon = 1e-06
GROUP = ("ctx", "clu")
CAP = 12
LOW = 8
VMEM = 56 * 1024 * 1024
LESS = 24 * 1024 * 1024
f32 = jnp.float32
bf16 = jnp.bfloat16


def dot_nn(a, b):
    return lax.dot_general(a, b, (((1,), (0,)), ((), ())), preferred_element_type=f32)


def dot_nt(a, b):
    return lax.dot_general(a, b, (((1,), (1,)), ((), ())), preferred_element_type=f32)


def iota(shape, dim):
    return lax.broadcasted_iota(jnp.int32, shape, dim).astype(f32)


def columns_of(rows):
    copies = 128 // rows.shape[0]
    return jnp.concatenate([rows] * copies, axis=0).T


def onehot(mask):
    return jnp.where(mask, 1.0, 0.0).astype(bf16)


def prep_body(members, blocks, tok_rows):
    heads, count = members.shape
    pieces, rows = [], []
    lane = iota((1, count), 1)
    block_col = iota((blocks, count), 0)
    for h in range(heads):
        member = members[h : h + 1, :]
        block = jnp.floor(member * (1.0 / tok_rows))
        local = member - block * tok_rows
        here = block == block_col
        start_of = jnp.sum(jnp.where(block < block_col, 1.0, 0.0), axis=1, keepdims=True)
        start = jnp.sum(jnp.where(here, start_of, 0.0), axis=0, keepdims=True)
        rank = lane - start
        low = block * LOW + rank
        high = block * LOW + (h % 2) * (CAP - LOW) + (rank - LOW)
        rows += [member, jnp.where(rank < LOW, low, -1.0), jnp.where(rank >= LOW, high, -1.0)]
        at_rank = rank == iota((16, count), 0)
        large = jnp.floor(local * (1.0 / 32))
        small = local - large * 32
        right = jnp.concatenate(
            [
                jnp.where(at_rank, large, 0.0),
                jnp.where(at_rank, small, 0.0),
                jnp.where(at_rank, 1.0, 0.0),
                jnp.zeros((80, count), f32),
            ],
            axis=0,
        ).astype(bf16)
        got = dot_nt(onehot(here), right)
        value = got[:, 0:16] * 32 + got[:, 16:32]
        filled = got[:, 32:48] > 0.5
        pieces.append((value, filled))
    low_cols = [jnp.where(f, v, -1.0)[:, :LOW] for v, f in pieces]
    high_cols = [
        jnp.where(f, v + (h % 2) * tok_rows, -1.0)[:, LOW:CAP]
        for h, (v, f) in enumerate(pieces)
    ]
    used = heads * CAP
    table = jnp.concatenate(
        low_cols + high_cols + [jnp.full((blocks, 128 - used), -1.0, f32)], axis=1
    )
    return table, jnp.concatenate(rows + [jnp.zeros((4, count), f32)], axis=0)


def pack_body(index_rows, sources):
    cols = columns_of(index_rows)
    tokens = sources[0].shape[0]
    slots = index_rows.shape[1]
    n = sources[0].shape[1]
    token = iota((slots, tokens), 1)

    def part(value):
        return value.reshape(slots // LOW, LOW, n)

    low = [
        part(dot_nn(onehot(cols[:, h : h + 1] == token), sources[h]))
        for h in range(4)
    ]
    high = []
    for p in range(2):
        col = cols[:, 4 + p : 5 + p]
        high.append(
            part(
                dot_nn(onehot(col == token), sources[2 * p])
                + dot_nn(onehot(col == token + tokens), sources[2 * p + 1])
            )
        )
    return [
        jnp.concatenate(two, axis=1).astype(bf16)
        for two in (low[:2], low[2:], high)
    ]


def head_slots(parts, h):
    p, q = divmod(h, 2)

    def take(part, q):
        part = part.astype(f32)[:, 8 * q : 8 * q + 8, :]
        return part.reshape(part.shape[0] * 8, part.shape[2]).astype(bf16)

    return take(parts[p], q), take(parts[2], p)


def unpack_body(index_rows, parts, h, tokens):
    low, high = head_slots(parts, h)
    token = iota((tokens, index_rows.shape[1]), 0)
    row_low = index_rows[h : h + 1, :]
    row_high = index_rows[4 + h // 2 : 5 + h // 2, :]
    return dot_nn(onehot(token == row_low), low) + dot_nn(
        onehot(token + (h % 2) * tokens == row_high), high
    )


def compact(cols, parts, h, slots):
    low, high = head_slots(parts, h)
    count = cols.shape[0]
    slot = iota((count, slots), 1)
    return (
        dot_nn(onehot(cols[:, 3 * h + 1 : 3 * h + 2] == slot), low)
        + dot_nn(onehot(cols[:, 3 * h + 2 : 3 * h + 3] == slot), high)
    ).astype(bf16)


def weights_of(rows, cols, query, key, h, scaling):
    scores = dot_nt(key, query) * scaling
    allowed = cols[:, 3 * h : 3 * h + 1] <= rows[3 * h : 3 * h + 1, :]
    scores = jnp.where(allowed, scores, -jnp.inf)
    highest = jnp.max(scores, axis=0, keepdims=True)
    weights = jnp.exp(scores - highest)
    return weights * (1.0 / jnp.sum(weights, axis=0, keepdims=True))


def spread(rows, h, transposed, plain):
    slots = rows.shape[1]
    slot = iota((slots, rows.shape[1]), 0)
    out = []
    for k in (1, 2):
        pick = onehot(slot == rows[3 * h + k : 3 * h + k + 1, :])
        got = [dot_nt(pick, t) for t in transposed] + [dot_nn(pick, v) for v in plain]
        out.append(jnp.concatenate(got, axis=1) if len(got) > 1 else got[0])
    return out


def gathered_parts(results):
    def part(value):
        return value.reshape(value.shape[0] // LOW, LOW, value.shape[1])

    low = [part(r[0]) for r in results]
    high = [part(results[2 * p][1] + results[2 * p + 1][1]) for p in range(2)]
    return [
        jnp.concatenate(two, axis=1).astype(bf16)
        for two in (low[:2], low[2:], high)
    ]


def prep_kernel(tok_rows, members_ref, table_ref, rows_ref):
    table, rows = prep_body(members_ref[:, 0, :].astype(f32), table_ref.shape[0], tok_rows)
    table_ref[...] = table.astype(jnp.int32)
    rows_ref[...] = rows


def load_parts(ref):
    return [ref[:, 16 * k : 16 * k + 16, :] for k in range(3)]


def store_parts(ref, parts):
    for k in range(3):
        ref[:, 16 * k : 16 * k + 16, :] = parts[k]


def pack_kernel(index_ref, source_ref, out_ref):
    sources = []
    for h in range(4):
        starts = range(128 * h, source_ref.shape[1], 512)
        got = [source_ref[:, i : i + 128] for i in starts]
        sources.append(jnp.concatenate(got, axis=1) if len(got) > 1 else got[0])
    store_parts(out_ref, pack_body(index_ref[...].astype(f32), sources))


def unpack_kernel(index_ref, packed_ref, *out_refs):
    parts = load_parts(packed_ref)
    index_rows = index_ref[...].astype(f32)
    for h in range(4):
        got = unpack_body(index_rows, parts, h, out_refs[0].shape[0]).astype(bf16)
        for k, ref in enumerate(out_refs):
            ref[:, 128 * h : 128 * h + 128] = got[:, 128 * k : 128 * k + 128]


def forward_kernel(scaling, rows_ref, centroids_ref, qkv_ref, out_ref, centers_ref):
    rows = rows_ref[...]
    cols = columns_of(rows)
    parts = load_parts(qkv_ref)
    slots = qkv_ref.shape[0] * LOW
    count = rows.shape[1]
    results = []
    for h in range(4):
        got = compact(cols, parts, h, slots)
        query, key, value = (got[:, 128 * k : 128 * k + 128] for k in range(3))
        keys = key.astype(f32)
        unit = keys / jnp.sqrt(jnp.mean(keys * keys, axis=1, keepdims=True) + epsilon)
        mixed = 0.5 * centroids_ref[h : h + 1, :] + 0.5 * jnp.sum(
            unit, axis=0, keepdims=True
        ) * (1.0 / count)
        centers_ref[h : h + 1, :] = mixed / jnp.sqrt(
            jnp.mean(mixed * mixed, axis=1, keepdims=True) + epsilon
        )
        weights = weights_of(rows, cols, query, key, h, scaling).astype(bf16)
        attended = dot_nn(value.T, weights).astype(bf16)
        results.append(spread(rows, h, [attended], []))
    store_parts(out_ref, gathered_parts(results))


def backward_kernel(scaling, rows_ref, qkv_ref, grad_ref, out_ref):
    rows = rows_ref[...]
    cols = columns_of(rows)
    parts = load_parts(qkv_ref)
    grad_parts = load_parts(grad_ref)
    slots = qkv_ref.shape[0] * LOW
    results = []
    for h in range(4):
        got = compact(cols, parts, h, slots)
        query, key, value = (got[:, 128 * k : 128 * k + 128] for k in range(3))
        grad = compact(cols, grad_parts, h, slots)
        weights = weights_of(rows, cols, query, key, h, scaling)
        weights_b = weights.astype(bf16)
        attended = dot_nn(value.T, weights_b)
        grad_t = grad.astype(f32).T
        delta = jnp.sum(grad_t * attended, axis=0, keepdims=True)
        probs = dot_nt(value, grad)
        dscore = (weights * (probs - delta) * scaling).astype(bf16)
        query_g = dot_nn(key.T, dscore).astype(bf16)
        key_g = dot_nn(dscore, query).astype(bf16)
        value_g = dot_nn(weights_b, grad).astype(bf16)
        results.append(spread(rows, h, [query_g], [jnp.concatenate([key_g, value_g], axis=1)]))
    store_parts(out_ref, gathered_parts(results))


def call(kernel, outs, flops, *args, vmem=VMEM):
    size = sum(a.size * a.dtype.itemsize for a in args)
    size += sum(o.size * o.dtype.itemsize for o in outs)
    whole = pl.BlockSpec(memory_space=pltpu.VMEM)
    got = pl.pallas_call(
        kernel,
        out_shape=outs,
        in_specs=[whole] * len(args),
        out_specs=[whole] * len(outs),
        compiler_params=pltpu.CompilerParams(vmem_limit_bytes=vmem),
        cost_estimate=pl.CostEstimate(flops=flops, bytes_accessed=size, transcendentals=0),
    )(*args)
    return got[0] if len(outs) == 1 else got


def shape_of(dims, dtype):
    return jax.ShapeDtypeStruct(dims, dtype)


def shifted(x, axis, step, unit=1):
    n = lax.axis_size(axis)
    return lax.ppermute(x, axis, [(i, (i + step * unit) % n) for i in range(n)])


def crossed(x, axis, bits):
    n = lax.axis_size(axis)
    return lax.ppermute(x, axis, [(i, i ^ bits) for i in range(n)])


def swapped(x):
    n = lax.axis_size("ctx")
    return lax.ppermute(x, "ctx", [(i, i ^ 1) for i in range(n)])


def neighbour_tokens(out_grad):
    n = lax.axis_size("mp")
    return shifted(out_grad, "mp", 1), shifted(out_grad, "mp", n - 1)


def all_tokens(out_grad, before, after):
    n = lax.axis_size("mp")
    me = lax.axis_index("mp")
    rows, width = out_grad.shape
    half = rows // 2
    upper = shifted(before[:half], "mp", 1)
    lower = shifted(after[half:], "mp", n - 1)
    full = jnp.zeros((rows, n * width), out_grad.dtype)
    full = lax.dynamic_update_slice(full, out_grad, (0, me * width))
    full = lax.dynamic_update_slice(full, before, (0, (me + n - 1) % n * width))
    full = lax.dynamic_update_slice(full, after, (0, (me + 1) % n * width))
    opposite = (me + 2) % n * width
    full = lax.dynamic_update_slice(full, upper, (0, opposite))
    return lax.dynamic_update_slice(full, lower, (half, opposite))


def clu_weight_parts(weight):
    n = lax.axis_size("clu")
    pair = lax.axis_index("clu") // 2
    rows, width = weight.shape
    mine = jnp.zeros((n // 2, 1, rows, width), weight.dtype)
    for k in range(n // 2):
        part = crossed(weight, "clu", 2 * k) if k else weight
        mine = lax.dynamic_update_slice(
            mine, part[None, None], (pair ^ k, 0, 0, 0)
        )
    return mine, lax.ppermute(mine, "clu", [(i, i ^ 1) for i in range(n)])


def clu_weight(parts):
    mine, other = parts
    bit = lax.axis_index("clu") % 2
    pairs, _, rows, width = mine.shape
    full = jnp.zeros((pairs, 2, rows, width), mine.dtype)
    full = lax.dynamic_update_slice(full, mine, (0, bit, 0, 0))
    full = lax.dynamic_update_slice(full, other, (0, 1 - bit, 0, 0))
    return full.reshape(2 * pairs * rows, width)


def ctx_weight(part):
    rows, width = part.shape
    chips = lax.axis_size("ctx") // 2
    index = lax.axis_index("ctx")
    chip, core = index // 2, index % 2
    mine = jnp.zeros((chips, 1, rows, width), part.dtype)
    for k in range(chips):
        piece = crossed(part, "ctx", 2 * k) if k else part
        mine = lax.dynamic_update_slice(
            mine, piece[None, None], (chip ^ k, 0, 0, 0)
        )
    other = swapped(mine)
    full = jnp.zeros((chips, 2, rows, width), part.dtype)
    full = lax.dynamic_update_slice(full, mine, (0, core, 0, 0))
    full = lax.dynamic_update_slice(full, other, (0, 1 - core, 0, 0))
    return full.reshape(chips * 2 * rows, width)


def scatter_sum(partial):
    ctx, clu = lax.axis_size("ctx"), lax.axis_size("clu")
    chips = ctx // 2
    index = lax.axis_index("ctx")
    chip, core = index // 2, index % 2
    place = lax.axis_index("clu")
    rows = partial.shape[0] // ctx // clu
    width = partial.shape[1]
    shares = partial.reshape(chips, 2, clu * rows, width)

    def pick(x, i, dim):
        return lax.dynamic_index_in_dim(x, i, dim, keepdims=False)

    other = swapped(pick(shares, 1 - core, 1).astype(bf16))
    shares = pick(shares, core, 1) + other.astype(f32)
    total = pick(shares, chip, 0)
    for k in range(1, chips):
        piece = pick(shares, chip ^ k, 0).astype(bf16)
        total = total + crossed(piece, "ctx", 2 * k).astype(f32)
    shares = total.reshape(clu, rows, width)
    terms = [
        crossed(pick(shares, place ^ k, 0).astype(bf16), "clu", k)
        for k in range(1, clu)
    ]
    return pick(shares, place, 0), terms


def exchange(x):
    return lax.all_to_all(x, GROUP, split_axis=0, concat_axis=0, tiled=True)


def per_device(queries, tok_keys, tok_values, out_grad, out_weight, membership, centroids):
    tok_rows, width = queries.shape
    heads = membership.shape[0]
    count = membership.shape[2]
    head_size = width // heads
    owners = lax.axis_size(GROUP)
    pair_rows = heads * CAP
    slots = owners * LOW
    scaling = head_size ** (-0.5)

    table, rows = call(
        functools.partial(prep_kernel, tok_rows),
        [shape_of((owners, 128), jnp.int32), shape_of((16, count), f32)],
        10**8,
        membership,
    )
    before, after = neighbour_tokens(out_grad)
    weight_parts = clu_weight_parts(out_weight.T)
    table = exchange(table)
    index_low = table[:, : heads * LOW].reshape(owners, heads, LOW)
    index_high = table[:, heads * LOW : pair_rows].reshape(owners, heads // 2, LOW)
    index_rows = jnp.concatenate([index_low, index_high, index_high], axis=1)
    index_rows = index_rows.transpose(1, 0, 2).reshape(2 * heads, slots)
    index_rows, before, after, weight_parts = lax.optimization_barrier(
        (index_rows, before, after, weight_parts)
    )

    def packed_shape(n):
        return shape_of((owners, pair_rows, n * head_size), bf16)

    def pack(source):
        n = source.shape[1] // width
        return call(pack_kernel, [packed_shape(n)], n * 10**9, index_rows, source, vmem=LESS)

    def unpack(packed, n):
        outs = [shape_of((tok_rows, width), bf16)] * n
        vmem = LESS if n == 1 else VMEM
        return call(unpack_kernel, outs, n * 10**9, index_rows, packed, vmem=vmem)

    got_qkv = exchange(pack(jnp.concatenate([queries, tok_keys, tok_values], axis=1)))
    grad_full = all_tokens(out_grad, before, after)
    weight_full = ctx_weight(clu_weight(weight_parts))
    head_grad = dot_nn(grad_full, weight_full).astype(bf16)
    got_grad = exchange(pack(head_grad))

    attended, centers = call(
        functools.partial(forward_kernel, scaling),
        [packed_shape(1), shape_of((heads, head_size), f32)],
        4 * 10**9,
        rows,
        centroids[:, 0, :],
        got_qkv,
    )
    back_out = exchange(attended)
    grads = call(
        functools.partial(backward_kernel, scaling),
        [packed_shape(3)],
        8 * 10**9,
        rows,
        got_qkv,
        got_grad,
    )
    back_grads = exchange(grads)
    attn_out = unpack(back_out, 1)
    partial = lax.dot_general(
        grad_full, attn_out, (((0,), (0,)), ((), ())), preferred_element_type=f32
    )
    share, terms = scatter_sum(partial)
    query_g, key_g, value_g = unpack(back_grads, 3)
    query_g, terms = lax.optimization_barrier((query_g, terms))
    for term in terms:
        share = share + term.astype(f32)
    return (query_g, key_g, value_g, share.T, centers[:, None, :])


def solution(mesh):
    token = P(GROUP, "mp")
    owner = P("mp", GROUP, None)
    return jax.shard_map(
        per_device,
        mesh=mesh,
        in_specs=(token, token, token, token, P("mp", GROUP), owner, owner),
        out_specs=(token, token, token, P("mp", GROUP), owner),
        check_vma=False,
    )
```
